256 devices in a mesh: wave: 16 (over x, y), ny: 16 (over z, core).
Axes of the slice: x: 4, y: 4, z: 8, core: 2. Of those that a mesh axis runs over, the one named last changes fastest.
Arguments:
- spectra: bfloat16 [640, 48, 1281], P('wave', 'ny'), may hold values from -0.0024414062 to 0.0024414062
- legendre: bfloat16 [640, 256, 1281], P('wave', 'ny'), may hold values from -6 to 6
- lon_anchor: int32 [1], replicated, may hold values from 0 to 5119
- row_index: int32 [2048], P('ny'), may hold values from 0 to 254, as said below
- row_weight: float32 [2048], P('ny'), may hold values from 0 to 1
- col_index: int32 [2048], P('wave'), may hold values from 0 to 510, as said below
- col_weight: float32 [2048], P('wave'), may hold values from 0 to 1
- zone_width: int32 [4], replicated, may hold values from 8 to 16, as said below
- nest_state: bfloat16 [24, 2048, 2048], P(None, 'ny', 'wave'), may hold values from -6 to 6
Outputs:
- parent_band: float32 [24, 256, 512], P(None, 'ny', 'wave')
- nest_next: bfloat16 [24, 2048, 2048], P(None, 'ny', 'wave')
The draws below stay inside these ranges and needn't reach their ends.
Inputs may be any that keep to these rules, and one draw needn't show every extreme that they name: For a nest row in ny block y (rows y * 128 onward), row_index lies from y * 16 - 1 to (y + 1) * 16 - 1; both ends are reached in every block that is neither the first nor the last. For a nest column in wave block w, col_index lies from w * 32 - 1 to (w + 1) * 32 - 1; both ends are reached in every block that is neither the first nor the last. `zone_width`: at least one side has width exactly 16.
All inputs are finite; a program needn't handle non-finite values.
Results may differ from the reference program's by a relative error of at most 0.001.
Values may be sent and summed in bfloat16 or wider, within the bound.
A program may use at most 128 MiB of HBM per device.

```python
import math
import jax
import jax.numpy as jnp
from jax import lax

MW = 1280
NLON = 5120
NEST_DEV = 128
ZMAX = 16
NSWEEP = 4
MP = 640
NP = 1281
KF = 24
NB = 256
NLB = 512
NROW = 2048
NCOL = 2048


def index_ramp(key, cell_count, parent_count, block_cells):
    ratio_cells = cell_count // parent_count
    cells = jnp.arange(cell_count, dtype=jnp.int32)
    offsets = jax.random.randint(key, (cell_count,), 0, 2, dtype=jnp.int32)
    local_cell = cells % block_cells
    offsets = jnp.where(local_cell == 0, 0, jnp.where(local_cell == block_cells - 1, 1, offsets))
    return jnp.clip(cells // ratio_cells - 1 + offsets, 0, parent_count - 2).astype(jnp.int32)


def draw_row_index(key, part):
    key = jax.random.fold_in(key, 11)
    return index_ramp(key, NROW, NB, NEST_DEV)


def draw_col_index(key, part):
    key = jax.random.fold_in(key, 23)
    return index_ramp(key, NCOL, NLB, NEST_DEV)


def draw_zone_width(key, part):
    key = jax.random.fold_in(key, 37)
    width_key, side_key = jax.random.split(key)
    widths = jax.random.randint(width_key, (4,), ZMAX // 2, ZMAX + 1, dtype=jnp.int32)
    chosen = jax.random.randint(side_key, (), 0, 4, dtype=jnp.int32)
    return jnp.where(jnp.arange(4, dtype=jnp.int32) == chosen, ZMAX, widths).astype(jnp.int32)


def steps_of(rng, shape, pieces, least, top_value):
    def one(dim, blocks):
        draws = jax.random.uniform(jax.random.fold_in(jax.random.fold_in(rng, 6), dim), (blocks,), jnp.float32, least / len(pieces), top_value / len(pieces))
        return jnp.repeat(jnp.exp(draws), shape[dim] // blocks).reshape((-1,) + (1,) * (len(shape) - dim - 1))

    gain = one(*pieces[0])
    for cut in pieces[1:]:
        gain = gain * one(*cut)
    return gain


def gaussian(own_key, extent, width, most, cuts=(), kind=jnp.bfloat16):
    result = jax.random.normal(own_key, extent, jnp.float32) * width
    if len(cuts) > 0:
        result = steps_of(own_key, extent, cuts, -0.22, 0.18) * result
    return jnp.clip(result, min=-most, max=most).astype(kind)


def setup_inputs(seed: int = 0) -> dict:
    splits = jax.random.split(jax.random.key(seed), 10)
    spectra = gaussian(splits[0], (MP, 2 * KF, NP), (4 * MW * MW) ** -0.5, 0.0024414062, ((0, 16), (1, 16)))
    legendre = gaussian(splits[1], (MP, NB, NP), 1.0, 6.0, ((0, 16), (1, 16)))
    lon_anchor = jax.random.randint(splits[2], (1,), 0, NLON).astype(jnp.int32)
    row_index = draw_row_index(jax.random.fold_in(splits[9], 71), 0)
    row_weight = jnp.clip(1.0 * jax.random.uniform(splits[4], (NROW,), jnp.float32) ** steps_of(splits[4], (NROW,), ((0, 16),), -0.2, 0.2), 0.0, 1.0)
    col_index = draw_col_index(jax.random.fold_in(splits[9], 71), 0)
    col_weight = jnp.clip(1.0 * jax.random.uniform(splits[6], (NCOL,), jnp.float32) ** steps_of(splits[6], (NCOL,), ((0, 16),), -0.2, 0.2), 0.0, 1.0)
    zone_width = draw_zone_width(jax.random.fold_in(splits[9], 71), 0)
    nest_state = gaussian(splits[8], (KF, NROW, NCOL), 1.0, 6.0, ((1, 16), (2, 16)))
    return {"spectra": spectra, "legendre": legendre, "lon_anchor": lon_anchor, "row_index": row_index, "row_weight": row_weight, "col_index": col_index, "col_weight": col_weight, "zone_width": zone_width, "nest_state": nest_state}


DIFFUSION = 0.2


def ramp_weight(distance, zone_size):
    return jnp.maximum(0.0, 1.0 - distance / zone_size)


def reference(spectra, legendre, lon_anchor, row_index, row_weight, col_index, col_weight, zone_width, nest_state):
    positions = jnp.arange(NP, dtype=jnp.int32)

    def one_pair(bundle):
        pair_id, lat_table, coefficient = bundle
        lower_half = positions < (MW - pair_id)
        halves = jnp.stack([lower_half, jnp.logical_not(lower_half)]).astype(jnp.float32)
        masked = coefficient.astype(jnp.float32)[None, :, :] * halves[:, None, :]
        return jnp.einsum("lj,hcj->hlc", lat_table.astype(jnp.float32), masked, precision=lax.Precision.HIGHEST)

    pair_ids = jnp.arange(MP, dtype=jnp.int32)
    fourier = lax.map(one_pair, (pair_ids, legendre, spectra))
    wavenumbers = jnp.stack([pair_ids, MW - 1 - pair_ids], axis=1)
    longitudes = lon_anchor[0] + jnp.arange(NLB, dtype=jnp.int32)
    phases = (wavenumbers[:, :, None] * longitudes[None, None, :]) % NLON
    angles = phases.astype(jnp.float32) * (2.0 * math.pi / NLON)
    weights = jnp.where(wavenumbers == 0, 1.0, 2.0).astype(jnp.float32)[:, :, None]
    circle = jnp.stack([jnp.cos(angles) * weights, -jnp.sin(angles) * weights], axis=2)
    components = fourier.reshape(MP, 2, NB, 2, KF)
    parent_band = jnp.einsum("phlrk,phrn->kln", components, circle, precision=lax.Precision.HIGHEST)

    zone_sizes = zone_width.astype(jnp.float32)
    row_place = jnp.arange(NROW, dtype=jnp.int32).astype(jnp.float32)
    col_place = jnp.arange(NCOL, dtype=jnp.int32).astype(jnp.float32)
    row_ramp = jnp.maximum(ramp_weight(row_place, zone_sizes[0]), ramp_weight(NROW - 1 - row_place, zone_sizes[1]))
    col_ramp = jnp.maximum(ramp_weight(col_place, zone_sizes[2]), ramp_weight(NCOL - 1 - col_place, zone_sizes[3]))
    relax_share = jnp.maximum(row_ramp[:, None], col_ramp[None, :])
    row_share = row_weight[:, None]
    col_share = col_weight[None, :]

    def one_level(bundle):
        band_level, level_state = bundle
        row_mixed = (1.0 - row_share) * band_level[row_index] + row_share * band_level[row_index + 1]
        target = (1.0 - col_share) * row_mixed[:, col_index] + col_share * row_mixed[:, col_index + 1]
        nest_field = level_state.astype(jnp.float32)
        for repeat in range(NSWEEP):
            padded = jnp.pad(nest_field, 1)
            neighbours = padded[2:, 1:-1] + padded[:-2, 1:-1] + padded[1:-1, 2:] + padded[1:-1, :-2]
            nest_field = nest_field + DIFFUSION * (neighbours - 4.0 * nest_field)
            nest_field = nest_field + relax_share * (target - nest_field)
        return nest_field.astype(jnp.bfloat16)

    nest_next = lax.map(one_level, (parent_band, nest_state))
    return parent_band, nest_next
```

```python
import functools
import math

import jax
import jax.numpy as jnp
import numpy as np
from jax import lax
from jax.experimental import pallas as pl
from jax.experimental.pallas import tpu as pltpu
from jax.sharding import PartitionSpec as P

MESH = pl.DeviceIdType.MESH
NW = 16
NY = 16
PD = 40
TRUNC = 1280
NLON = 5120
LON = 32
KF = 24
NLB = 512
NSWEEP = 4
DIFFUSION = 0.2
F32 = jnp.float32
BF16 = jnp.bfloat16
CHUNKS = ((0, 8, 0, 32, 8), (8, 16, 32, 48, 0), (24, 16, 80, 48, 0))
PIECES = ((0, 0, 1280), (1, 0, 1280), (2, 0, 1280))
KOFF = (0, 256, 768)
NKEY = 1280
SLOTS = 56
EXT = 144
WIN = 128
MB = 256


def chunk_consts():
    out = []
    for _, n, _, rows, lead in CHUNKS:
        row = np.arange(2 * n * 16)
        col = np.arange(8 * rows)
        inner = col % rows - lead
        ok = (inner >= 0)
        cpair = np.where(ok, inner % n, -1)
        chan = (col // rows) * 3 + np.maximum(inner, 0) // n
        mask = ((row // 16) % n)[:, None] == cpair[None, :]
        fold = np.zeros((2, 2, 8 * rows, 128), np.float32)
        for nb in range(2):
            for i in range(8 * rows):
                if ok[i]:
                    fold[nb, 0, i, nb * 24 + chan[i]] = 1.0
                    fold[nb, 1, i, 48 + nb * 24 + chan[i]] = 1.0
        out.append((mask.astype(np.float32), fold))
    return out


def split2(x):
    hi = x.astype(BF16)
    lo = (x - hi.astype(F32)).astype(BF16)
    return hi, lo


def dot_nt(a, b):
    return lax.dot_general(a, b, (((1,), (1,)), ((), ())), preferred_element_type=F32)


def dot_nn(a, b):
    return lax.dot_general(a, b, (((1,), (0,)), ((), ())), preferred_element_type=F32)


def ramps(pos, first, last, total):
    return jnp.maximum(
        jnp.maximum(0.0, 1.0 - pos / first), jnp.maximum(0.0, 1.0 - (total - 1 - pos) / last)
    )


def shares(row, col, zone_ref):
    z = [zone_ref[i].astype(F32) for i in range(4)]
    share = jnp.maximum(ramps(row, z[0], z[1], 2048.0), ramps(col, z[2], z[3], 2048.0))
    inside = (row >= 0.0) & (row < 2048.0) & (col >= 0.0) & (col < 2048.0)
    inside = jnp.where(inside, 1.0, 0.0)
    return (1.0 - share) * inside, share * inside


def k1(
    anchor_ref, zone_ref, spec_ref, leg_ref, mask_a, mask_b, fold_a, fold_b, nest_ref,
    ridx_ref, rwt_ref, cidx_ref, cwt_ref,
    win_out, field_out, info_out,
    gath, sp32, leg2, legx, fs, fsend, frecv, tcos, tsin, acc_c, acc_s, psend, prow, pbuf,
    ext, damp, cpk_s, cpk_r, rpk, rpk_s, rpk_r, info_s, info_r, nest_s, nest_r,
    up_s, up_r, dn_s, dn_r, sib_s, sib_r, fa_s, fa_r, w_s, w_r,
):
    w = lax.axis_index("wave")
    y = lax.axis_index("ny")
    wedge = jnp.logical_or(w == 0, w == NW - 1)

    def near(d):
        return lax.rem(y + (NY + d), NY)

    def dev(ww, yy):
        return (ww, yy)

    up_y = lax.rem(y + 2, NY)
    dn_y = lax.rem(y + NY - 2, NY)
    sib_y = y + 1 - 2 * lax.rem(y, 2)

    def zero(i, c):
        pbuf[i] = jnp.zeros((KF, WIN), F32)
        return c
    lax.fori_loop(0, SLOTS, zero, 0)
    cpk_r[...] = jnp.zeros((2, 128, 128), BF16)
    rpk_r[...] = jnp.zeros((2, 96, 256), BF16)
    info_r[...] = jnp.zeros((4, 8, 128), F32)

    barrier = pltpu.get_barrier_semaphore()

    def greet(ww, yy):
        pl.semaphore_signal(barrier, inc=1, device_id=dev(ww, yy), device_id_type=MESH)

    for yy in (up_y, dn_y, sib_y):
        greet(w, yy)

    def greet_wave(o, c):
        greet(lax.rem(w + o, NW), y)
        return c
    lax.fori_loop(1, NW, greet_wave, 0)

    @pl.when(y > 0)
    def _():
        greet(w, near(-1))

    @pl.when(y < NY - 1)
    def _():
        greet(w, near(1))

    @pl.when(jnp.logical_and(wedge, y > 0))
    def _():
        lax.fori_loop(0, NW, lambda o, c: (greet(o, near(-1)), c)[1], 0)

    @pl.when(jnp.logical_and(wedge, y < NY - 1))
    def _():
        lax.fori_loop(0, NW, lambda o, c: (greet(o, near(1)), c)[1], 0)

    @pl.when(jnp.logical_and(wedge, y > 1))
    def _():
        greet(NW - 1, near(-2))

    @pl.when(jnp.logical_and(wedge, y < NY - 2))
    def _():
        greet(0, near(2))

    @pl.when(jnp.logical_and(jnp.logical_not(wedge), y == 0))
    def _():
        greet(0, 1)

    @pl.when(jnp.logical_and(jnp.logical_not(wedge), y == NY - 1))
    def _():
        greet(NW - 1, NY - 2)

    sp32[0:8, :] = jnp.zeros((8, 1408), F32)
    for c in range(3):
        v = spec_ref[c].astype(F32)
        last = jnp.broadcast_to(v[:, 1280:1281], (PD, 128))
        for p0, n, r0, rows, lead in CHUNKS:
            r = r0 + lead + c * n
            sp32[r : r + n, 0:1280] = v[p0 : p0 + n, 0:1280]
            sp32[r : r + n, 1280:1408] = last[p0 : p0 + n, :]
    tail = jnp.transpose(sp32[:, 1280:1408], (1, 0))[0:8, :]
    lane = lax.broadcasted_iota(jnp.int32, (8, 128), 1)
    sub = lax.broadcasted_iota(jnp.int32, (8, 896), 0)
    extra = jnp.zeros((8, 896), F32)
    for ch, (p0, n, r0, rows, lead) in enumerate(CHUNKS):
        part = jnp.where((lane >= r0 + lead) & (lane < r0 + rows), tail, 0.0)
        part = jnp.concatenate([part, jnp.zeros((8, 768), F32)], axis=1)
        part = pltpu.roll(part, lax.rem(y * rows - r0 + 896, 896), 1)
        part = jnp.broadcast_to(part[0:1, :], (8, 896))
        extra = jnp.where(sub == ch, part, extra)
    sp32[0:8, 0:768] = extra[:, 0:768]

    def cast_own(i, c):
        r = pl.multiple_of(i * 16, 16)
        gath[y, pl.ds(r, 16), :] = sp32[pl.ds(r, 16), 0:1280].astype(BF16)
        return c
    lax.fori_loop(0, 8, cast_own, 0)

    count = 15 + 3
    count += jnp.where(y < NY - 1, 3, 0) + jnp.where(y > 0, 3, 0)
    count += jnp.where(jnp.logical_and(w == NW - 1, y < NY - 2), 2, 0)
    count += jnp.where(jnp.logical_and(w == 0, y > 1), 2, 0)
    count += jnp.where(jnp.logical_and(w == 0, y == 1), 14, 0)
    count += jnp.where(jnp.logical_and(w == NW - 1, y == NY - 2), 14, 0)
    pl.semaphore_wait(barrier, count)

    def block(origin, piece, half):
        ch, l0, ln = PIECES[piece]
        _, _, r0, rows, _ = CHUNKS[ch]
        if half == 0:
            ln = ln // 2
        elif half == 1:
            l0, ln = l0 + ln // 2, ln // 2
        return gath.at[origin, pl.ds(r0, rows), pl.ds(l0, ln)]

    def ring(origin, piece, step, upward):
        half = None if step < 3 else (0 if upward else 1)
        ref = block(origin, piece, half)
        s, r = (up_s, up_r) if upward else (dn_s, dn_r)
        return pltpu.make_async_remote_copy(
            src_ref=ref, dst_ref=ref, send_sem=s.at[piece, step], recv_sem=r.at[piece, step],
            device_id=dev(w, up_y if upward else dn_y), device_id_type=MESH)

    def to_sib(origin, piece, idx, half=None):
        ref = block(origin, piece, half)
        return pltpu.make_async_remote_copy(
            src_ref=ref, dst_ref=ref, send_sem=sib_s.at[piece, idx], recv_sem=sib_r.at[piece, idx],
            device_id=dev(w, sib_y), device_id_type=MESH)

    def origin_of(step, upward):
        return lax.rem(y + NY - 2 * step, NY) if upward else lax.rem(y + 2 * step, NY)

    def send_own(piece):
        ring(y, piece, 0, True).start()
        ring(y, piece, 0, False).start()
        to_sib(y, piece, 0).start()

    def ring_step(piece, step):
        for upward in (True, False):
            org = origin_of(step, upward)
            ring(org, piece, step - 1, upward).wait_recv()
            if step < 4:
                ring(org, piece, step, upward).start()
                to_sib(org, piece, 2 * step - (1 if upward else 0)).start()
            else:
                to_sib(org, piece, 7 if upward else 8, 0 if upward else 1).start()

    def sib_wait(piece):
        base = sib_y
        to_sib(base, piece, 0).wait_recv()
        for step in range(1, 5):
            for upward in (True, False):
                org = lax.rem(base + NY - 2 * step, NY) if upward else lax.rem(base + 2 * step, NY)
                if step < 4:
                    to_sib(org, piece, 2 * step - (1 if upward else 0)).wait_recv()
                else:
                    to_sib(org, piece, 7 if upward else 8, 0 if upward else 1).wait_recv()

    def sends_done(piece):
        for step in range(4):
            for upward in (True, False):
                ring(y, piece, step, upward).wait_send()
        for idx in range(7):
            to_sib(y, piece, idx).wait_send()
        to_sib(y, piece, 7, 0).wait_send()
        to_sib(y, piece, 8, 1).wait_send()

    anchor = anchor_ref[0].astype(F32)

    def leg_rows(ch):
        p0, n, _, _, _ = CHUNKS[ch]
        pos = lax.broadcasted_iota(jnp.int32, (1, 1280), 1)
        lane16 = lax.broadcasted_iota(jnp.int32, (1, 256), 1) % 16

        def one(p, c):
            limit = TRUNC - (w * PD + p0 + p)
            low = jnp.where(pos < limit, 1.0, 0.0)
            rows = leg_ref[p0 + p]
            tile = rows[:, 0:1280].astype(F32)
            a = pl.multiple_of(p * 16, 16)
            b = pl.multiple_of(n * 16 + p * 16, 16)
            leg2[ch % 2, pl.ds(a, 16), :] = (tile * low).astype(BF16)
            leg2[ch % 2, pl.ds(b, 16), :] = (tile * (1.0 - low)).astype(BF16)
            last = rows[:, 1280:1281].astype(F32)
            legx[ch % 2, pl.ds(a, 16), :] = jnp.zeros((16, 256), BF16)
            legx[ch % 2, pl.ds(b, 16), :] = jnp.where(lane16 == ch, last, 0.0).astype(BF16)
            return c
        lax.fori_loop(0, n, one, 0)

    def fourier(ch):
        p0, n, r0, rows, lead = CHUNKS[ch]
        m = 2 * n * 16
        mask, fold = (mask_a, fold_a) if ch == 0 else (mask_b, fold_b)
        for nb in range(2):
            g = gath[8 * nb : 8 * nb + 8, r0 : r0 + rows, :].reshape(8 * rows, 1280)
            x = gath[:, 0:16, 8 * rows * nb : 8 * rows * (nb + 1)].reshape(256, 8 * rows)

            def blockm(i, c):
                a = pl.multiple_of(i * MB, MB)
                res = dot_nt(leg2[ch % 2, pl.ds(a, MB), :], g)
                res = res + dot_nn(legx[ch % 2, pl.ds(a, MB), :], x)
                hi, lo = split2(res * mask[pl.ds(a, MB), :].astype(F32))
                part = dot_nn(hi, fold[nb, 0]) + dot_nn(lo, fold[nb, 1])
                part = part.reshape(MB // 16, 16, 128)
                t = pl.ds(pl.multiple_of(i * (MB // 16), MB // 16), MB // 16)
                if nb == 0:
                    fs[t] = part
                else:
                    fs[t] = fs[t] + part
                return c
            lax.fori_loop(0, m // MB, blockm, 0)
        f0 = (0, 16, 48)[ch]
        for l in range(16):
            v = fs[0 : 2 * n, l, :].astype(BF16)
            fsend[l, f0 : f0 + 2 * n, :] = v

    def wave_copy(ch, o):
        n = CHUNKS[ch][1]
        f0 = (0, 16, 48)[ch]
        to = lax.rem(w + o, NW)
        return pltpu.make_async_remote_copy(
            src_ref=fsend.at[to, pl.ds(f0, 2 * n), :], dst_ref=frecv.at[ch, w, pl.ds(0, 2 * n), :],
            send_sem=fa_s.at[ch, o], recv_sem=fa_r.at[ch, o],
            device_id=dev(to, y), device_id_type=MESH)

    def wave_send(ch):
        n = CHUNKS[ch][1]
        f0 = (0, 16, 48)[ch]
        lax.fori_loop(1, NW, lambda o, c: (wave_copy(ch, o).start(), c)[1], 0)
        frecv[ch, w, 0 : 2 * n, :] = fsend[w, f0 : f0 + 2 * n, :]

    def wave_recv(ch):
        lax.fori_loop(1, NW, lambda o, c: (wave_copy(ch, o).wait_recv(), c)[1], 0)

    def wave_done(ch):
        lax.fori_loop(1, NW, lambda o, c: (wave_copy(ch, o).wait_send(), c)[1], 0)

    def table(ch):
        p0, n, _, _, _ = CHUNKS[ch]
        k0 = KOFF[ch]
        shift = 4 if n == 16 else 3

        def one(t, c):
            q = t * 128 + lax.broadcasted_iota(jnp.int32, (1, 128), 1)
            ww = q >> (shift + 1)
            h = (q >> shift) & 1
            pg = ww * PD + p0 + (q & (n - 1))
            mi = jnp.where(h == 0, pg, TRUNC - 1 - pg)
            m = mi.astype(F32)
            s = jnp.where(mi == 0, 1.0, 2.0)

            def angle(x):
                return (x - NLON * jnp.floor(x * (1.0 / NLON))) * (2.0 * math.pi / NLON)

            d = lax.broadcasted_iota(jnp.int32, (LON, 128), 0).astype(F32)
            fine = angle(m * d)
            cf, sf = jnp.cos(fine) * s, jnp.sin(fine) * s
            b = lax.broadcasted_iota(jnp.int32, (16, 128), 0).astype(F32) * LON
            coarse = angle(m * (anchor + b))
            cc, sc = jnp.cos(coarse), jnp.sin(coarse)
            col = pl.multiple_of(k0 + t * 128, 128)
            for i in range(16):
                ci, si = cc[i : i + 1, :], sc[i : i + 1, :]
                vc = ci * cf - si * sf
                vs = -(si * cf + ci * sf)
                hi, lo = split2(vc)
                tcos[0, LON * i : LON * i + LON, pl.ds(col, 128)] = hi
                tcos[1, LON * i : LON * i + LON, pl.ds(col, 128)] = lo
                hi, lo = split2(vs)
                tsin[0, LON * i : LON * i + LON, pl.ds(col, 128)] = hi
                tsin[1, LON * i : LON * i + LON, pl.ds(col, 128)] = lo
            return c
        lax.fori_loop(0, 2 * n * 16 // 128, one, 0)

    def contract(ch):
        n = CHUNKS[ch][1]
        k0, k = KOFF[ch], 2 * n * 16
        f = frecv[ch, :, 0 : 2 * n, :].reshape(k, 128)

        def one(i, c):
            a = pl.multiple_of(i * 128, 128)
            for tab, acc in ((tcos, acc_c), (tsin, acc_s)):
                v = dot_nn(tab[0, pl.ds(a, 128), k0 : k0 + k], f)
                v = v + dot_nn(tab[1, pl.ds(a, 128), k0 : k0 + k], f)
                if ch == 0:
                    acc[pl.ds(a, 128), :] = v
                else:
                    acc[pl.ds(a, 128), :] = acc[pl.ds(a, 128), :] + v
            return c
        lax.fori_loop(0, 4, one, 0)

    lane_h = lax.broadcasted_iota(jnp.int32, (128, 128), 1)

    def nest_copy(i):
        if i < 4:
            src, dst = (cpk_s, cpk_r) if i < 2 else (rpk_s, rpk_r)
            src, dst = src.at[i % 2], dst.at[i % 2]
        else:
            src, dst = info_s, info_r.at[i - 4]
        to = (dev(lax.rem(w + NW - 1, NW), y), dev(lax.rem(w + 1, NW), y), dev(w, near(-1)), dev(w, near(1)))[i % 4]
        return pltpu.make_async_remote_copy(
            src_ref=src, dst_ref=dst, send_sem=nest_s.at[i], recv_sem=nest_r.at[i],
            device_id=to, device_id_type=MESH)

    can_send = (w > 0, w < NW - 1, y > 0, y < NY - 1)
    can_recv = (w < NW - 1, w > 0, y < NY - 1, y > 0)

    def nest_do(which, cond, go):
        for i in which:
            @pl.when(cond[i % 4])
            def _(i=i):
                go(nest_copy(i))

    def nest_pack():
        info_s[...] = jnp.zeros((8, 128), F32)
        info_s[0:1, :] = ridx_ref[...].astype(F32)
        info_s[1:2, :] = rwt_ref[...]
        info_s[2:3, :] = cidx_ref[...].astype(F32)
        info_s[3:4, :] = cwt_ref[...]
        left = jnp.zeros((128, 128), F32)
        right = jnp.zeros((128, 128), F32)
        for k in range(KF):
            v = nest_ref[k].astype(F32)
            here = (lane_h >= 4 * k) & (lane_h < 4 * k + 4)
            left = jnp.where(here, pltpu.roll(v, 4 * k, 1) if k else v, left)
            right = jnp.where(here, pltpu.roll(v, 4 * k + 4, 1), right)
        cpk_s[0] = left.astype(BF16)
        cpk_s[1] = right.astype(BF16)
        row = (lax.broadcasted_iota(jnp.int32, (EXT, 256), 0) + (128 * y - 8)).astype(F32)
        j = lax.broadcasted_iota(jnp.int32, (EXT, 256), 1)
        col = (jnp.where(j < 192, j, j - 256) + 128 * w).astype(F32)
        keep, _ = shares(row, col, zone_ref)
        damp[...] = keep * DIFFUSION
        nest_do((0, 1, 4, 5, 6, 7), can_send, lambda c: c.start())

    def nest_cols():
        nest_do((0, 1), can_recv, lambda c: c.wait_recv())
        from_right = cpk_r[0].astype(F32)
        from_left = cpk_r[1].astype(F32)

        def one(k, c):
            a = pltpu.roll(from_right, lax.rem(128 - 4 * k, 128), 1)
            b = pltpu.roll(from_left, lax.rem(252 - 4 * k, 128), 1)
            e = jnp.where(lane_h < 4, a, jnp.where(lane_h >= 124, b, 0.0))
            ext[k, 0:8, :] = jnp.zeros((8, 256), F32)
            ext[k, 136:144, :] = jnp.zeros((8, 256), F32)
            ext[k, 8:136, 0:128] = nest_ref[k].astype(F32)
            ext[k, 8:136, 128:256] = e
            return c
        lax.fori_loop(0, KF, one, 0)
        for i, r in ((0, 8), (1, 132)):
            for k in range(KF):
                rpk[4 * k : 4 * k + 4, :] = ext[k, r : r + 4, :]
            rpk_s[i] = rpk[...].astype(BF16)
        nest_do((2, 3), can_send, lambda c: c.start())

    def nest_rows():
        nest_do((2, 3), can_recv, lambda c: c.wait_recv())
        for i, r in ((0, 136), (1, 4)):
            rpk[...] = rpk_r[i].astype(F32)
            for k in range(KF):
                ext[k, r : r + 4, :] = rpk[4 * k : 4 * k + 4, :]

    def nest_sweeps(k0, k1_):
        def one(k, c):
            x = ext[k]
            for _ in range(NSWEEP):
                t = x + pltpu.roll(x, 1, 0) + pltpu.roll(x, EXT - 1, 0)
                t = t + pltpu.roll(x, 1, 1) + pltpu.roll(x, 255, 1)
                x = t * damp[...]
            field_out[k] = x[8:136, 0:128]
            return c
        lax.fori_loop(k0, k1_, one, 0)

    def nest_done():
        nest_do((4, 5, 6, 7), can_recv, lambda c: c.wait_recv())
        nest_do(range(8), can_send, lambda c: c.wait_send())
        info_out[0] = info_s[...]
        info_out[1:5] = info_r[...]

    send_own(0)
    send_own(1)
    nest_pack()
    ring_step(0, 1)
    send_own(2)
    table(0)
    table(1)
    leg_rows(0)
    nest_cols()
    ring_step(0, 2)
    ring_step(1, 1)
    table(2)
    nest_rows()
    leg_rows(1)
    ring_step(0, 3)
    ring_step(2, 1)
    nest_sweeps(0, 8)
    ring_step(1, 2)
    ring_step(0, 4)
    sib_wait(0)
    fourier(0)
    wave_send(0)
    ring_step(2, 2)
    nest_sweeps(8, 16)
    ring_step(1, 3)
    wave_recv(0)
    contract(0)
    ring_step(2, 3)
    nest_sweeps(16, KF)
    nest_done()
    ring_step(1, 4)
    sib_wait(1)
    leg_rows(2)
    fourier(1)
    wave_send(1)
    ring_step(2, 4)
    sib_wait(2)
    fourier(2)
    wave_send(2)
    wave_recv(1)
    contract(1)
    wave_recv(2)
    contract(2)

    prow[:, 0:128] = jnp.zeros((KF, 128), F32)
    prow[:, 512:640] = jnp.zeros((KF, 128), F32)
    for i in range(4):
        tc = jnp.transpose(acc_c[128 * i : 128 * i + 128, :], (1, 0))
        ts = jnp.transpose(acc_s[128 * i : 128 * i + 128, :], (1, 0))
        val = tc[0:24] + tc[48:72] + ts[24:48] + ts[72:96]
        prow[:, 48 + 128 * i : 176 + 128 * i] = val
    for v in range(NW):
        psend[v] = prow[:, LON * v : LON * v + WIN]

    def win(src, to_w, to_y, slot, sem):
        return pltpu.make_async_remote_copy(
            src_ref=psend.at[src], dst_ref=pbuf.at[slot], send_sem=w_s.at[sem], recv_sem=w_r.at[slot],
            device_id=dev(to_w, to_y), device_id_type=MESH)

    def edges(go):
        @pl.when(y < NY - 1)
        def _():
            go(0, 0, near(1), 1 + w, 16)
            go(NW - 1, NW - 1, near(1), 1 + w, 17)

        @pl.when(y > 0)
        def _():
            go(0, 0, near(-1), 33 + w, 18)
            go(NW - 1, NW - 1, near(-1), 33 + w, 19)

        @pl.when(jnp.logical_and(w == NW - 1, y < NY - 2))
        def _():
            go(0, 0, near(2), 0, 20)
            go(NW - 1, NW - 1, near(2), 0, 21)

        @pl.when(jnp.logical_and(w == 0, y > 1))
        def _():
            go(0, 0, near(-2), 49, 22)
            go(NW - 1, NW - 1, near(-2), 49, 23)

        @pl.when(jnp.logical_and(w == 0, y == 1))
        def _():
            lax.fori_loop(1, NW - 1, lambda v, c: (go(v, v, near(-1), 33 + w, 24 + v), c)[1], 0)

        @pl.when(jnp.logical_and(w == NW - 1, y == NY - 2))
        def _():
            lax.fori_loop(1, NW - 1, lambda v, c: (go(v, v, near(1), 1 + w, 24 + v), c)[1], 0)

    def own_win(o):
        to = lax.rem(w + o, NW)
        return win(to, to, y, 17 + w, o)

    lax.fori_loop(1, NW, lambda o, c: (own_win(o).start(), c)[1], 0)
    edges(lambda *a: win(*a).start())
    pbuf[17 + w] = psend[w]

    for ch in range(3):
        wave_done(ch)
    for piece in range(len(PIECES)):
        sends_done(piece)

    def got(slot):
        win(0, w, sib_y, slot, 0).wait_recv()

    lax.fori_loop(1, NW, lambda o, c: (got(17 + lax.rem(w + o, NW)), c)[1], 0)

    @pl.when(jnp.logical_and(wedge, y > 0))
    def _():
        lax.fori_loop(0, NW, lambda o, c: (got(1 + o), c)[1], 0)

    @pl.when(jnp.logical_and(wedge, y < NY - 1))
    def _():
        lax.fori_loop(0, NW, lambda o, c: (got(33 + o), c)[1], 0)

    @pl.when(jnp.logical_and(wedge, y > 1))
    def _():
        got(0)

    @pl.when(jnp.logical_and(wedge, y < NY - 2))
    def _():
        got(49)

    @pl.when(jnp.logical_and(jnp.logical_not(wedge), y == 0))
    def _():
        got(33)

    @pl.when(jnp.logical_and(jnp.logical_not(wedge), y == NY - 1))
    def _():
        got(16)

    def copy_out(i, c):
        win_out[i] = pbuf[i]
        return c
    lax.fori_loop(0, SLOTS, copy_out, 0)
    lax.fori_loop(1, NW, lambda o, c: (own_win(o).wait_send(), c)[1], 0)
    edges(lambda *a: win(*a).wait_send())


def vmem_spec():
    return pl.BlockSpec(memory_space=pltpu.VMEM)


def spectral(spectra, legendre, lon_anchor, zone_width, nest_state, ridx, rwt, cidx, cwt):
    spec = jnp.transpose(spectra, (1, 0, 2))
    (mask_a, fold_a), (mask_b, fold_b), _ = chunk_consts()
    np_ = len(PIECES)
    smem = pl.BlockSpec(memory_space=pltpu.SMEM)
    dma = pltpu.SemaphoreType.DMA
    return pl.pallas_call(
        k1,
        out_shape=(
            jax.ShapeDtypeStruct((SLOTS, KF, WIN), F32),
            jax.ShapeDtypeStruct((KF, 128, 128), F32),
            jax.ShapeDtypeStruct((5, 8, 128), F32),
        ),
        in_specs=[smem, smem] + [vmem_spec()] * 11,
        out_specs=(vmem_spec(), vmem_spec(), vmem_spec()),
        scratch_shapes=[
            pltpu.VMEM((NY, 128, 1280), BF16),
            pltpu.VMEM((128, 1408), F32),
            pltpu.VMEM((2, 512, 1280), BF16),
            pltpu.VMEM((2, 512, 256), BF16),
            pltpu.VMEM((32, 16, 128), F32),
            pltpu.VMEM((16, 80, 128), BF16),
            pltpu.VMEM((3, 16, 32, 128), BF16),
            pltpu.VMEM((2, NLB, NKEY), BF16),
            pltpu.VMEM((2, NLB, NKEY), BF16),
            pltpu.VMEM((NLB, 128), F32),
            pltpu.VMEM((NLB, 128), F32),
            pltpu.VMEM((16, KF, WIN), F32),
            pltpu.VMEM((KF, 640), F32),
            pltpu.VMEM((SLOTS, KF, WIN), F32),
            pltpu.VMEM((KF, EXT, 256), F32),
            pltpu.VMEM((EXT, 256), F32),
            pltpu.VMEM((2, 128, 128), BF16),
            pltpu.VMEM((2, 128, 128), BF16),
            pltpu.VMEM((96, 256), F32),
            pltpu.VMEM((2, 96, 256), BF16),
            pltpu.VMEM((2, 96, 256), BF16),
            pltpu.VMEM((8, 128), F32),
            pltpu.VMEM((4, 8, 128), F32),
            dma((8,)), dma((8,)),
            dma((np_, 4)), dma((np_, 4)),
            dma((np_, 4)), dma((np_, 4)),
            dma((np_, 9)), dma((np_, 9)),
            dma((3, 16)), dma((3, 16)),
            dma((40,)), dma((SLOTS,)),
        ],
        compiler_params=pltpu.CompilerParams(
            collective_id=0, has_side_effects=True, vmem_limit_bytes=60 * 1024 * 1024),
    )(lon_anchor, zone_width, spec, legendre,
      jnp.asarray(mask_a, BF16), jnp.asarray(mask_b, BF16),
      jnp.asarray(fold_a, BF16), jnp.asarray(fold_b, BF16),
      nest_state, ridx, rwt, cidx, cwt)


def dot3(a, b):
    ah, al = split2(a)
    bh, bl = split2(b)
    return dot_nn(ah, bh) + dot_nn(ah, bl) + dot_nn(al, bh)


def pick(axis_iota, index, weight):
    return jnp.where(axis_iota == index, 1.0 - weight, 0.0) + jnp.where(
        axis_iota == index + 1.0, weight, 0.0
    )


def fiota(shape, axis):
    return lax.broadcasted_iota(jnp.int32, shape, axis).astype(F32)


def k2(zone_ref, win_ref, field_ref, info_ref, band_out, nest_out, acc, xs, tau):
    w = lax.axis_index("wave")
    y = lax.axis_index("ny")

    def band(k, c):
        v = win_ref[17:33, k, :]
        band_out[k] = pltpu.roll(v, 80, 1)[:, 0:LON]
        return c
    lax.fori_loop(0, KF, band, 0)

    def base(k, c):
        acc[k] = field_ref[k]
        return c
    lax.fori_loop(0, KF, base, 0)

    own, right, left, below, above = (info_ref[i] for i in range(5))
    turned = [jnp.transpose(jnp.concatenate([v, jnp.zeros((120, 128), F32)], 0), (1, 0))
              for v in (own, below, above)]
    lon0 = (w * LON - 48).astype(F32)
    lat0 = (y * 16 - 17).astype(F32)

    @pl.when(jnp.logical_or(y == 0, y == NY - 1))
    def _():
        first = jnp.where(y == 0, 0, 104)
        lane = lax.broadcasted_iota(jnp.int32, (1, 128), 1)
        far_i = jnp.where(lane < 4, right[2:3], jnp.where(lane >= 124, left[2:3], -4096.0))
        far_w = jnp.where(lane < 4, right[3:4], left[3:4])
        cidx = jnp.concatenate([own[2:3], far_i], 1) - lon0
        cwt = jnp.concatenate([own[3:4], far_w], 1)
        cmat = pick(fiota((128, 256), 0), cidx, cwt)

        def cross(i, c):
            xs[i] = dot3(win_ref[16 + i], cmat)
            return c
        lax.fori_loop(0, 18, cross, 0)

        cols = jnp.where(y == 0, turned[0][0:24, :], turned[0][104:128, :])
        ridx = cols[:, 0:1] - lat0 - 16.0
        rwt = cols[:, 1:2]
        row = fiota((24, 256), 0) + (128 * y + first).astype(F32)
        j = lax.broadcasted_iota(jnp.int32, (24, 256), 1)
        col = (jnp.where(j < 192, j, j - 256) + 128 * w).astype(F32)
        keep, share = shares(row, col, zone_ref)
        keep = keep * DIFFUSION
        keep = jnp.where((row < 20.0) | (row >= 2028.0), keep, 0.0)
        share = jnp.where((row < 16.0) | (row >= 2032.0), share, 0.0)
        blend = [jnp.broadcast_to(pick(float(i), ridx, rwt), (24, 256)) for i in range(18)]

        def level(k, c):
            t = jnp.zeros((24, 256), F32)
            for i in range(18):
                t = t + blend[i] * xs[i, pl.ds(k, 1), :]
            q = share * t
            g = q
            for _ in range(NSWEEP - 1):
                v = g + pltpu.roll(g, 1, 0) + pltpu.roll(g, 23, 0)
                v = v + pltpu.roll(g, 1, 1) + pltpu.roll(g, 255, 1)
                g = v * keep + q
            at = pl.ds(pl.multiple_of(first, 8), 24)
            acc[k, at, :] = acc[k, at, :] + g[:, 0:128]
            return c
        lax.fori_loop(0, KF, level, 0)

    @pl.when(jnp.logical_or(w == 0, w == NW - 1))
    def _():
        cbase = jnp.where(w == 0, 0, 96)
        lane = lax.broadcasted_iota(jnp.int32, (1, 128), 1)
        vec = jnp.concatenate([own[2:4] - jnp.where(fiota((2, 128), 0) == 0.0, lon0, 0.0),
                               jnp.zeros((6, 128), F32)], 0)
        vec = jnp.where(w == 0, vec, pltpu.roll(vec, 32, 1))
        mats = []
        for i in range(4):
            v = pltpu.roll(vec, LON * i, 1) if i else vec
            here = (lane >= LON * i) & (lane < LON * i + LON)
            mats.append(jnp.where(here, pick(fiota((128, 128), 0), v[0:1], v[1:2]), 0.0))
        cmat = jnp.concatenate(mats, 0)
        rows = jnp.concatenate([turned[2][120:128], turned[0], turned[1][0:8]], 0)
        rmat = pick(fiota((EXT, SLOTS), 1), rows[:, 0:1] - lat0, rows[:, 1:2])

        row = fiota((EXT, 128), 0) + (128 * y - 8).astype(F32)
        inner = lax.broadcasted_iota(jnp.int32, (EXT, 128), 1) % LON
        col = (inner + cbase + 128 * w).astype(F32)
        keep, share = shares(row, col, zone_ref)
        keep = keep * DIFFUSION
        share = jnp.where((col < 16.0) | (col >= 2032.0), share, 0.0)
        share = jnp.where((row >= 16.0) & (row < 2032.0), share, 0.0)
        not_first = jnp.where(inner == 0, 0.0, 1.0)
        not_last = jnp.where(inner == LON - 1, 0.0, 1.0)
        lane_h = lax.broadcasted_iota(jnp.int32, (128, 128), 1)
        strip = (lane_h >= cbase) & (lane_h < cbase + LON)

        def group(t, c):
            p = jnp.concatenate([win_ref[:, 4 * t + i, :] for i in range(4)], 1)
            q = share * dot3(rmat, dot3(p, cmat))
            g = q
            for _ in range(NSWEEP - 1):
                v = g + pltpu.roll(g, 1, 0) + pltpu.roll(g, EXT - 1, 0)
                v = v + pltpu.roll(g, 1, 1) * not_first + pltpu.roll(g, 127, 1) * not_last
                g = v * keep + q
            g = g[8:136, :]
            for i in range(4):
                part = pltpu.roll(g, lax.rem(cbase + 128 - LON * i, 128), 1)
                acc[4 * t + i] = acc[4 * t + i] + jnp.where(strip, part, 0.0)
            return c
        lax.fori_loop(0, KF // 4, group, 0)

    def last(k, c):
        nest_out[k] = acc[k].astype(BF16)
        return c
    lax.fori_loop(0, KF, last, 0)


def relax(zone_width, windows, field, info):
    return pl.pallas_call(
        k2,
        out_shape=(
            jax.ShapeDtypeStruct((KF, 16, LON), F32),
            jax.ShapeDtypeStruct((KF, 128, 128), BF16),
        ),
        in_specs=[pl.BlockSpec(memory_space=pltpu.SMEM)] + [vmem_spec()] * 3,
        out_specs=(vmem_spec(), vmem_spec()),
        scratch_shapes=[
            pltpu.VMEM((KF, 128, 128), F32),
            pltpu.VMEM((18, KF, 256), F32),
            pltpu.VMEM((8, 128), F32),
        ],
        compiler_params=pltpu.CompilerParams(vmem_limit_bytes=40 * 1024 * 1024),
    )(zone_width, windows, field, info)


def body(
    spectra, legendre, lon_anchor, row_index, row_weight, col_index, col_weight, zone_width,
    nest_state,
):
    windows, field, info = spectral(
        spectra, legendre, lon_anchor, zone_width, nest_state,
        row_index.reshape(1, 128), row_weight.reshape(1, 128),
        col_index.reshape(1, 128), col_weight.reshape(1, 128),
    )
    return relax(zone_width, windows, field, info)


def solution(mesh):
    placed = (
        P("wave", "ny", None), P("wave", "ny", None), P(), P("ny"), P("ny"), P("wave"), P("wave"),
        P(), P(None, "ny", "wave"),
    )
    return jax.shard_map(
        body, mesh=mesh, in_specs=placed,
        out_specs=(P(None, "ny", "wave"), P(None, "ny", "wave")), check_vma=False,
    )
```

```python
import functools
import math

import jax
import jax.numpy as jnp
import numpy as np
from jax import lax
from jax.experimental import pallas as pl
from jax.experimental.pallas import tpu as pltpu
from jax.sharding import PartitionSpec as P

MESH = pl.DeviceIdType.MESH
NW = 16
NY = 16
PD = 40
TRUNC = 1280
NLON = 5120
LON = 32
KF = 24
NLB = 512
NSWEEP = 4
DIFFUSION = 0.2
F32 = jnp.float32
BF16 = jnp.bfloat16
CHUNKS = ((0, 8, 0, 32, 8), (8, 16, 32, 48, 0), (24, 16, 80, 48, 0))
HALVES = (((0, 16), (16, 16)), ((0, 48), (0, 0)), ((0, 0), (0, 48)))
KOFF = (0, 256, 768)
NKEY = 1280
SLOTS = 24
EXT = 144
WIN = 128


def lane_of(chan):
    return 16 * (chan % 8) + chan // 8


def first_consts():
    _, n, _, rows, lead = CHUNKS[0]
    row = np.arange(2 * n * 16)
    col = np.arange(16 * rows)
    inner = col % rows - lead
    cpair = np.where(inner >= 0, inner % n, -1)
    mask = ((row // 16) % n)[:, None] == cpair[None, :]
    fold = np.zeros((2, 16 * rows, 128), np.float32)
    for i in range(16 * rows):
        if inner[i] >= 0:
            lane = lane_of((i // rows) * 3 + inner[i] // n)
            fold[0, i, lane] = 1.0
            fold[1, i, lane + 8] = 1.0
    return mask.astype(np.float32), fold


def split2(x):
    hi = x.astype(BF16)
    lo = (x - hi.astype(F32)).astype(BF16)
    return hi, lo


def dot_nt(a, b):
    return lax.dot_general(a, b, (((1,), (1,)), ((), ())), preferred_element_type=F32)


def dot_nn(a, b):
    return lax.dot_general(a, b, (((1,), (0,)), ((), ())), preferred_element_type=F32)


def ramps(pos, first, last, total):
    return jnp.maximum(
        jnp.maximum(0.0, 1.0 - pos / first), jnp.maximum(0.0, 1.0 - (total - 1 - pos) / last)
    )


def shares(row, col, zone_ref):
    z = [zone_ref[i].astype(F32) for i in range(4)]
    share = jnp.maximum(ramps(row, z[0], z[1], 2048.0), ramps(col, z[2], z[3], 2048.0))
    inside = (row >= 0.0) & (row < 2048.0) & (col >= 0.0) & (col < 2048.0)
    inside = jnp.where(inside, 1.0, 0.0)
    return (1.0 - share) * inside, share * inside


def dot3(a, bh, bl):
    ah, al = split2(a)
    return dot_nn(ah, bh) + dot_nn(ah, bl) + dot_nn(al, bh)


def pick(axis_iota, index, weight):
    return jnp.where(axis_iota == index, 1.0 - weight, 0.0) + jnp.where(
        axis_iota == index + 1.0, weight, 0.0
    )


def fiota(shape, axis):
    return lax.broadcasted_iota(jnp.int32, shape, axis).astype(F32)


def k1(
    anchor_ref, zone_ref, spec_ref, ridx_ref, rwt_ref, cidx_ref, cwt_ref,
    leg_hbm, mask_hbm, fold_hbm, nest_hbm,
    band_out, nest_out,
    leg_ref, mask_ref, fold_ref, nest_ref, load_s,
    gath, sp32, leg2, legx, fs, fsend, frecv, tcos, tsin, acc_c, acc_s, turn, psend, prow, pbuf,
    ext, damp, cpk_s, cpk_r, rpk, rpk_s, rpk_r, info_s, info_r, nest_s, nest_r,
    field, row_mats, row_part, row_blend, row_x, col_mats, col_part, col_blend, col_p, col_q,
    q_out, q_in, q_s, q_r,
    up_s, up_r, dn_s, dn_r, sib_s, sib_r, fa_s, fa_r, w_s, w_r,
):
    w = lax.axis_index("wave")
    y = lax.axis_index("ny")
    wedge = jnp.logical_or(w == 0, w == NW - 1)

    def near(d):
        return lax.rem(y + (NY + d), NY)

    def dev(ww, yy):
        return (ww, yy)

    up_y = lax.rem(y + 2, NY)
    dn_y = lax.rem(y + NY - 2, NY)
    sib_y = y + 1 - 2 * lax.rem(y, 2)

    loads = [pltpu.make_async_copy(a, b, load_s.at[i]) for i, (a, b) in enumerate((
        (nest_hbm, nest_ref), (leg_hbm, leg_ref), (mask_hbm, mask_ref), (fold_hbm, fold_ref)))]
    for c in loads:
        c.start()

    def zero(i, c):
        pbuf[i] = jnp.zeros((KF, WIN), F32)
        return c
    lax.fori_loop(0, SLOTS, zero, 0)
    cpk_r[...] = jnp.zeros((2, 128, 128), BF16)
    rpk_r[...] = jnp.zeros((2, 96, 256), BF16)
    info_r[...] = jnp.zeros((2, 8, 128), F32)
    q_in[...] = jnp.zeros((2, 8, 768), F32)

    barrier = pltpu.get_barrier_semaphore()

    def greet(ww, yy):
        pl.semaphore_signal(barrier, inc=1, device_id=dev(ww, yy), device_id_type=MESH)

    for yy in (up_y, dn_y, sib_y):
        greet(w, yy)

    def greet_wave(o, c):
        greet(lax.rem(w + o, NW), y)
        return c
    lax.fori_loop(1, NW, greet_wave, 0)

    @pl.when(y > 0)
    def _():
        greet(w, near(-1))

    @pl.when(y < NY - 1)
    def _():
        greet(w, near(1))

    @pl.when(jnp.logical_or(jnp.logical_and(wedge, y > 0), y == NY - 1))
    def _():
        greet(NW - 1, near(-1))

    @pl.when(jnp.logical_or(jnp.logical_and(wedge, y < NY - 1), y == 0))
    def _():
        greet(0, near(1))

    sp32[0:8, :] = jnp.zeros((8, 1408), F32)
    for c in range(3):
        v = spec_ref[c].astype(F32)
        last = jnp.broadcast_to(v[:, 1280:1281], (PD, 128))
        for p0, n, r0, rows, lead in CHUNKS:
            r = r0 + lead + c * n
            sp32[r : r + n, 0:1280] = v[p0 : p0 + n, 0:1280]
            sp32[r : r + n, 1280:1408] = last[p0 : p0 + n, :]
    tail = jnp.transpose(sp32[:, 1280:1408], (1, 0))[0:8, :]
    lane = lax.broadcasted_iota(jnp.int32, (8, 128), 1)
    sub = lax.broadcasted_iota(jnp.int32, (8, 896), 0)
    extra = jnp.zeros((8, 896), F32)
    for ch, (p0, n, r0, rows, lead) in enumerate(CHUNKS):
        part = jnp.where((lane >= r0 + lead) & (lane < r0 + rows), tail, 0.0)
        part = jnp.concatenate([part, jnp.zeros((8, 768), F32)], axis=1)
        part = pltpu.roll(part, lax.rem(y * rows - r0 + 896, 896), 1)
        part = jnp.broadcast_to(part[0:1, :], (8, 896))
        extra = jnp.where(sub == ch, part, extra)
    sp32[0:8, 0:768] = extra[:, 0:768]

    def cast_own(i, c):
        r = pl.multiple_of(i * 16, 16)
        gath[y, pl.ds(r, 16), :] = sp32[pl.ds(r, 16), 0:1280].astype(BF16)
        return c
    lax.fori_loop(0, 8, cast_own, 0)

    count = 15 + 3
    count += jnp.where(y < NY - 1, 1, 0) + jnp.where(y > 0, 1, 0)
    count += jnp.where(jnp.logical_and(w == NW - 1, y < NY - 1), 2, 0)
    count += jnp.where(jnp.logical_and(w == 0, y > 0), 2, 0)
    count += jnp.where(jnp.logical_and(w == 0, y == 1), 14, 0)
    count += jnp.where(jnp.logical_and(w == NW - 1, y == NY - 2), 14, 0)
    pl.semaphore_wait(barrier, count)

    def block(origin, piece, half):
        _, _, r0, rows, _ = CHUNKS[piece]
        if half is not None:
            first, count_ = HALVES[piece][half]
            r0, rows = r0 + first, count_
        return gath.at[origin, pl.ds(r0, rows), :]

    def ring(origin, piece, step, upward):
        ref = block(origin, piece, None if step < 3 else (0 if upward else 1))
        s, r = (up_s, up_r) if upward else (dn_s, dn_r)
        return pltpu.make_async_remote_copy(
            src_ref=ref, dst_ref=ref, send_sem=s.at[piece, step], recv_sem=r.at[piece, step],
            device_id=dev(w, up_y if upward else dn_y), device_id_type=MESH)

    def to_sib(origin, piece, idx, half=None):
        ref = block(origin, piece, half)
        return pltpu.make_async_remote_copy(
            src_ref=ref, dst_ref=ref, send_sem=sib_s.at[piece, idx], recv_sem=sib_r.at[piece, idx],
            device_id=dev(w, sib_y), device_id_type=MESH)

    def origin_of(base, step, upward):
        return lax.rem(base + NY - 2 * step, NY) if upward else lax.rem(base + 2 * step, NY)

    def far(piece, upward):
        return HALVES[piece][0 if upward else 1][1] > 0

    def send_own(piece):
        ring(y, piece, 0, True).start()
        ring(y, piece, 0, False).start()
        to_sib(y, piece, 0).start()

    def ring_step(piece, step):
        for upward in (True, False):
            org = origin_of(y, step, upward)
            if step < 4:
                ring(org, piece, step - 1, upward).wait_recv()
                if step < 3 or far(piece, upward):
                    ring(org, piece, step, upward).start()
                to_sib(org, piece, 2 * step - (1 if upward else 0)).start()
            elif far(piece, upward):
                ring(org, piece, 3, upward).wait_recv()
                to_sib(org, piece, 7 if upward else 8, 0 if upward else 1).start()

    def sib_each(base, piece, go):
        go(to_sib(base, piece, 0))
        for step in range(1, 5):
            for upward in (True, False):
                org = origin_of(base, step, upward)
                if step < 4:
                    go(to_sib(org, piece, 2 * step - (1 if upward else 0)))
                elif far(piece, upward):
                    go(to_sib(org, piece, 7 if upward else 8, 0 if upward else 1))

    def sib_wait(piece):
        sib_each(sib_y, piece, lambda c: c.wait_recv())

    def sends_done(piece):
        for step in range(4):
            for upward in (True, False):
                if step < 3 or far(piece, upward):
                    ring(y, piece, step, upward).wait_send()
        sib_each(y, piece, lambda c: c.wait_send())

    anchor = anchor_ref[0].astype(F32)

    def leg_rows(ch):
        p0, n, _, _, _ = CHUNKS[ch]
        pos = lax.broadcasted_iota(jnp.int32, (1, 1280), 1)

        def one(p, c):
            limit = TRUNC - (w * PD + p0 + p)
            low = jnp.where(pos < limit, 1.0, 0.0)
            rows = leg_ref[p0 + p]
            tile = rows[:, 0:1280]
            a = pl.multiple_of(p * 16, 16)
            b = pl.multiple_of(n * 16 + p * 16, 16)
            leg2[ch % 2, pl.ds(a, 16), :] = tile * low.astype(BF16)
            leg2[ch % 2, pl.ds(b, 16), :] = tile * (1.0 - low).astype(BF16)
            last = rows[:, 1280:1281].astype(F32)
            legx[ch % 2, pl.ds(a, 16), :] = jnp.broadcast_to(last, (16, 128))
            return c
        lax.fori_loop(0, n, one, 0)

    def last_row(ch, width):
        v = gath[0, 0:16, 0:width].astype(F32)
        for i in range(1, NY):
            v = v + gath[i, 0:16, 0:width].astype(F32)
        return v[ch : ch + 1, :]

    def fourier(ch):
        p0, n, r0, rows, lead = CHUNKS[ch]
        width = 16 * rows
        g = gath[:, r0 : r0 + rows, :].reshape(width, 1280)
        x = last_row(ch, width)
        lane16 = lax.broadcasted_iota(jnp.int32, (16, 128), 1) % 16
        if ch == 0:
            res = dot_nt(leg2[0, 0:256, :], g)
            rank1 = jnp.concatenate([jnp.zeros((128, width), F32),
                                     jnp.tile(legx[0, 0:128, :], (1, width // 128)) * x], 0)
            hi, lo = split2((res + rank1) * mask_ref[...].astype(F32))
            fs[0:16] = (dot_nn(hi, fold_ref[0]) + dot_nn(lo, fold_ref[1])).reshape(16, 16, 128)
        else:
            for h in range(2):
                res = dot_nt(leg2[ch % 2, 256 * h : 256 * h + 256, :], g)
                for p in range(n):
                    v = jnp.zeros((16, 128), F32)
                    for j in range(width // 128):
                        q = res[16 * p : 16 * p + 16, 128 * j : 128 * j + 128]
                        if h == 1:
                            q = q + legx[ch % 2, 16 * p : 16 * p + 16, :] * x[:, 128 * j : 128 * j + 128]
                        q = jnp.where(lane16 == p, q, 0.0)
                        v = v + (pltpu.roll(q, (j - p) % 128, 1) if j != p else q)
                    hi = v.astype(BF16).astype(F32)
                    lo = (v - hi).astype(BF16).astype(F32)
                    fs[16 * h + p] = hi + pltpu.roll(lo, 8, 1)
        f0 = (0, 16, 48)[ch]
        for l in range(16):
            fsend[l, f0 : f0 + 2 * n, :] = fs[0 : 2 * n, l, :].astype(BF16)

    def wave_copy(ch, o):
        n = CHUNKS[ch][1]
        f0 = (0, 16, 48)[ch]
        to = lax.rem(w + o, NW)
        return pltpu.make_async_remote_copy(
            src_ref=fsend.at[to, pl.ds(f0, 2 * n), :], dst_ref=frecv.at[ch, w, pl.ds(0, 2 * n), :],
            send_sem=fa_s.at[ch, o], recv_sem=fa_r.at[ch, o],
            device_id=dev(to, y), device_id_type=MESH)

    def wave_send(ch):
        n = CHUNKS[ch][1]
        f0 = (0, 16, 48)[ch]
        lax.fori_loop(1, NW, lambda o, c: (wave_copy(ch, o).start(), c)[1], 0)
        frecv[ch, w, 0 : 2 * n, :] = fsend[w, f0 : f0 + 2 * n, :]

    def wave_recv(ch):
        lax.fori_loop(1, NW, lambda o, c: (wave_copy(ch, o).wait_recv(), c)[1], 0)

    def wave_done(ch):
        lax.fori_loop(1, NW, lambda o, c: (wave_copy(ch, o).wait_send(), c)[1], 0)

    def table(ch):
        p0, n, _, _, _ = CHUNKS[ch]
        k0 = KOFF[ch]
        shift = 4 if n == 16 else 3

        def one(t, c):
            q = t * 128 + lax.broadcasted_iota(jnp.int32, (1, 128), 1)
            ww = q >> (shift + 1)
            h = (q >> shift) & 1
            pg = ww * PD + p0 + (q & (n - 1))
            mi = jnp.where(h == 0, pg, TRUNC - 1 - pg)
            m = mi.astype(F32)
            s = jnp.where(mi == 0, 1.0, 2.0)

            def angle(x):
                return (x - NLON * jnp.floor(x * (1.0 / NLON))) * (2.0 * math.pi / NLON)

            d = lax.broadcasted_iota(jnp.int32, (LON, 128), 0).astype(F32)
            fine = angle(m * d)
            cf, sf = jnp.cos(fine) * s, jnp.sin(fine) * s
            b = lax.broadcasted_iota(jnp.int32, (16, 128), 0).astype(F32) * LON
            coarse = angle(m * (anchor + b))
            cc, sc = jnp.cos(coarse), jnp.sin(coarse)
            col = pl.multiple_of(k0 + t * 128, 128)
            for i in range(16):
                ci, si = cc[i : i + 1, :], sc[i : i + 1, :]
                vc = ci * cf - si * sf
                vs = -(si * cf + ci * sf)
                hi, lo = split2(vc)
                tcos[0, LON * i : LON * i + LON, pl.ds(col, 128)] = hi
                tcos[1, LON * i : LON * i + LON, pl.ds(col, 128)] = lo
                hi, lo = split2(vs)
                tsin[0, LON * i : LON * i + LON, pl.ds(col, 128)] = hi
                tsin[1, LON * i : LON * i + LON, pl.ds(col, 128)] = lo
            return c
        lax.fori_loop(0, 2 * n * 16 // 128, one, 0)

    def contract(ch):
        n = CHUNKS[ch][1]
        k0, k = KOFF[ch], 2 * n * 16
        f = frecv[ch, :, 0 : 2 * n, :].reshape(k, 128)

        for tab, acc in ((tcos, acc_c), (tsin, acc_s)):
            v = dot_nn(tab[0, :, k0 : k0 + k], f) + dot_nn(tab[1, :, k0 : k0 + k], f)
            if ch == 0:
                acc[...] = v
            else:
                acc[...] = acc[...] + v

    lane_h = lax.broadcasted_iota(jnp.int32, (128, 128), 1)

    def nest_copy(i):
        if i < 4:
            src, dst = (cpk_s, cpk_r) if i < 2 else (rpk_s, rpk_r)
            src, dst = src.at[i % 2], dst.at[i % 2]
        else:
            src, dst = info_s, info_r.at[i - 4]
        to = (dev(lax.rem(w + NW - 1, NW), y), dev(lax.rem(w + 1, NW), y), dev(w, near(-1)), dev(w, near(1)))[i % 4]
        return pltpu.make_async_remote_copy(
            src_ref=src, dst_ref=dst, send_sem=nest_s.at[i], recv_sem=nest_r.at[i],
            device_id=to, device_id_type=MESH)

    can_send = (w > 0, w < NW - 1, y > 0, y < NY - 1)
    can_recv = (w < NW - 1, w > 0, y < NY - 1, y > 0)

    def nest_do(which, cond, go):
        for i in which:
            @pl.when(cond[i % 4])
            def _(i=i):
                go(nest_copy(i))

    def nest_pack():
        info_s[...] = jnp.zeros((8, 128), F32)
        info_s[0:1, :] = ridx_ref[...].astype(F32)
        info_s[1:2, :] = rwt_ref[...]
        loads[0].wait()
        info_s[2:3, :] = cidx_ref[...].astype(F32)
        info_s[3:4, :] = cwt_ref[...]
        left = jnp.zeros((128, 128), F32)
        right = jnp.zeros((128, 128), F32)
        for k in range(KF):
            v = nest_ref[k].astype(F32)
            here = (lane_h >= 4 * k) & (lane_h < 4 * k + 4)
            left = jnp.where(here, pltpu.roll(v, 4 * k, 1) if k else v, left)
            right = jnp.where(here, pltpu.roll(v, 4 * k + 4, 1), right)
        cpk_s[0] = left.astype(BF16)
        cpk_s[1] = right.astype(BF16)
        row = (lax.broadcasted_iota(jnp.int32, (EXT, 256), 0) + (128 * y - 8)).astype(F32)
        j = lax.broadcasted_iota(jnp.int32, (EXT, 256), 1)
        col = (jnp.where(j < 192, j, j - 256) + 128 * w).astype(F32)
        keep, _ = shares(row, col, zone_ref)
        damp[...] = keep * DIFFUSION
        nest_do((0, 1, 4, 5), can_send, lambda c: c.start())

    def nest_cols():
        nest_do((0, 1), can_recv, lambda c: c.wait_recv())
        from_right = cpk_r[0].astype(F32)
        from_left = cpk_r[1].astype(F32)

        def one(k, c):
            a = pltpu.roll(from_right, lax.rem(128 - 4 * k, 128), 1)
            b = pltpu.roll(from_left, lax.rem(252 - 4 * k, 128), 1)
            e = jnp.where(lane_h < 4, a, jnp.where(lane_h >= 124, b, 0.0))
            ext[k, 0:8, :] = jnp.zeros((8, 256), F32)
            ext[k, 136:144, :] = jnp.zeros((8, 256), F32)
            ext[k, 8:136, 0:128] = nest_ref[k].astype(F32)
            ext[k, 8:136, 128:256] = e
            return c
        lax.fori_loop(0, KF, one, 0)
        for i, r in ((0, 8), (1, 132)):
            for k in range(KF):
                rpk[4 * k : 4 * k + 4, :] = ext[k, r : r + 4, :]
            rpk_s[i] = rpk[...].astype(BF16)
        nest_do((2, 3), can_send, lambda c: c.start())

    def nest_rows():
        nest_do((2, 3), can_recv, lambda c: c.wait_recv())
        for i, r in ((0, 136), (1, 4)):
            rpk[...] = rpk_r[i].astype(F32)
            for k in range(KF):
                ext[k, r : r + 4, :] = rpk[4 * k : 4 * k + 4, :]

    def nest_sweeps(k0, k1_):
        def one(k, c):
            x = ext[k]
            for _ in range(NSWEEP):
                t = x + pltpu.roll(x, 1, 0) + pltpu.roll(x, EXT - 1, 0)
                t = t + pltpu.roll(x, 1, 1) + pltpu.roll(x, 255, 1)
                x = t * damp[...]
            field[k] = x[8:136, 0:128]
            nest_out[k] = x[8:136, 0:128].astype(BF16)
            return c
        lax.fori_loop(k0, k1_, one, 0)

    def nest_done():
        nest_do((4, 5), can_recv, lambda c: c.wait_recv())
        nest_do(range(6), can_send, lambda c: c.wait_send())

    row_edge = jnp.logical_or(y == 0, y == NY - 1)
    first = jnp.where(y == 0, 0, 104)
    cbase = jnp.where(w == 0, 0, 96)

    def strip_prep():
        lon0 = (w * LON - 48).astype(F32)
        lat0 = (y * 16 - 1).astype(F32)
        own, right, left = info_s[...], info_r[0], info_r[1]
        lane = lax.broadcasted_iota(jnp.int32, (1, 128), 1)
        turned = jnp.transpose(jnp.concatenate([own, jnp.zeros((120, 128), F32)], 0), (1, 0))

        @pl.when(row_edge)
        def _():
            far_i = jnp.where(lane < 4, right[2:3], jnp.where(lane >= 124, left[2:3], -4096.0))
            far_w = jnp.where(lane < 4, right[3:4], left[3:4])
            cidx = jnp.concatenate([own[2:3], far_i], 1) - lon0
            cwt = jnp.concatenate([own[3:4], far_w], 1)
            hi, lo = split2(pick(fiota((128, 256), 0), cidx, cwt))
            row_mats[0] = hi
            row_mats[1] = lo
            cols = jnp.where(y == 0, turned[0:24, :], turned[104:128, :])
            ridx = cols[:, 0:1] - lat0
            rwt = cols[:, 1:2]
            row = fiota((24, 256), 0) + (128 * y + first).astype(F32)
            j = lax.broadcasted_iota(jnp.int32, (24, 256), 1)
            col = (jnp.where(j < 192, j, j - 256) + 128 * w).astype(F32)
            keep, share = shares(row, col, zone_ref)
            row_part[0] = jnp.where((row < 20.0) | (row >= 2028.0), keep * DIFFUSION, 0.0)
            row_part[1] = jnp.where((row < 16.0) | (row >= 2032.0), share, 0.0)
            for i in range(18):
                row_blend[i] = jnp.broadcast_to(pick(float(i), ridx, rwt), (24, 256))

        @pl.when(wedge)
        def _():
            vec = jnp.concatenate([own[2:4] - jnp.where(fiota((2, 128), 0) == 0.0, lon0, 0.0),
                                   jnp.zeros((6, 128), F32)], 0)
            vec = jnp.where(w == 0, vec, pltpu.roll(vec, 32, 1))
            for i in range(4):
                v = pltpu.roll(vec, LON * i, 1) if i else vec
                here = (lane >= LON * i) & (lane < LON * i + LON)
                m = jnp.where(here, pick(fiota((128, 128), 0), v[0:1], v[1:2]), 0.0)
                hi, lo = split2(m)
                col_mats[0, 128 * i : 128 * i + 128, :] = hi
                col_mats[1, 128 * i : 128 * i + 128, :] = lo
            col_blend[...] = pick(fiota((128, SLOTS), 1), turned[:, 0:1] - lat0, turned[:, 1:2])
            row = fiota((EXT, 128), 0) + (128 * y - 8).astype(F32)
            inner = lax.broadcasted_iota(jnp.int32, (EXT, 128), 1) % LON
            col = (inner + cbase + 128 * w).astype(F32)
            keep, share = shares(row, col, zone_ref)
            share = jnp.where((col < 16.0) | (col >= 2032.0), share, 0.0)
            col_part[0] = keep * DIFFUSION
            col_part[1] = jnp.where((row >= 16.0) & (row < 2032.0), share, 0.0)

    def q_copy(i):
        return pltpu.make_async_remote_copy(
            src_ref=q_out.at[i], dst_ref=q_in.at[i], send_sem=q_s.at[i], recv_sem=q_r.at[i],
            device_id=dev(w, near(1 if i else -1)), device_id_type=MESH)

    def q_each(cond, go):
        for i in range(2):
            @pl.when(jnp.logical_and(wedge, cond[i]))
            def _(i=i):
                go(q_copy(i))

    q_send = (y > 0, y < NY - 1)
    q_recv = (y < NY - 1, y > 0)

    def col_source():
        @pl.when(wedge)
        def _():
            for t in range(KF // 4):
                for i in range(4):
                    col_p[24 * t : 24 * t + 24, 128 * i : 128 * i + 128] = pbuf[:, 4 * t + i, :]
            v = dot3(col_p[...], col_mats[0], col_mats[1])
            v = jnp.concatenate([v[24 * t : 24 * t + 24, :] for t in range(KF // 4)], 1)
            hi, lo = split2(v)
            v = dot3(col_blend[...], hi, lo)
            share = col_part[1, 8:136, :]
            for t in range(KF // 4):
                col_q[8:136, 128 * t : 128 * t + 128] = v[:, 128 * t : 128 * t + 128] * share
            q_out[0] = col_q[8:16, :]
            q_out[1] = col_q[128:136, :]

        q_each(q_send, lambda c: c.start())

    def row_strip():
        @pl.when(row_edge)
        def _():
            x = dot3(pbuf[0:18].reshape(18 * KF, WIN), row_mats[0], row_mats[1])
            row_x[...] = x.reshape(18, KF, 256)
            at = pl.ds(pl.multiple_of(first, 8), 24)

            def some(n, c):
                ks = [n * 6 + i for i in range(6)]
                qs = []
                for k in ks:
                    v = jnp.zeros((24, 256), F32)
                    for i in range(18):
                        v = v + row_blend[i] * row_x[i, pl.ds(k, 1), :]
                    qs.append(v * row_part[1])
                gs = list(qs)
                for _ in range(NSWEEP - 1):
                    vs = [g + pltpu.roll(g, 1, 0) + pltpu.roll(g, 23, 0)
                          + pltpu.roll(g, 1, 1) + pltpu.roll(g, 255, 1) for g in gs]
                    gs = [v * row_part[0] + q for v, q in zip(vs, qs)]
                for k, g in zip(ks, gs):
                    field[k, at, :] = field[k, at, :] + g[:, 0:128]
                return c
            lax.fori_loop(0, KF // 6, some, 0)

    def col_strip():
        q_each(q_recv, lambda c: c.wait_recv())

        @pl.when(wedge)
        def _():
            col_q[136:144, :] = q_in[0]
            col_q[0:8, :] = q_in[1]
            inner = lax.broadcasted_iota(jnp.int32, (EXT, 128), 1) % LON
            not_first = inner != 0
            not_last = inner != LON - 1
            lane_h = lax.broadcasted_iota(jnp.int32, (128, 128), 1)
            strip = (lane_h >= cbase) & (lane_h < cbase + LON)

            def some(n, c):
                ts = [n * 2 + i for i in range(2)]
                at = [pl.ds(pl.multiple_of(t * 128, 128), 128) for t in ts]
                gs = [col_q[:, a] for a in at]
                for _ in range(NSWEEP - 1):
                    vs = [g + pltpu.roll(g, 1, 0) + pltpu.roll(g, EXT - 1, 0)
                          + jnp.where(not_first, pltpu.roll(g, 1, 1), 0.0)
                          + jnp.where(not_last, pltpu.roll(g, 127, 1), 0.0) for g in gs]
                    gs = [v * col_part[0] + col_q[:, a] for v, a in zip(vs, at)]
                for t, g in zip(ts, gs):
                    g = g[8:136, :]
                    for i in range(4):
                        part = pltpu.roll(g, lax.rem(cbase + 128 - LON * i, 128), 1)
                        field[4 * t + i] = field[4 * t + i] + jnp.where(strip, part, 0.0)
                return c
            lax.fori_loop(0, KF // 8, some, 0)

    send_own(0)
    send_own(1)
    nest_pack()
    ring_step(0, 1)
    send_own(2)
    table(0)
    table(1)
    loads[1].wait()
    leg_rows(0)
    nest_cols()
    ring_step(0, 2)
    ring_step(1, 1)
    table(2)
    nest_rows()
    leg_rows(1)
    ring_step(0, 3)
    ring_step(2, 1)
    nest_sweeps(0, 8)
    ring_step(1, 2)
    ring_step(0, 4)
    sib_wait(0)
    loads[2].wait()
    loads[3].wait()
    fourier(0)
    wave_send(0)
    ring_step(2, 2)
    nest_sweeps(8, 16)
    ring_step(1, 3)
    wave_recv(0)
    contract(0)
    ring_step(2, 3)
    nest_sweeps(16, KF)
    nest_done()
    strip_prep()
    ring_step(1, 4)
    sib_wait(1)
    leg_rows(2)
    fourier(1)
    wave_send(1)
    ring_step(2, 4)
    sib_wait(2)
    fourier(2)
    wave_send(2)
    wave_recv(1)
    contract(1)
    wave_recv(2)
    contract(2)

    prow[:, 0:128] = jnp.zeros((KF, 128), F32)
    prow[:, 512:640] = jnp.zeros((KF, 128), F32)
    for i in range(4):
        turn[0] = jnp.transpose(acc_c[128 * i : 128 * i + 128, :], (1, 0)).reshape(8, 16, 128)
        turn[1] = jnp.transpose(acc_s[128 * i : 128 * i + 128, :], (1, 0)).reshape(8, 16, 128)
        val = [turn[0, :, j, :] + turn[0, :, j + 8, :] + turn[1, :, j + 3, :] + turn[1, :, j + 11, :]
               for j in range(3)]
        prow[:, 48 + 128 * i : 176 + 128 * i] = jnp.concatenate(val, 0)
    for v in range(NW):
        psend[v] = prow[:, LON * v : LON * v + WIN]

    def win(src, to_w, to_y, slot, sem):
        return pltpu.make_async_remote_copy(
            src_ref=psend.at[src], dst_ref=pbuf.at[slot], send_sem=w_s.at[sem], recv_sem=w_r.at[slot],
            device_id=dev(to_w, to_y), device_id_type=MESH)

    def edges(go):
        @pl.when(jnp.logical_and(w == 0, y > 0))
        def _():
            go(0, 0, near(-1), 17, 16)
            go(NW - 1, NW - 1, near(-1), 17, 17)

        @pl.when(jnp.logical_and(w == NW - 1, y < NY - 1))
        def _():
            go(0, 0, near(1), 0, 18)
            go(NW - 1, NW - 1, near(1), 0, 19)

        @pl.when(jnp.logical_and(w == 0, y == 1))
        def _():
            lax.fori_loop(1, NW - 1, lambda v, c: (go(v, v, near(-1), 17, 20 + v), c)[1], 0)

        @pl.when(jnp.logical_and(w == NW - 1, y == NY - 2))
        def _():
            lax.fori_loop(1, NW - 1, lambda v, c: (go(v, v, near(1), 0, 20 + v), c)[1], 0)

    def own_win(o):
        to = lax.rem(w + o, NW)
        return win(to, to, y, 1 + w, o)

    lax.fori_loop(1, NW, lambda o, c: (own_win(o).start(), c)[1], 0)
    edges(lambda *a: win(*a).start())
    pbuf[1 + w] = psend[w]

    for ch in range(3):
        wave_done(ch)
    for piece in range(len(CHUNKS)):
        sends_done(piece)

    def got(slot):
        win(0, w, sib_y, slot, 0).wait_recv()

    lax.fori_loop(1, NW, lambda o, c: (got(1 + lax.rem(w + o, NW)), c)[1], 0)

    @pl.when(jnp.logical_or(jnp.logical_and(wedge, y > 0), y == NY - 1))
    def _():
        got(0)

    @pl.when(jnp.logical_or(jnp.logical_and(wedge, y < NY - 1), y == 0))
    def _():
        got(17)

    col_source()
    row_strip()
    col_strip()

    @pl.when(jnp.logical_or(wedge, row_edge))
    def _():
        def last(k, c):
            nest_out[k] = field[k].astype(BF16)
            return c
        lax.fori_loop(0, KF, last, 0)

    for k in range(KF):
        band_out[k] = pltpu.roll(pbuf[1:17, k, :], 80, 1)[:, 0:LON]
    q_each(q_send, lambda c: c.wait_send())
    lax.fori_loop(1, NW, lambda o, c: (own_win(o).wait_send(), c)[1], 0)
    edges(lambda *a: win(*a).wait_send())


def vmem_spec():
    return pl.BlockSpec(memory_space=pltpu.VMEM)


def spectral(spectra, legendre, lon_anchor, zone_width, nest_state, ridx, rwt, cidx, cwt):
    spec = jnp.transpose(spectra, (1, 0, 2))
    mask, fold = first_consts()
    np_ = len(CHUNKS)
    smem = pl.BlockSpec(memory_space=pltpu.SMEM)
    dma = pltpu.SemaphoreType.DMA
    return pl.pallas_call(
        k1,
        out_shape=(
            jax.ShapeDtypeStruct((KF, 16, LON), F32),
            jax.ShapeDtypeStruct((KF, 128, 128), BF16),
        ),
        in_specs=[smem, smem] + [vmem_spec()] * 5 + [pl.BlockSpec(memory_space=pl.ANY)] * 4,
        out_specs=(vmem_spec(), vmem_spec()),
        scratch_shapes=[
            pltpu.VMEM((PD, 16, 1281), BF16),
            pltpu.VMEM(mask.shape, BF16), pltpu.VMEM(fold.shape, BF16),
            pltpu.VMEM((KF, 128, 128), BF16),
            dma((4,)),
            pltpu.VMEM((NY, 128, 1280), BF16),
            pltpu.VMEM((128, 1408), F32),
            pltpu.VMEM((2, 512, 1280), BF16),
            pltpu.VMEM((2, 256, 128), F32),
            pltpu.VMEM((32, 16, 128), F32),
            pltpu.VMEM((16, 80, 128), BF16),
            pltpu.VMEM((3, 16, 32, 128), BF16),
            pltpu.VMEM((2, NLB, NKEY), BF16),
            pltpu.VMEM((2, NLB, NKEY), BF16),
            pltpu.VMEM((NLB, 128), F32),
            pltpu.VMEM((NLB, 128), F32),
            pltpu.VMEM((2, 8, 16, 128), F32),
            pltpu.VMEM((16, KF, WIN), F32),
            pltpu.VMEM((KF, 640), F32),
            pltpu.VMEM((SLOTS, KF, WIN), F32),
            pltpu.VMEM((KF, EXT, 256), F32),
            pltpu.VMEM((EXT, 256), F32),
            pltpu.VMEM((2, 128, 128), BF16),
            pltpu.VMEM((2, 128, 128), BF16),
            pltpu.VMEM((96, 256), F32),
            pltpu.VMEM((2, 96, 256), BF16),
            pltpu.VMEM((2, 96, 256), BF16),
            pltpu.VMEM((8, 128), F32),
            pltpu.VMEM((2, 8, 128), F32),
            dma((6,)), dma((6,)),
            pltpu.VMEM((KF, 128, 128), F32),
            pltpu.VMEM((2, 128, 256), BF16),
            pltpu.VMEM((2, 24, 256), F32),
            pltpu.VMEM((18, 24, 256), F32),
            pltpu.VMEM((18, KF, 256), F32),
            pltpu.VMEM((2, 512, 128), BF16),
            pltpu.VMEM((2, EXT, 128), F32),
            pltpu.VMEM((128, SLOTS), F32),
            pltpu.VMEM((144, 512), F32),
            pltpu.VMEM((EXT, 768), F32),
            pltpu.VMEM((2, 8, 768), F32),
            pltpu.VMEM((2, 8, 768), F32),
            dma((2,)), dma((2,)),
            dma((np_, 4)), dma((np_, 4)),
            dma((np_, 4)), dma((np_, 4)),
            dma((np_, 9)), dma((np_, 9)),
            dma((3, 16)), dma((3, 16)),
            dma((40,)), dma((SLOTS,)),
        ],
        compiler_params=pltpu.CompilerParams(
            collective_id=0, has_side_effects=True, vmem_limit_bytes=60 * 1024 * 1024),
    )(lon_anchor, zone_width, spec, ridx, rwt, cidx, cwt, legendre,
      jnp.asarray(mask, BF16), jnp.asarray(fold, BF16), nest_state)


def hand_over(band_in, nest_in, band_out, nest_out, band_v, nest_v, sem):
    trips = [((band_in, band_v), (band_v, band_out))]
    for i in range(4):
        at = pl.ds(6 * i, 6)
        trips.append(((nest_in.at[at], nest_v.at[at]), (nest_v.at[at], nest_out.at[at])))
    trips = [tuple(pltpu.make_async_copy(*c, sem.at[way, i]) for way, c in enumerate(trip))
             for i, trip in enumerate(trips)]
    for get, _ in trips:
        get.start()
    for get, put in trips:
        get.wait()
        put.start()
    for _, put in trips:
        put.wait()


def results(band, nest):
    hbm = pl.BlockSpec(memory_space=pl.ANY)
    return pl.pallas_call(
        hand_over,
        out_shape=(jax.ShapeDtypeStruct(band.shape, F32), jax.ShapeDtypeStruct(nest.shape, BF16)),
        in_specs=[hbm, hbm], out_specs=(hbm, hbm),
        scratch_shapes=[pltpu.VMEM(band.shape, F32), pltpu.VMEM(nest.shape, BF16),
                        pltpu.SemaphoreType.DMA((2, 5))],
        compiler_params=pltpu.CompilerParams(vmem_limit_bytes=60 * 1024 * 1024),
    )(band, nest)


def body(
    spectra, legendre, lon_anchor, row_index, row_weight, col_index, col_weight, zone_width,
    nest_state,
):
    band, nest = spectral(
        spectra, legendre, lon_anchor, zone_width, nest_state,
        row_index.reshape(1, 128), row_weight.reshape(1, 128),
        col_index.reshape(1, 128), col_weight.reshape(1, 128),
    )
    return results(band, nest)


def solution(mesh):
    placed = (
        P("wave", "ny", None), P("wave", "ny", None), P(), P("ny"), P("ny"), P("wave"), P("wave"),
        P(), P(None, "ny", "wave"),
    )
    return jax.shard_map(
        body, mesh=mesh, in_specs=placed,
        out_specs=(P(None, "ny", "wave"), P(None, "ny", "wave")), check_vma=False,
    )
```

```python
import functools
import math

import jax
import jax.numpy as jnp
import numpy as np
from jax import lax
from jax.experimental import pallas as pl
from jax.experimental.pallas import tpu as pltpu
from jax.sharding import PartitionSpec as P

MESH = pl.DeviceIdType.MESH
NW = 16
NY = 16
PD = 40
TRUNC = 1280
NLON = 5120
LON = 32
KF = 24
NLB = 512
NSWEEP = 4
DIFFUSION = 0.2
F32 = jnp.float32
BF16 = jnp.bfloat16
CHUNKS = ((0, 8, 0, 32, 8), (8, 16, 32, 48, 0), (24, 16, 80, 48, 0))
HALVES = (((0, 16), (16, 16)), ((0, 48), (0, 0)), ((0, 0), (0, 48)))
KOFF = (0, 256, 768)
NKEY = 1280
SLOTS = 24
EXT = 144
WIN = 128


def lane_of(chan):
    return 16 * (chan % 8) + chan // 8


def first_consts():
    _, n, _, rows, lead = CHUNKS[0]
    row = np.arange(2 * n * 16)
    col = np.arange(16 * rows)
    inner = col % rows - lead
    cpair = np.where(inner >= 0, inner % n, -1)
    mask = ((row // 16) % n)[:, None] == cpair[None, :]
    fold = np.zeros((2, 16 * rows, 128), np.float32)
    for i in range(16 * rows):
        if inner[i] >= 0:
            lane = lane_of((i // rows) * 3 + inner[i] // n)
            fold[0, i, lane] = 1.0
            fold[1, i, lane + 8] = 1.0
    return mask.astype(np.float32), fold


def split2(x):
    hi = x.astype(BF16)
    lo = (x - hi.astype(F32)).astype(BF16)
    return hi, lo


def dot_nt(a, b):
    return lax.dot_general(a, b, (((1,), (1,)), ((), ())), preferred_element_type=F32)


def dot_nn(a, b):
    return lax.dot_general(a, b, (((1,), (0,)), ((), ())), preferred_element_type=F32)


def ramps(pos, first, last, total):
    return jnp.maximum(
        jnp.maximum(0.0, 1.0 - pos / first), jnp.maximum(0.0, 1.0 - (total - 1 - pos) / last)
    )


def shares(row, col, zone_ref):
    z = [zone_ref[i].astype(F32) for i in range(4)]
    share = jnp.maximum(ramps(row, z[0], z[1], 2048.0), ramps(col, z[2], z[3], 2048.0))
    inside = (row >= 0.0) & (row < 2048.0) & (col >= 0.0) & (col < 2048.0)
    inside = jnp.where(inside, 1.0, 0.0)
    return (1.0 - share) * inside, share * inside


def dot3(a, bh, bl):
    ah, al = split2(a)
    return dot_nn(ah, bh) + dot_nn(ah, bl) + dot_nn(al, bh)


def pick(axis_iota, index, weight):
    return jnp.where(axis_iota == index, 1.0 - weight, 0.0) + jnp.where(
        axis_iota == index + 1.0, weight, 0.0
    )


def fiota(shape, axis):
    return lax.broadcasted_iota(jnp.int32, shape, axis).astype(F32)


def k1(
    anchor_ref, zone_ref, spec_ref, ridx_ref, rwt_ref, cidx_ref, cwt_ref,
    leg_hbm, mask_hbm, fold_hbm, nest_hbm,
    band_out, nest_out,
    leg_ref, mask_ref, fold_ref, nest_ref, load_s,
    gath, sp32, leg2, legx, fs, fsend, frecv, tcos, tsin, acc_c, acc_s, turn, psend, pack_s, pack_r, prow, pbuf,
    ext, damp, cpk_s, cpk_r, rpk, rpk_s, rpk_r, info_s, info_r, nest_s, nest_r,
    field, row_mats, row_part, row_blend, row_x, col_mats, col_part, col_blend, lats, col_q,
    q_out, q_in, q_s, q_r,
    up_s, up_r, dn_s, dn_r, sib_s, sib_r, fa_s, fa_r, w_s, w_r,
):
    w = lax.axis_index("wave")
    y = lax.axis_index("ny")
    wedge = jnp.logical_or(w == 0, w == NW - 1)

    def near(d):
        return lax.rem(y + (NY + d), NY)

    def dev(ww, yy):
        return (ww, yy)

    up_y = lax.rem(y + 2, NY)
    dn_y = lax.rem(y + NY - 2, NY)
    sib_y = y + 1 - 2 * lax.rem(y, 2)

    loads = [pltpu.make_async_copy(a, b, load_s.at[i]) for i, (a, b) in enumerate((
        (nest_hbm, nest_ref), (leg_hbm, leg_ref), (mask_hbm, mask_ref), (fold_hbm, fold_ref)))]
    for c in loads:
        c.start()

    def zero(i, c):
        pbuf[i] = jnp.zeros((KF, WIN), F32)
        return c
    lax.fori_loop(0, SLOTS, zero, 0)
    cpk_r[...] = jnp.zeros((2, 128, 128), BF16)
    rpk_r[...] = jnp.zeros((2, 96, 256), BF16)
    info_r[...] = jnp.zeros((2, 8, 128), F32)
    q_in[...] = jnp.zeros((2, 8, 768), F32)

    barrier = pltpu.get_barrier_semaphore()

    def greet(ww, yy):
        pl.semaphore_signal(barrier, inc=1, device_id=dev(ww, yy), device_id_type=MESH)

    for yy in (up_y, dn_y, sib_y):
        greet(w, yy)

    def greet_wave(o, c):
        greet(lax.rem(w + o, NW), y)
        return c
    lax.fori_loop(1, NW, greet_wave, 0)

    @pl.when(y > 0)
    def _():
        greet(w, near(-1))

    @pl.when(y < NY - 1)
    def _():
        greet(w, near(1))

    @pl.when(jnp.logical_or(jnp.logical_and(wedge, y > 0), y == NY - 1))
    def _():
        greet(NW - 1, near(-1))

    @pl.when(jnp.logical_or(jnp.logical_and(wedge, y < NY - 1), y == 0))
    def _():
        greet(0, near(1))

    sp32[0:8, :] = jnp.zeros((8, 1408), F32)
    for c in range(3):
        v = spec_ref[c].astype(F32)
        last = jnp.broadcast_to(v[:, 1280:1281], (PD, 128))
        for p0, n, r0, rows, lead in CHUNKS:
            r = r0 + lead + c * n
            sp32[r : r + n, 0:1280] = v[p0 : p0 + n, 0:1280]
            sp32[r : r + n, 1280:1408] = last[p0 : p0 + n, :]
    tail = jnp.transpose(sp32[:, 1280:1408], (1, 0))[0:8, :]
    lane = lax.broadcasted_iota(jnp.int32, (8, 128), 1)
    sub = lax.broadcasted_iota(jnp.int32, (8, 896), 0)
    extra = jnp.zeros((8, 896), F32)
    for ch, (p0, n, r0, rows, lead) in enumerate(CHUNKS):
        part = jnp.where((lane >= r0 + lead) & (lane < r0 + rows), tail, 0.0)
        part = jnp.concatenate([part, jnp.zeros((8, 768), F32)], axis=1)
        part = pltpu.roll(part, lax.rem(y * rows - r0 + 896, 896), 1)
        part = jnp.broadcast_to(part[0:1, :], (8, 896))
        extra = jnp.where(sub == ch, part, extra)
    sp32[0:8, 0:768] = extra[:, 0:768]

    def cast_own(i, c):
        r = pl.multiple_of(i * 16, 16)
        gath[y, pl.ds(r, 16), :] = sp32[pl.ds(r, 16), 0:1280].astype(BF16)
        return c
    lax.fori_loop(0, 8, cast_own, 0)

    count = 15 + 3
    count += jnp.where(y < NY - 1, 1, 0) + jnp.where(y > 0, 1, 0)
    count += jnp.where(jnp.logical_and(w == NW - 1, y < NY - 1), 2, 0)
    count += jnp.where(jnp.logical_and(w == 0, y > 0), 2, 0)
    count += jnp.where(jnp.logical_and(w == 0, y == 1), 14, 0)
    count += jnp.where(jnp.logical_and(w == NW - 1, y == NY - 2), 14, 0)
    pl.semaphore_wait(barrier, count)

    def block(origin, piece, half):
        _, _, r0, rows, _ = CHUNKS[piece]
        if half is not None:
            first, count_ = HALVES[piece][half]
            r0, rows = r0 + first, count_
        return gath.at[origin, pl.ds(r0, rows), :]

    def ring(origin, piece, step, upward):
        ref = block(origin, piece, None if step < 3 else (0 if upward else 1))
        s, r = (up_s, up_r) if upward else (dn_s, dn_r)
        return pltpu.make_async_remote_copy(
            src_ref=ref, dst_ref=ref, send_sem=s.at[piece, step], recv_sem=r.at[piece, step],
            device_id=dev(w, up_y if upward else dn_y), device_id_type=MESH)

    def to_sib(origin, piece, idx, half=None):
        ref = block(origin, piece, half)
        return pltpu.make_async_remote_copy(
            src_ref=ref, dst_ref=ref, send_sem=sib_s.at[piece, idx], recv_sem=sib_r.at[piece, idx],
            device_id=dev(w, sib_y), device_id_type=MESH)

    def origin_of(base, step, upward):
        return lax.rem(base + NY - 2 * step, NY) if upward else lax.rem(base + 2 * step, NY)

    def far(piece, upward):
        return HALVES[piece][0 if upward else 1][1] > 0

    def send_own(piece):
        ring(y, piece, 0, True).start()
        ring(y, piece, 0, False).start()
        to_sib(y, piece, 0).start()

    def ring_step(piece, step):
        for upward in (True, False):
            org = origin_of(y, step, upward)
            if step < 4:
                ring(org, piece, step - 1, upward).wait_recv()
                if step < 3 or far(piece, upward):
                    ring(org, piece, step, upward).start()
                to_sib(org, piece, 2 * step - (1 if upward else 0)).start()
            elif far(piece, upward):
                ring(org, piece, 3, upward).wait_recv()
                to_sib(org, piece, 7 if upward else 8, 0 if upward else 1).start()

    def sib_each(base, piece, go):
        go(to_sib(base, piece, 0))
        for step in range(1, 5):
            for upward in (True, False):
                org = origin_of(base, step, upward)
                if step < 4:
                    go(to_sib(org, piece, 2 * step - (1 if upward else 0)))
                elif far(piece, upward):
                    go(to_sib(org, piece, 7 if upward else 8, 0 if upward else 1))

    def sib_wait(piece):
        sib_each(sib_y, piece, lambda c: c.wait_recv())

    def sends_done(piece):
        for step in range(4):
            for upward in (True, False):
                if step < 3 or far(piece, upward):
                    ring(y, piece, step, upward).wait_send()
        sib_each(y, piece, lambda c: c.wait_send())

    anchor = anchor_ref[0].astype(F32)

    def leg_rows(ch):
        p0, n, _, _, _ = CHUNKS[ch]
        pos = lax.broadcasted_iota(jnp.int32, (1, 1280), 1)

        def one(p, c):
            limit = TRUNC - (w * PD + p0 + p)
            low = jnp.where(pos < limit, 1.0, 0.0)
            rows = leg_ref[p0 + p]
            tile = rows[:, 0:1280]
            a = pl.multiple_of(p * 16, 16)
            b = pl.multiple_of(n * 16 + p * 16, 16)
            leg2[ch % 2, pl.ds(a, 16), :] = tile * low.astype(BF16)
            leg2[ch % 2, pl.ds(b, 16), :] = tile * (1.0 - low).astype(BF16)
            last = rows[:, 1280:1281].astype(F32)
            legx[ch % 2, pl.ds(a, 16), :] = jnp.broadcast_to(last, (16, 128))
            return c
        lax.fori_loop(0, n, one, 0)

    def last_row(ch, width):
        v = gath[0, 0:16, 0:width].astype(F32)
        for i in range(1, NY):
            v = v + gath[i, 0:16, 0:width].astype(F32)
        return v[ch : ch + 1, :]

    def fourier(ch):
        p0, n, r0, rows, lead = CHUNKS[ch]
        width = 16 * rows
        g = gath[:, r0 : r0 + rows, :].reshape(width, 1280)
        x = last_row(ch, width)
        lane16 = lax.broadcasted_iota(jnp.int32, (16, 128), 1) % 16
        if ch == 0:
            res = dot_nt(leg2[0, 0:256, :], g)
            rank1 = jnp.concatenate([jnp.zeros((128, width), F32),
                                     jnp.tile(legx[0, 0:128, :], (1, width // 128)) * x], 0)
            hi, lo = split2((res + rank1) * mask_ref[...].astype(F32))
            fs[0:16] = (dot_nn(hi, fold_ref[0]) + dot_nn(lo, fold_ref[1])).reshape(16, 16, 128)
        else:
            for h in range(2):
                res = dot_nt(leg2[ch % 2, 256 * h : 256 * h + 256, :], g)
                for p in range(n):
                    v = jnp.zeros((16, 128), F32)
                    for j in range(width // 128):
                        q = res[16 * p : 16 * p + 16, 128 * j : 128 * j + 128]
                        if h == 1:
                            q = q + legx[ch % 2, 16 * p : 16 * p + 16, :] * x[:, 128 * j : 128 * j + 128]
                        q = jnp.where(lane16 == p, q, 0.0)
                        v = v + (pltpu.roll(q, (j - p) % 128, 1) if j != p else q)
                    hi = v.astype(BF16).astype(F32)
                    lo = (v - hi).astype(BF16).astype(F32)
                    fs[16 * h + p] = hi + pltpu.roll(lo, 8, 1)
        f0 = (0, 16, 48)[ch]
        for l in range(16):
            fsend[l, f0 : f0 + 2 * n, :] = fs[0 : 2 * n, l, :].astype(BF16)

    def wave_copy(ch, o):
        n = CHUNKS[ch][1]
        f0 = (0, 16, 48)[ch]
        to = lax.rem(w + o, NW)
        return pltpu.make_async_remote_copy(
            src_ref=fsend.at[to, pl.ds(f0, 2 * n), :], dst_ref=frecv.at[ch, w, pl.ds(0, 2 * n), :],
            send_sem=fa_s.at[ch, o], recv_sem=fa_r.at[ch, o],
            device_id=dev(to, y), device_id_type=MESH)

    def wave_send(ch):
        n = CHUNKS[ch][1]
        f0 = (0, 16, 48)[ch]
        lax.fori_loop(1, NW, lambda o, c: (wave_copy(ch, o).start(), c)[1], 0)
        frecv[ch, w, 0 : 2 * n, :] = fsend[w, f0 : f0 + 2 * n, :]

    def wave_recv(ch):
        lax.fori_loop(1, NW, lambda o, c: (wave_copy(ch, o).wait_recv(), c)[1], 0)

    def wave_done(ch):
        lax.fori_loop(1, NW, lambda o, c: (wave_copy(ch, o).wait_send(), c)[1], 0)

    def table(ch):
        p0, n, _, _, _ = CHUNKS[ch]
        k0 = KOFF[ch]
        shift = 4 if n == 16 else 3

        def one(t, c):
            q = t * 128 + lax.broadcasted_iota(jnp.int32, (1, 128), 1)
            ww = q >> (shift + 1)
            h = (q >> shift) & 1
            pg = ww * PD + p0 + (q & (n - 1))
            mi = jnp.where(h == 0, pg, TRUNC - 1 - pg)
            m = mi.astype(F32)
            s = jnp.where(mi == 0, 1.0, 2.0)

            def angle(x):
                return (x - NLON * jnp.floor(x * (1.0 / NLON))) * (2.0 * math.pi / NLON)

            d = lax.broadcasted_iota(jnp.int32, (LON, 128), 0).astype(F32)
            fine = angle(m * d)
            cf, sf = jnp.cos(fine) * s, jnp.sin(fine) * s
            b = lax.broadcasted_iota(jnp.int32, (16, 128), 0).astype(F32) * LON
            coarse = angle(m * (anchor + b))
            cc, sc = jnp.cos(coarse), jnp.sin(coarse)
            col = pl.multiple_of(k0 + t * 128, 128)
            for i in range(16):
                ci, si = cc[i : i + 1, :], sc[i : i + 1, :]
                vc = ci * cf - si * sf
                vs = -(si * cf + ci * sf)
                hi, lo = split2(vc)
                tcos[0, LON * i : LON * i + LON, pl.ds(col, 128)] = hi
                tcos[1, LON * i : LON * i + LON, pl.ds(col, 128)] = lo
                hi, lo = split2(vs)
                tsin[0, LON * i : LON * i + LON, pl.ds(col, 128)] = hi
                tsin[1, LON * i : LON * i + LON, pl.ds(col, 128)] = lo
            return c
        lax.fori_loop(0, 2 * n * 16 // 128, one, 0)

    def contract(ch):
        n = CHUNKS[ch][1]
        k0, k = KOFF[ch], 2 * n * 16
        f = frecv[ch, :, 0 : 2 * n, :].reshape(k, 128)

        for tab, acc in ((tcos, acc_c), (tsin, acc_s)):
            v = dot_nn(tab[0, :, k0 : k0 + k], f) + dot_nn(tab[1, :, k0 : k0 + k], f)
            if ch == 0:
                acc[...] = v
            else:
                acc[...] = acc[...] + v

    lane_h = lax.broadcasted_iota(jnp.int32, (128, 128), 1)

    def nest_copy(i):
        if i < 4:
            src, dst = (cpk_s, cpk_r) if i < 2 else (rpk_s, rpk_r)
            src, dst = src.at[i % 2], dst.at[i % 2]
        else:
            src, dst = info_s, info_r.at[i - 4]
        to = (dev(lax.rem(w + NW - 1, NW), y), dev(lax.rem(w + 1, NW), y), dev(w, near(-1)), dev(w, near(1)))[i % 4]
        return pltpu.make_async_remote_copy(
            src_ref=src, dst_ref=dst, send_sem=nest_s.at[i], recv_sem=nest_r.at[i],
            device_id=to, device_id_type=MESH)

    can_send = (w > 0, w < NW - 1, y > 0, y < NY - 1)
    can_recv = (w < NW - 1, w > 0, y < NY - 1, y > 0)

    def nest_do(which, cond, go):
        for i in which:
            @pl.when(cond[i % 4])
            def _(i=i):
                go(nest_copy(i))

    def nest_pack():
        info_s[...] = jnp.zeros((8, 128), F32)
        info_s[0:1, :] = ridx_ref[...].astype(F32)
        info_s[1:2, :] = rwt_ref[...]
        loads[0].wait()
        info_s[2:3, :] = cidx_ref[...].astype(F32)
        info_s[3:4, :] = cwt_ref[...]
        left = jnp.zeros((128, 128), F32)
        right = jnp.zeros((128, 128), F32)
        for k in range(KF):
            v = nest_ref[k].astype(F32)
            here = (lane_h >= 4 * k) & (lane_h < 4 * k + 4)
            left = jnp.where(here, pltpu.roll(v, 4 * k, 1) if k else v, left)
            right = jnp.where(here, pltpu.roll(v, 4 * k + 4, 1), right)
        cpk_s[0] = left.astype(BF16)
        cpk_s[1] = right.astype(BF16)
        row = (lax.broadcasted_iota(jnp.int32, (EXT, 256), 0) + (128 * y - 8)).astype(F32)
        j = lax.broadcasted_iota(jnp.int32, (EXT, 256), 1)
        col = (jnp.where(j < 192, j, j - 256) + 128 * w).astype(F32)
        keep, _ = shares(row, col, zone_ref)
        damp[...] = keep * DIFFUSION
        nest_do((0, 1, 4, 5), can_send, lambda c: c.start())

    def nest_cols():
        nest_do((0, 1), can_recv, lambda c: c.wait_recv())
        from_right = cpk_r[0].astype(F32)
        from_left = cpk_r[1].astype(F32)

        def one(k, c):
            a = pltpu.roll(from_right, lax.rem(128 - 4 * k, 128), 1)
            b = pltpu.roll(from_left, lax.rem(252 - 4 * k, 128), 1)
            e = jnp.where(lane_h < 4, a, jnp.where(lane_h >= 124, b, 0.0))
            ext[k, 0:8, :] = jnp.zeros((8, 256), F32)
            ext[k, 136:144, :] = jnp.zeros((8, 256), F32)
            ext[k, 8:136, 0:128] = nest_ref[k].astype(F32)
            ext[k, 8:136, 128:256] = e
            return c
        lax.fori_loop(0, KF, one, 0)
        for i, r in ((0, 8), (1, 132)):
            for k in range(KF):
                rpk[4 * k : 4 * k + 4, :] = ext[k, r : r + 4, :]
            rpk_s[i] = rpk[...].astype(BF16)
        nest_do((2, 3), can_send, lambda c: c.start())

    def nest_rows():
        nest_do((2, 3), can_recv, lambda c: c.wait_recv())
        for i, r in ((0, 136), (1, 4)):
            rpk[...] = rpk_r[i].astype(F32)
            for k in range(KF):
                ext[k, r : r + 4, :] = rpk[4 * k : 4 * k + 4, :]

    def nest_sweeps(k0, k1_):
        def one(k, c):
            x = ext[k]
            for _ in range(NSWEEP):
                t = x + pltpu.roll(x, 1, 0) + pltpu.roll(x, EXT - 1, 0)
                t = t + pltpu.roll(x, 1, 1) + pltpu.roll(x, 255, 1)
                x = t * damp[...]
            field[k] = x[8:136, 0:128]
            nest_out[k] = x[8:136, 0:128].astype(BF16)
            return c
        lax.fori_loop(k0, k1_, one, 0)

    def nest_done():
        nest_do((4, 5), can_recv, lambda c: c.wait_recv())
        nest_do(range(6), can_send, lambda c: c.wait_send())

    row_edge = jnp.logical_or(y == 0, y == NY - 1)
    first = jnp.where(y == 0, 0, 104)
    cbase = jnp.where(w == 0, 0, 96)

    def strip_prep():
        lon0 = (w * LON - 48).astype(F32)
        lat0 = (y * 16 - 1).astype(F32)
        own, right, left = info_s[...], info_r[0], info_r[1]
        lane = lax.broadcasted_iota(jnp.int32, (1, 128), 1)
        turned = jnp.transpose(jnp.concatenate([own, jnp.zeros((120, 128), F32)], 0), (1, 0))

        @pl.when(row_edge)
        def _():
            far_i = jnp.where(lane < 4, right[2:3], jnp.where(lane >= 124, left[2:3], -4096.0))
            far_w = jnp.where(lane < 4, right[3:4], left[3:4])
            cidx = jnp.concatenate([own[2:3], far_i], 1) - lon0
            cwt = jnp.concatenate([own[3:4], far_w], 1)
            hi, lo = split2(pick(fiota((128, 256), 0), cidx, cwt))
            row_mats[0] = hi
            row_mats[1] = lo
            cols = jnp.where(y == 0, turned[0:24, :], turned[104:128, :])
            ridx = cols[:, 0:1] - lat0
            rwt = cols[:, 1:2]
            row = fiota((24, 256), 0) + (128 * y + first).astype(F32)
            j = lax.broadcasted_iota(jnp.int32, (24, 256), 1)
            col = (jnp.where(j < 192, j, j - 256) + 128 * w).astype(F32)
            keep, share = shares(row, col, zone_ref)
            row_part[0] = jnp.where((row < 20.0) | (row >= 2028.0), keep * DIFFUSION, 0.0)
            row_part[1] = jnp.where((row < 16.0) | (row >= 2032.0), share, 0.0)
            row_blend[...] = pick(fiota((24, SLOTS), 1), ridx, rwt)

        @pl.when(wedge)
        def _():
            vec = jnp.concatenate([own[2:4] - jnp.where(fiota((2, 128), 0) == 0.0, lon0, 0.0),
                                   jnp.zeros((6, 128), F32)], 0)
            vec = jnp.where(w == 0, vec, pltpu.roll(vec, 32, 1))
            for i in range(4):
                v = pltpu.roll(vec, LON * i, 1) if i else vec
                here = (lane >= LON * i) & (lane < LON * i + LON)
                m = jnp.where(here, pick(fiota((128, 128), 0), v[0:1], v[1:2]), 0.0)
                hi, lo = split2(m)
                col_mats[0, 128 * i : 128 * i + 128, :] = hi
                col_mats[1, 128 * i : 128 * i + 128, :] = lo
            col_blend[...] = pick(fiota((128, SLOTS), 1), turned[:, 0:1] - lat0, turned[:, 1:2])
            row = fiota((EXT, 128), 0) + (128 * y - 8).astype(F32)
            inner = lax.broadcasted_iota(jnp.int32, (EXT, 128), 1) % LON
            col = (inner + cbase + 128 * w).astype(F32)
            keep, share = shares(row, col, zone_ref)
            share = jnp.where((col < 16.0) | (col >= 2032.0), share, 0.0)
            col_part[0] = keep * DIFFUSION
            col_part[1] = jnp.where((row >= 16.0) & (row < 2032.0), share, 0.0)

    def q_copy(i):
        return pltpu.make_async_remote_copy(
            src_ref=q_out.at[i], dst_ref=q_in.at[i], send_sem=q_s.at[i], recv_sem=q_r.at[i],
            device_id=dev(w, near(1 if i else -1)), device_id_type=MESH)

    def q_each(cond, go):
        for i in range(2):
            @pl.when(jnp.logical_and(wedge, cond[i]))
            def _(i=i):
                go(q_copy(i))

    q_send = (y > 0, y < NY - 1)
    q_recv = (y < NY - 1, y > 0)

    def gather_rows():
        for k in range(KF):
            lats[:, 128 * k : 128 * k + 128] = pbuf[:, k, :]

    def col_source():
        @pl.when(wedge)
        def _():
            v = jnp.concatenate([lats[:, 512 * t : 512 * t + 512] for t in range(KF // 4)], 0)
            v = dot3(v, col_mats[0], col_mats[1])
            v = jnp.concatenate([v[24 * t : 24 * t + 24, :] for t in range(KF // 4)], 1)
            hi, lo = split2(v)
            v = dot3(col_blend[...], hi, lo)
            share = col_part[1, 8:136, :]
            col_q[0:8, :] = jnp.zeros((8, 768), F32)
            col_q[136:144, :] = jnp.zeros((8, 768), F32)
            for t in range(KF // 4):
                col_q[8:136, 128 * t : 128 * t + 128] = v[:, 128 * t : 128 * t + 128] * share
            q_out[0] = col_q[8:16, :]
            q_out[1] = col_q[128:136, :]

        q_each(q_send, lambda c: c.start())

    def row_strip():
        @pl.when(row_edge)
        def _():
            hi, lo = split2(lats[...])
            v = dot3(row_blend[...], hi, lo)
            v = jnp.concatenate([v[:, 128 * k : 128 * k + 128] for k in range(KF)], 0)
            row_x[...] = dot3(v, row_mats[0], row_mats[1])
            at = pl.ds(pl.multiple_of(first, 8), 24)

            def some(n, c):
                ks = [n * 6 + i for i in range(6)]
                qs = [row_x[pl.ds(pl.multiple_of(k * 24, 8), 24), :] * row_part[1] for k in ks]
                gs = list(qs)
                for _ in range(NSWEEP - 1):
                    vs = [g + pltpu.roll(g, 1, 0) + pltpu.roll(g, 23, 0)
                          + pltpu.roll(g, 1, 1) + pltpu.roll(g, 255, 1) for g in gs]
                    gs = [v * row_part[0] + q for v, q in zip(vs, qs)]
                for k, g in zip(ks, gs):
                    field[k, at, :] = field[k, at, :] + g[:, 0:128]
                return c
            lax.fori_loop(0, KF // 6, some, 0)

        @pl.when(jnp.logical_and(row_edge, jnp.logical_not(wedge)))
        def _():
            at = pl.ds(pl.multiple_of(jnp.where(y == 0, 0, 96), 32), 32)

            def last(k, c):
                nest_out[k, at, :] = field[k, at, :].astype(BF16)
                return c
            lax.fori_loop(0, KF, last, 0)

    def side_masks(rows):
        inner = lax.broadcasted_iota(jnp.int32, (rows, 128), 1) % LON
        return inner != 0, inner != LON - 1

    def side_sweeps(qs, keep, rows):
        not_first, not_last = side_masks(rows)
        gs = list(qs)
        for _ in range(NSWEEP - 1):
            vs = [g + pltpu.roll(g, 1, 0) + pltpu.roll(g, rows - 1, 0)
                  + jnp.where(not_first, pltpu.roll(g, 1, 1), 0.0)
                  + jnp.where(not_last, pltpu.roll(g, 127, 1), 0.0) for g in gs]
            gs = [v * keep + q for v, q in zip(vs, qs)]
        return gs

    def col_strip():
        @pl.when(wedge)
        def _():
            def some(n, c):
                at = [pl.ds(pl.multiple_of((n * 2 + i) * 128, 128), 128) for i in range(2)]
                gs = side_sweeps([col_q[:, a] for a in at], col_part[0], EXT)
                for a, g in zip(at, gs):
                    col_q[:, a] = g
                return c
            lax.fori_loop(0, KF // 8, some, 0)

        q_each(q_recv, lambda c: c.wait_recv())

        @pl.when(wedge)
        def _():
            sub = lax.broadcasted_iota(jnp.int32, (8, 768), 0)
            blank = jnp.zeros((8, 768), F32)
            above = jnp.concatenate([jnp.where(sub >= 4, q_in[1], 0.0), blank], 0)
            below = jnp.concatenate([blank, jnp.where(sub < 4, q_in[0], 0.0)], 0)
            tiles = range(KF // 4)
            ga = side_sweeps([above[:, 128 * t : 128 * t + 128] for t in tiles], col_part[0, 0:16, :], 16)
            gb = side_sweeps([below[:, 128 * t : 128 * t + 128] for t in tiles], col_part[0, 128:144, :], 16)
            for t in tiles:
                a = slice(128 * t, 128 * t + 128)
                col_q[8:16, a] = col_q[8:16, a] + ga[t][8:16]
                col_q[128:136, a] = col_q[128:136, a] + gb[t][0:8]
            lane_h = lax.broadcasted_iota(jnp.int32, (128, 128), 1)
            strip = (lane_h >= cbase) & (lane_h < cbase + LON)

            def add(n, c):
                for t in (n * 2, n * 2 + 1):
                    g = col_q[8:136, pl.ds(pl.multiple_of(t * 128, 128), 128)]
                    for i in range(4):
                        part = pltpu.roll(g, lax.rem(cbase + 128 - LON * i, 128), 1)
                        k = 4 * t + i
                        nest_out[k] = (field[k] + jnp.where(strip, part, 0.0)).astype(BF16)
                return c
            lax.fori_loop(0, KF // 8, add, 0)

    send_own(0)
    send_own(1)
    nest_pack()
    ring_step(0, 1)
    send_own(2)
    table(0)
    table(1)
    loads[1].wait()
    leg_rows(0)
    nest_cols()
    ring_step(0, 2)
    ring_step(1, 1)
    table(2)
    nest_rows()
    leg_rows(1)
    ring_step(0, 3)
    ring_step(2, 1)
    nest_sweeps(0, 8)
    ring_step(1, 2)
    ring_step(0, 4)
    sib_wait(0)
    loads[2].wait()
    loads[3].wait()
    fourier(0)
    wave_send(0)
    ring_step(2, 2)
    nest_sweeps(8, 16)
    ring_step(1, 3)
    wave_recv(0)
    contract(0)
    ring_step(2, 3)
    nest_sweeps(16, KF)
    nest_done()
    strip_prep()
    ring_step(1, 4)
    leg_rows(2)
    ring_step(2, 4)
    sib_wait(1)
    fourier(1)
    wave_send(1)
    sib_wait(2)
    fourier(2)
    wave_send(2)
    wave_recv(1)
    contract(1)
    wave_recv(2)
    contract(2)

    prow[:, 0:128] = jnp.zeros((KF, 128), F32)
    prow[:, 512:640] = jnp.zeros((KF, 128), F32)
    for i in range(4):
        turn[0] = jnp.transpose(acc_c[128 * i : 128 * i + 128, :], (1, 0)).reshape(8, 16, 128)
        turn[1] = jnp.transpose(acc_s[128 * i : 128 * i + 128, :], (1, 0)).reshape(8, 16, 128)
        val = [turn[0, :, j, :] + turn[0, :, j + 8, :] + turn[1, :, j + 3, :] + turn[1, :, j + 11, :]
               for j in range(3)]
        prow[:, 48 + 128 * i : 176 + 128 * i] = jnp.concatenate(val, 0)
    lane = lax.broadcasted_iota(jnp.int32, (8, 128), 1)
    for v in range(NW):
        window = prow[:, LON * v : LON * v + WIN]
        psend[v] = window
        packed = jnp.zeros((8, 128), F32)
        for j in range(3):
            part = pltpu.roll(window[8 * j : 8 * j + 8], (LON * j + 80) % 128, 1)
            packed = jnp.where((lane >= LON * j) & (lane < LON * j + LON), part, packed)
        pack_s[v] = packed

    def win(src, to_w, to_y, slot, sem):
        return pltpu.make_async_remote_copy(
            src_ref=psend.at[src], dst_ref=pbuf.at[slot], send_sem=w_s.at[sem], recv_sem=w_r.at[slot],
            device_id=dev(to_w, to_y), device_id_type=MESH)

    def edges(go):
        @pl.when(jnp.logical_and(w == 0, y > 0))
        def _():
            go(0, 0, near(-1), 17, 16)
            go(NW - 1, NW - 1, near(-1), 17, 17)

        @pl.when(jnp.logical_and(w == NW - 1, y < NY - 1))
        def _():
            go(0, 0, near(1), 0, 18)
            go(NW - 1, NW - 1, near(1), 0, 19)

        @pl.when(jnp.logical_and(w == 0, y == 1))
        def _():
            lax.fori_loop(1, NW - 1, lambda v, c: (go(v, v, near(-1), 17, 20 + v), c)[1], 0)

        @pl.when(jnp.logical_and(w == NW - 1, y == NY - 2))
        def _():
            lax.fori_loop(1, NW - 1, lambda v, c: (go(v, v, near(1), 0, 20 + v), c)[1], 0)

    def own_win(o):
        to = lax.rem(w + o, NW)
        return win(to, to, y, 1 + w, o)

    def own_pack(o):
        to = lax.rem(w + o, NW)
        return pltpu.make_async_remote_copy(
            src_ref=pack_s.at[to], dst_ref=pack_r.at[w], send_sem=w_s.at[o], recv_sem=w_r.at[1 + w],
            device_id=dev(to, y), device_id_type=MESH)

    def own_each(go):
        def one(o, c):
            to = lax.rem(w + o, NW)
            whole = jnp.logical_or(row_edge, jnp.logical_or(to == 0, to == NW - 1))

            @pl.when(whole)
            def _():
                go(own_win(o))

            @pl.when(jnp.logical_not(whole))
            def _():
                go(own_pack(o))
            return c
        lax.fori_loop(1, NW, one, 0)

    own_each(lambda c: c.start())
    edges(lambda *a: win(*a).start())
    pbuf[1 + w] = psend[w]
    pack_r[w] = pack_s[w]

    for ch in range(3):
        wave_done(ch)
    for piece in range(len(CHUNKS)):
        sends_done(piece)

    def got(slot):
        win(0, w, sib_y, slot, 0).wait_recv()

    here_whole = jnp.logical_or(row_edge, wedge)

    @pl.when(here_whole)
    def _():
        lax.fori_loop(1, NW, lambda o, c: (got(1 + lax.rem(w + o, NW)), c)[1], 0)

    @pl.when(jnp.logical_not(here_whole))
    def _():
        def one(o, c):
            src = lax.rem(w + o, NW)
            pltpu.make_async_remote_copy(
                src_ref=pack_s.at[0], dst_ref=pack_r.at[src], send_sem=w_s.at[0],
                recv_sem=w_r.at[1 + src], device_id=dev(w, sib_y), device_id_type=MESH).wait_recv()
            return c
        lax.fori_loop(1, NW, one, 0)

    @pl.when(jnp.logical_or(jnp.logical_and(wedge, y > 0), y == NY - 1))
    def _():
        got(0)

    @pl.when(jnp.logical_or(jnp.logical_and(wedge, y < NY - 1), y == 0))
    def _():
        got(17)

    @pl.when(here_whole)
    def _():
        gather_rows()

    col_source()
    row_strip()
    col_strip()

    @pl.when(here_whole)
    def _():
        for k in range(KF):
            band_out[k] = pltpu.roll(pbuf[1:17, k, :], 80, 1)[:, 0:LON]

    @pl.when(jnp.logical_not(here_whole))
    def _():
        for i in range(8):
            v = pack_r[:, i, :]
            for j in range(3):
                band_out[8 * j + i] = (pltpu.roll(v, 128 - LON * j, 1) if j else v)[:, 0:LON]

    q_each(q_send, lambda c: c.wait_send())
    own_each(lambda c: c.wait_send())
    edges(lambda *a: win(*a).wait_send())


def vmem_spec():
    return pl.BlockSpec(memory_space=pltpu.VMEM)


def spectral(spectra, legendre, lon_anchor, zone_width, nest_state, ridx, rwt, cidx, cwt):
    spec = jnp.transpose(spectra, (1, 0, 2))
    mask, fold = first_consts()
    np_ = len(CHUNKS)
    smem = pl.BlockSpec(memory_space=pltpu.SMEM)
    dma = pltpu.SemaphoreType.DMA
    return pl.pallas_call(
        k1,
        out_shape=(
            jax.ShapeDtypeStruct((KF, 16, LON), F32),
            jax.ShapeDtypeStruct((KF, 128, 128), BF16),
        ),
        in_specs=[smem, smem] + [vmem_spec()] * 5 + [pl.BlockSpec(memory_space=pl.ANY)] * 4,
        out_specs=(vmem_spec(), vmem_spec()),
        scratch_shapes=[
            pltpu.VMEM((PD, 16, 1281), BF16),
            pltpu.VMEM(mask.shape, BF16), pltpu.VMEM(fold.shape, BF16),
            pltpu.VMEM((KF, 128, 128), BF16),
            dma((4,)),
            pltpu.VMEM((NY, 128, 1280), BF16),
            pltpu.VMEM((128, 1408), F32),
            pltpu.VMEM((2, 512, 1280), BF16),
            pltpu.VMEM((2, 256, 128), F32),
            pltpu.VMEM((32, 16, 128), F32),
            pltpu.VMEM((16, 80, 128), BF16),
            pltpu.VMEM((3, 16, 32, 128), BF16),
            pltpu.VMEM((2, NLB, NKEY), BF16),
            pltpu.VMEM((2, NLB, NKEY), BF16),
            pltpu.VMEM((NLB, 128), F32),
            pltpu.VMEM((NLB, 128), F32),
            pltpu.VMEM((2, 8, 16, 128), F32),
            pltpu.VMEM((16, KF, WIN), F32),
            pltpu.VMEM((16, 8, 128), F32),
            pltpu.VMEM((16, 8, 128), F32),
            pltpu.VMEM((KF, 640), F32),
            pltpu.VMEM((SLOTS, KF, WIN), F32),
            pltpu.VMEM((KF, EXT, 256), F32),
            pltpu.VMEM((EXT, 256), F32),
            pltpu.VMEM((2, 128, 128), BF16),
            pltpu.VMEM((2, 128, 128), BF16),
            pltpu.VMEM((96, 256), F32),
            pltpu.VMEM((2, 96, 256), BF16),
            pltpu.VMEM((2, 96, 256), BF16),
            pltpu.VMEM((8, 128), F32),
            pltpu.VMEM((2, 8, 128), F32),
            dma((6,)), dma((6,)),
            pltpu.VMEM((KF, 128, 128), F32),
            pltpu.VMEM((2, 128, 256), BF16),
            pltpu.VMEM((2, 24, 256), F32),
            pltpu.VMEM((24, SLOTS), F32),
            pltpu.VMEM((24 * KF, 256), F32),
            pltpu.VMEM((2, 512, 128), BF16),
            pltpu.VMEM((2, EXT, 128), F32),
            pltpu.VMEM((128, SLOTS), F32),
            pltpu.VMEM((SLOTS, 128 * KF), F32),
            pltpu.VMEM((EXT, 768), F32),
            pltpu.VMEM((2, 8, 768), F32),
            pltpu.VMEM((2, 8, 768), F32),
            dma((2,)), dma((2,)),
            dma((np_, 4)), dma((np_, 4)),
            dma((np_, 4)), dma((np_, 4)),
            dma((np_, 9)), dma((np_, 9)),
            dma((3, 16)), dma((3, 16)),
            dma((40,)), dma((SLOTS,)),
        ],
        compiler_params=pltpu.CompilerParams(
            collective_id=0, has_side_effects=True, vmem_limit_bytes=60 * 1024 * 1024),
    )(lon_anchor, zone_width, spec, ridx, rwt, cidx, cwt, legendre,
      jnp.asarray(mask, BF16), jnp.asarray(fold, BF16), nest_state)


def hand_over(band_in, nest_in, band_out, nest_out, band_v, nest_v, sem):
    trips = [((band_in, band_v), (band_v, band_out))]
    for i in range(4):
        at = pl.ds(6 * i, 6)
        trips.append(((nest_in.at[at], nest_v.at[at]), (nest_v.at[at], nest_out.at[at])))
    trips = [tuple(pltpu.make_async_copy(*c, sem.at[way, i]) for way, c in enumerate(trip))
             for i, trip in enumerate(trips)]
    for get, _ in trips:
        get.start()
    for get, put in trips:
        get.wait()
        put.start()
    for _, put in trips:
        put.wait()


def results(band, nest):
    hbm = pl.BlockSpec(memory_space=pl.ANY)
    return pl.pallas_call(
        hand_over,
        out_shape=(jax.ShapeDtypeStruct(band.shape, F32), jax.ShapeDtypeStruct(nest.shape, BF16)),
        in_specs=[hbm, hbm], out_specs=(hbm, hbm),
        scratch_shapes=[pltpu.VMEM(band.shape, F32), pltpu.VMEM(nest.shape, BF16),
                        pltpu.SemaphoreType.DMA((2, 5))],
        compiler_params=pltpu.CompilerParams(vmem_limit_bytes=60 * 1024 * 1024),
    )(band, nest)


def body(
    spectra, legendre, lon_anchor, row_index, row_weight, col_index, col_weight, zone_width,
    nest_state,
):
    band, nest = spectral(
        spectra, legendre, lon_anchor, zone_width, nest_state,
        row_index.reshape(1, 128), row_weight.reshape(1, 128),
        col_index.reshape(1, 128), col_weight.reshape(1, 128),
    )
    return results(band, nest)


def solution(mesh):
    placed = (
        P("wave", "ny", None), P("wave", "ny", None), P(), P("ny"), P("ny"), P("wave"), P("wave"),
        P(), P(None, "ny", "wave"),
    )
    return jax.shard_map(
        body, mesh=mesh, in_specs=placed,
        out_specs=(P(None, "ny", "wave"), P(None, "ny", "wave")), check_vma=False,
    )
```

```python
import functools
import math

import jax
import jax.numpy as jnp
import numpy as np
from jax import lax
from jax.experimental import pallas as pl
from jax.experimental.pallas import tpu as pltpu
from jax.sharding import PartitionSpec as P

MESH = pl.DeviceIdType.MESH
NW = 16
NY = 16
PD = 40
TRUNC = 1280
NLON = 5120
LON = 32
KF = 24
NLB = 512
NSWEEP = 4
DIFFUSION = 0.2
F32 = jnp.float32
BF16 = jnp.bfloat16
CHUNKS = ((0, 8, 0, 32, 8), (8, 16, 32, 48, 0), (24, 16, 80, 48, 0))
HALVES = (((0, 16), (16, 16)), ((0, 48), (0, 0)), ((0, 0), (0, 48)))
KOFF = (0, 256, 768)
NKEY = 1280
SLOTS = 24
EXT = 144
WIN = 128


def lane_of(chan):
    return 16 * (chan % 8) + chan // 8


def first_consts():
    _, n, _, rows, lead = CHUNKS[0]
    row = np.arange(2 * n * 16)
    col = np.arange(16 * rows)
    inner = col % rows - lead
    cpair = np.where(inner >= 0, inner % n, -1)
    mask = ((row // 16) % n)[:, None] == cpair[None, :]
    fold = np.zeros((2, 16 * rows, 128), np.float32)
    for i in range(16 * rows):
        if inner[i] >= 0:
            lane = lane_of((i // rows) * 3 + inner[i] // n)
            fold[0, i, lane] = 1.0
            fold[1, i, lane + 8] = 1.0
    return mask.astype(np.float32), fold


def split2(x):
    hi = x.astype(BF16)
    lo = (x - hi.astype(F32)).astype(BF16)
    return hi, lo


def dot_nt(a, b):
    return lax.dot_general(a, b, (((1,), (1,)), ((), ())), preferred_element_type=F32)


def dot_nn(a, b):
    return lax.dot_general(a, b, (((1,), (0,)), ((), ())), preferred_element_type=F32)


def ramps(pos, first, last, total):
    return jnp.maximum(
        jnp.maximum(0.0, 1.0 - pos / first), jnp.maximum(0.0, 1.0 - (total - 1 - pos) / last)
    )


def shares(row, col, zone_ref):
    z = [zone_ref[i].astype(F32) for i in range(4)]
    share = jnp.maximum(ramps(row, z[0], z[1], 2048.0), ramps(col, z[2], z[3], 2048.0))
    inside = (row >= 0.0) & (row < 2048.0) & (col >= 0.0) & (col < 2048.0)
    inside = jnp.where(inside, 1.0, 0.0)
    return (1.0 - share) * inside, share * inside


def dot3(a, bh, bl):
    ah, al = split2(a)
    return dot_nn(ah, bh) + dot_nn(ah, bl) + dot_nn(al, bh)


def pick(axis_iota, index, weight):
    return jnp.where(axis_iota == index, 1.0 - weight, 0.0) + jnp.where(
        axis_iota == index + 1.0, weight, 0.0
    )


def fiota(shape, axis):
    return lax.broadcasted_iota(jnp.int32, shape, axis).astype(F32)


def k1(
    anchor_ref, zone_ref, spec_ref, ridx_ref, rwt_ref, cidx_ref, cwt_ref,
    leg_hbm, mask_hbm, fold_hbm, nest_hbm,
    band_out, nest_out,
    leg_ref, mask_ref, fold_ref, nest_ref, load_s,
    gath, sp32, leg2, legx, fs, fsend, frecv, tcos, tsin, acc_c, acc_s, turn, psend, pack_s, pack_r, prow, pbuf,
    ext, damp, cpk_s, cpk_r, rpk, rpk_s, rpk_r, info_s, info_r, nest_s, nest_r,
    field, row_mats, row_part, row_blend, row_x, col_mats, col_part, col_blend, lats, col_q,
    q_out, q_in, q_s, q_r,
    up_s, up_r, dn_s, dn_r, sib_s, sib_r, fa_s, fa_r, w_s, w_r,
):
    w = lax.axis_index("wave")
    y = lax.axis_index("ny")
    wedge = jnp.logical_or(w == 0, w == NW - 1)

    def near(d):
        return lax.rem(y + (NY + d), NY)

    def dev(ww, yy):
        return (ww, yy)

    up_y = lax.rem(y + 2, NY)
    dn_y = lax.rem(y + NY - 2, NY)
    sib_y = y + 1 - 2 * lax.rem(y, 2)

    loads = [pltpu.make_async_copy(a, b, load_s.at[i]) for i, (a, b) in enumerate((
        (nest_hbm, nest_ref), (leg_hbm, leg_ref), (mask_hbm, mask_ref), (fold_hbm, fold_ref)))]
    for c in loads:
        c.start()

    def zero(i, c):
        pbuf[i] = jnp.zeros((KF, WIN), F32)
        return c
    lax.fori_loop(0, SLOTS, zero, 0)
    cpk_r[...] = jnp.zeros((2, 128, 128), BF16)
    rpk_r[...] = jnp.zeros((2, 96, 256), BF16)
    info_r[...] = jnp.zeros((2, 8, 128), F32)
    q_in[...] = jnp.zeros((2, 8, 768), F32)

    barrier = pltpu.get_barrier_semaphore()

    def greet(ww, yy):
        pl.semaphore_signal(barrier, inc=1, device_id=dev(ww, yy), device_id_type=MESH)

    for yy in (up_y, dn_y, sib_y):
        greet(w, yy)

    def greet_wave(o, c):
        greet(lax.rem(w + o, NW), y)
        return c
    lax.fori_loop(1, NW, greet_wave, 0)

    @pl.when(y > 0)
    def _():
        greet(w, near(-1))

    @pl.when(y < NY - 1)
    def _():
        greet(w, near(1))

    @pl.when(jnp.logical_or(jnp.logical_and(wedge, y > 0), y == NY - 1))
    def _():
        greet(NW - 1, near(-1))

    @pl.when(jnp.logical_or(jnp.logical_and(wedge, y < NY - 1), y == 0))
    def _():
        greet(0, near(1))

    sp32[0:8, :] = jnp.zeros((8, 1408), F32)
    for c in range(3):
        v = spec_ref[c].astype(F32)
        last = jnp.broadcast_to(v[:, 1280:1281], (PD, 128))
        for p0, n, r0, rows, lead in CHUNKS:
            r = r0 + lead + c * n
            sp32[r : r + n, 0:1280] = v[p0 : p0 + n, 0:1280]
            sp32[r : r + n, 1280:1408] = last[p0 : p0 + n, :]
    tail = jnp.transpose(sp32[:, 1280:1408], (1, 0))[0:8, :]
    lane = lax.broadcasted_iota(jnp.int32, (8, 128), 1)
    sub = lax.broadcasted_iota(jnp.int32, (8, 896), 0)
    extra = jnp.zeros((8, 896), F32)
    for ch, (p0, n, r0, rows, lead) in enumerate(CHUNKS):
        part = jnp.where((lane >= r0 + lead) & (lane < r0 + rows), tail, 0.0)
        part = jnp.concatenate([part, jnp.zeros((8, 768), F32)], axis=1)
        part = pltpu.roll(part, lax.rem(y * rows - r0 + 896, 896), 1)
        part = jnp.broadcast_to(part[0:1, :], (8, 896))
        extra = jnp.where(sub == ch, part, extra)
    sp32[0:8, 0:768] = extra[:, 0:768]

    def cast_own(i, c):
        r = pl.multiple_of(i * 16, 16)
        gath[y, pl.ds(r, 16), :] = sp32[pl.ds(r, 16), 0:1280].astype(BF16)
        return c
    lax.fori_loop(0, 8, cast_own, 0)

    count = 15 + 3
    count += jnp.where(y < NY - 1, 1, 0) + jnp.where(y > 0, 1, 0)
    count += jnp.where(jnp.logical_and(w == NW - 1, y < NY - 1), 2, 0)
    count += jnp.where(jnp.logical_and(w == 0, y > 0), 2, 0)
    count += jnp.where(jnp.logical_and(w == 0, y == 1), 14, 0)
    count += jnp.where(jnp.logical_and(w == NW - 1, y == NY - 2), 14, 0)
    pl.semaphore_wait(barrier, count)

    def block(origin, piece, half):
        _, _, r0, rows, _ = CHUNKS[piece]
        if half is not None:
            first, count_ = HALVES[piece][half]
            r0, rows = r0 + first, count_
        return gath.at[origin, pl.ds(r0, rows), :]

    def ring(origin, piece, step, upward):
        ref = block(origin, piece, None if step < 3 else (0 if upward else 1))
        s, r = (up_s, up_r) if upward else (dn_s, dn_r)
        return pltpu.make_async_remote_copy(
            src_ref=ref, dst_ref=ref, send_sem=s.at[piece, step], recv_sem=r.at[piece, step],
            device_id=dev(w, up_y if upward else dn_y), device_id_type=MESH)

    def to_sib(origin, piece, idx, half=None):
        ref = block(origin, piece, half)
        return pltpu.make_async_remote_copy(
            src_ref=ref, dst_ref=ref, send_sem=sib_s.at[piece, idx], recv_sem=sib_r.at[piece, idx],
            device_id=dev(w, sib_y), device_id_type=MESH)

    def origin_of(base, step, upward):
        return lax.rem(base + NY - 2 * step, NY) if upward else lax.rem(base + 2 * step, NY)

    def far(piece, upward):
        return HALVES[piece][0 if upward else 1][1] > 0

    def send_own(piece):
        ring(y, piece, 0, True).start()
        ring(y, piece, 0, False).start()
        to_sib(y, piece, 0).start()

    def ring_step(piece, step):
        for upward in (True, False):
            org = origin_of(y, step, upward)
            if step < 4:
                ring(org, piece, step - 1, upward).wait_recv()
                if step < 3 or far(piece, upward):
                    ring(org, piece, step, upward).start()
                to_sib(org, piece, 2 * step - (1 if upward else 0)).start()
            elif far(piece, upward):
                ring(org, piece, 3, upward).wait_recv()
                to_sib(org, piece, 7 if upward else 8, 0 if upward else 1).start()

    def sib_each(base, piece, go):
        go(to_sib(base, piece, 0))
        for step in range(1, 5):
            for upward in (True, False):
                org = origin_of(base, step, upward)
                if step < 4:
                    go(to_sib(org, piece, 2 * step - (1 if upward else 0)))
                elif far(piece, upward):
                    go(to_sib(org, piece, 7 if upward else 8, 0 if upward else 1))

    def sib_wait(piece):
        sib_each(sib_y, piece, lambda c: c.wait_recv())

    def sends_done(piece):
        for step in range(4):
            for upward in (True, False):
                if step < 3 or far(piece, upward):
                    ring(y, piece, step, upward).wait_send()
        sib_each(y, piece, lambda c: c.wait_send())

    anchor = anchor_ref[0].astype(F32)

    def leg_rows(ch):
        p0, n, _, _, _ = CHUNKS[ch]
        pos = lax.broadcasted_iota(jnp.int32, (1, 1280), 1)

        def one(p, c):
            limit = TRUNC - (w * PD + p0 + p)
            low = jnp.where(pos < limit, 1.0, 0.0)
            rows = leg_ref[p0 + p]
            tile = rows[:, 0:1280]
            a = pl.multiple_of(p * 16, 16)
            b = pl.multiple_of(n * 16 + p * 16, 16)
            leg2[ch % 2, pl.ds(a, 16), :] = tile * low.astype(BF16)
            leg2[ch % 2, pl.ds(b, 16), :] = tile * (1.0 - low).astype(BF16)
            last = rows[:, 1280:1281].astype(F32)
            legx[ch % 2, pl.ds(a, 16), :] = jnp.broadcast_to(last, (16, 128))
            return c
        lax.fori_loop(0, n, one, 0)

    def last_row(ch, width):
        v = gath[0, 0:16, 0:width].astype(F32)
        for i in range(1, NY):
            v = v + gath[i, 0:16, 0:width].astype(F32)
        return v[ch : ch + 1, :]

    def fourier(ch):
        p0, n, r0, rows, lead = CHUNKS[ch]
        width = 16 * rows
        g = gath[:, r0 : r0 + rows, :].reshape(width, 1280)
        x = last_row(ch, width)
        lane16 = lax.broadcasted_iota(jnp.int32, (16, 128), 1) % 16
        if ch == 0:
            res = dot_nt(leg2[0, 0:256, :], g)
            rank1 = jnp.concatenate([jnp.zeros((128, width), F32),
                                     jnp.tile(legx[0, 0:128, :], (1, width // 128)) * x], 0)
            hi, lo = split2((res + rank1) * mask_ref[...].astype(F32))
            fs[0:16] = (dot_nn(hi, fold_ref[0]) + dot_nn(lo, fold_ref[1])).reshape(16, 16, 128)
        else:
            for h in range(2):
                res = dot_nt(leg2[ch % 2, 256 * h : 256 * h + 256, :], g)
                for p in range(n):
                    v = jnp.zeros((16, 128), F32)
                    for j in range(width // 128):
                        q = res[16 * p : 16 * p + 16, 128 * j : 128 * j + 128]
                        if h == 1:
                            q = q + legx[ch % 2, 16 * p : 16 * p + 16, :] * x[:, 128 * j : 128 * j + 128]
                        q = jnp.where(lane16 == p, q, 0.0)
                        v = v + (pltpu.roll(q, (j - p) % 128, 1) if j != p else q)
                    hi = v.astype(BF16).astype(F32)
                    lo = (v - hi).astype(BF16).astype(F32)
                    fs[16 * h + p] = hi + pltpu.roll(lo, 8, 1)
        f0 = (0, 16, 48)[ch]
        for l in range(16):
            fsend[l, f0 : f0 + 2 * n, :] = fs[0 : 2 * n, l, :].astype(BF16)

    def wave_copy(ch, o):
        n = CHUNKS[ch][1]
        f0 = (0, 16, 48)[ch]
        to = lax.rem(w + o, NW)
        return pltpu.make_async_remote_copy(
            src_ref=fsend.at[to, pl.ds(f0, 2 * n), :], dst_ref=frecv.at[ch, w, pl.ds(0, 2 * n), :],
            send_sem=fa_s.at[ch, o], recv_sem=fa_r.at[ch, o],
            device_id=dev(to, y), device_id_type=MESH)

    def wave_send(ch):
        n = CHUNKS[ch][1]
        f0 = (0, 16, 48)[ch]
        lax.fori_loop(1, NW, lambda o, c: (wave_copy(ch, o).start(), c)[1], 0)
        frecv[ch, w, 0 : 2 * n, :] = fsend[w, f0 : f0 + 2 * n, :]

    def wave_recv(ch):
        lax.fori_loop(1, NW, lambda o, c: (wave_copy(ch, o).wait_recv(), c)[1], 0)

    def wave_done(ch):
        lax.fori_loop(1, NW, lambda o, c: (wave_copy(ch, o).wait_send(), c)[1], 0)

    def table(ch):
        p0, n, _, _, _ = CHUNKS[ch]
        k0 = KOFF[ch]
        shift = 4 if n == 16 else 3

        def one(t, c):
            q = t * 128 + lax.broadcasted_iota(jnp.int32, (1, 128), 1)
            ww = q >> (shift + 1)
            h = (q >> shift) & 1
            pg = ww * PD + p0 + (q & (n - 1))
            mi = jnp.where(h == 0, pg, TRUNC - 1 - pg)
            m = mi.astype(F32)
            s = jnp.where(mi == 0, 1.0, 2.0)

            def angle(x):
                return (x - NLON * jnp.floor(x * (1.0 / NLON))) * (2.0 * math.pi / NLON)

            d = lax.broadcasted_iota(jnp.int32, (LON, 128), 0).astype(F32)
            fine = angle(m * d)
            cf, sf = jnp.cos(fine) * s, jnp.sin(fine) * s
            b = lax.broadcasted_iota(jnp.int32, (16, 128), 0).astype(F32) * LON
            coarse = angle(m * (anchor + b))
            cc, sc = jnp.cos(coarse), jnp.sin(coarse)
            col = pl.multiple_of(k0 + t * 128, 128)
            for i in range(16):
                ci, si = cc[i : i + 1, :], sc[i : i + 1, :]
                vc = ci * cf - si * sf
                vs = -(si * cf + ci * sf)
                hi, lo = split2(vc)
                tcos[0, LON * i : LON * i + LON, pl.ds(col, 128)] = hi
                tcos[1, LON * i : LON * i + LON, pl.ds(col, 128)] = lo
                hi, lo = split2(vs)
                tsin[0, LON * i : LON * i + LON, pl.ds(col, 128)] = hi
                tsin[1, LON * i : LON * i + LON, pl.ds(col, 128)] = lo
            return c
        lax.fori_loop(0, 2 * n * 16 // 128, one, 0)

    def contract(ch):
        n = CHUNKS[ch][1]
        k0, k = KOFF[ch], 2 * n * 16
        f = frecv[ch, :, 0 : 2 * n, :].reshape(k, 128)

        for tab, acc in ((tcos, acc_c), (tsin, acc_s)):
            v = dot_nn(tab[0, :, k0 : k0 + k], f) + dot_nn(tab[1, :, k0 : k0 + k], f)
            if ch == 0:
                acc[...] = v
            else:
                acc[...] = acc[...] + v

    lane_h = lax.broadcasted_iota(jnp.int32, (128, 128), 1)

    def nest_copy(i):
        if i < 4:
            src, dst = (cpk_s, cpk_r) if i < 2 else (rpk_s, rpk_r)
            src, dst = src.at[i % 2], dst.at[i % 2]
        else:
            src, dst = info_s, info_r.at[i - 4]
        to = (dev(lax.rem(w + NW - 1, NW), y), dev(lax.rem(w + 1, NW), y), dev(w, near(-1)), dev(w, near(1)))[i % 4]
        return pltpu.make_async_remote_copy(
            src_ref=src, dst_ref=dst, send_sem=nest_s.at[i], recv_sem=nest_r.at[i],
            device_id=to, device_id_type=MESH)

    can_send = (w > 0, w < NW - 1, y > 0, y < NY - 1)
    can_recv = (w < NW - 1, w > 0, y < NY - 1, y > 0)

    def nest_do(which, cond, go):
        for i in which:
            @pl.when(cond[i % 4])
            def _(i=i):
                go(nest_copy(i))

    def nest_pack():
        info_s[...] = jnp.zeros((8, 128), F32)
        info_s[0:1, :] = ridx_ref[...].astype(F32)
        info_s[1:2, :] = rwt_ref[...]
        loads[0].wait()
        info_s[2:3, :] = cidx_ref[...].astype(F32)
        info_s[3:4, :] = cwt_ref[...]
        left = jnp.zeros((128, 128), F32)
        right = jnp.zeros((128, 128), F32)
        for k in range(KF):
            v = nest_ref[k].astype(F32)
            here = (lane_h >= 4 * k) & (lane_h < 4 * k + 4)
            left = jnp.where(here, pltpu.roll(v, 4 * k, 1) if k else v, left)
            right = jnp.where(here, pltpu.roll(v, 4 * k + 4, 1), right)
        cpk_s[0] = left.astype(BF16)
        cpk_s[1] = right.astype(BF16)
        row = (lax.broadcasted_iota(jnp.int32, (EXT, 256), 0) + (128 * y - 8)).astype(F32)
        j = lax.broadcasted_iota(jnp.int32, (EXT, 256), 1)
        col = (jnp.where(j < 192, j, j - 256) + 128 * w).astype(F32)
        keep, _ = shares(row, col, zone_ref)
        damp[...] = keep * DIFFUSION
        nest_do((0, 1, 4, 5), can_send, lambda c: c.start())

    def nest_cols():
        nest_do((0, 1), can_recv, lambda c: c.wait_recv())
        from_right = cpk_r[0].astype(F32)
        from_left = cpk_r[1].astype(F32)

        def one(k, c):
            a = pltpu.roll(from_right, lax.rem(128 - 4 * k, 128), 1)
            b = pltpu.roll(from_left, lax.rem(252 - 4 * k, 128), 1)
            e = jnp.where(lane_h < 4, a, jnp.where(lane_h >= 124, b, 0.0))
            ext[k, 0:8, :] = jnp.zeros((8, 256), F32)
            ext[k, 136:144, :] = jnp.zeros((8, 256), F32)
            ext[k, 8:136, 0:128] = nest_ref[k].astype(F32)
            ext[k, 8:136, 128:256] = e
            return c
        lax.fori_loop(0, KF, one, 0)
        for i, r in ((0, 8), (1, 132)):
            for k in range(KF):
                rpk[4 * k : 4 * k + 4, :] = ext[k, r : r + 4, :]
            rpk_s[i] = rpk[...].astype(BF16)
        nest_do((2, 3), can_send, lambda c: c.start())

    def nest_rows():
        nest_do((2, 3), can_recv, lambda c: c.wait_recv())
        for i, r in ((0, 136), (1, 4)):
            rpk[...] = rpk_r[i].astype(F32)
            for k in range(KF):
                ext[k, r : r + 4, :] = rpk[4 * k : 4 * k + 4, :]

    def nest_sweeps(k0, k1_):
        def one(k, c):
            x = ext[k]
            for _ in range(NSWEEP):
                t = x + pltpu.roll(x, 1, 0) + pltpu.roll(x, EXT - 1, 0)
                t = t + pltpu.roll(x, 1, 1) + pltpu.roll(x, 255, 1)
                x = t * damp[...]
            field[k] = x[8:136, 0:128]
            nest_out[k] = x[8:136, 0:128].astype(BF16)
            return c
        lax.fori_loop(k0, k1_, one, 0)

    def nest_done():
        nest_do((4, 5), can_recv, lambda c: c.wait_recv())
        nest_do(range(6), can_send, lambda c: c.wait_send())

    row_edge = jnp.logical_or(y == 0, y == NY - 1)
    first = jnp.where(y == 0, 0, 104)
    cbase = jnp.where(w == 0, 0, 96)

    def strip_prep():
        lon0 = (w * LON - 48).astype(F32)
        lat0 = (y * 16 - 1).astype(F32)
        own, right, left = info_s[...], info_r[0], info_r[1]
        lane = lax.broadcasted_iota(jnp.int32, (1, 128), 1)
        turned = jnp.transpose(jnp.concatenate([own, jnp.zeros((120, 128), F32)], 0), (1, 0))

        @pl.when(row_edge)
        def _():
            far_i = jnp.where(lane < 4, right[2:3], jnp.where(lane >= 124, left[2:3], -4096.0))
            far_w = jnp.where(lane < 4, right[3:4], left[3:4])
            cidx = jnp.concatenate([own[2:3], far_i], 1) - lon0
            cwt = jnp.concatenate([own[3:4], far_w], 1)
            hi, lo = split2(pick(fiota((128, 256), 0), cidx, cwt))
            row_mats[0] = hi
            row_mats[1] = lo
            cols = jnp.where(y == 0, turned[0:24, :], turned[104:128, :])
            ridx = cols[:, 0:1] - lat0
            rwt = cols[:, 1:2]
            row = fiota((24, 256), 0) + (128 * y + first).astype(F32)
            j = lax.broadcasted_iota(jnp.int32, (24, 256), 1)
            col = (jnp.where(j < 192, j, j - 256) + 128 * w).astype(F32)
            keep, share = shares(row, col, zone_ref)
            row_part[0] = jnp.where((row < 20.0) | (row >= 2028.0), keep * DIFFUSION, 0.0)
            row_part[1] = jnp.where((row < 16.0) | (row >= 2032.0), share, 0.0)
            row_blend[...] = pick(fiota((24, SLOTS), 1), ridx, rwt)

        @pl.when(wedge)
        def _():
            vec = jnp.concatenate([own[2:4] - jnp.where(fiota((2, 128), 0) == 0.0, lon0, 0.0),
                                   jnp.zeros((6, 128), F32)], 0)
            vec = jnp.where(w == 0, vec, pltpu.roll(vec, 32, 1))
            for i in range(4):
                v = pltpu.roll(vec, LON * i, 1) if i else vec
                here = (lane >= LON * i) & (lane < LON * i + LON)
                m = jnp.where(here, pick(fiota((128, 128), 0), v[0:1], v[1:2]), 0.0)
                hi, lo = split2(m)
                col_mats[0, 128 * i : 128 * i + 128, :] = hi
                col_mats[1, 128 * i : 128 * i + 128, :] = lo
            col_blend[...] = pick(fiota((128, SLOTS), 1), turned[:, 0:1] - lat0, turned[:, 1:2])
            row = fiota((EXT, 128), 0) + (128 * y - 8).astype(F32)
            inner = lax.broadcasted_iota(jnp.int32, (EXT, 128), 1) % LON
            col = (inner + cbase + 128 * w).astype(F32)
            keep, share = shares(row, col, zone_ref)
            share = jnp.where((col < 16.0) | (col >= 2032.0), share, 0.0)
            col_part[0] = keep * DIFFUSION
            col_part[1] = jnp.where((row >= 16.0) & (row < 2032.0), share, 0.0)

    def q_copy(i):
        return pltpu.make_async_remote_copy(
            src_ref=q_out.at[i], dst_ref=q_in.at[i], send_sem=q_s.at[i], recv_sem=q_r.at[i],
            device_id=dev(w, near(1 if i else -1)), device_id_type=MESH)

    def q_each(cond, go):
        for i in range(2):
            @pl.when(jnp.logical_and(wedge, cond[i]))
            def _(i=i):
                go(q_copy(i))

    q_send = (y > 0, y < NY - 1)
    q_recv = (y < NY - 1, y > 0)

    def gather_rows():
        for k in range(KF):
            lats[:, 128 * k : 128 * k + 128] = pbuf[:, k, :]

    def col_source():
        @pl.when(wedge)
        def _():
            v = jnp.concatenate([lats[:, 512 * t : 512 * t + 512] for t in range(KF // 4)], 0)
            v = dot3(v, col_mats[0], col_mats[1])
            v = jnp.concatenate([v[24 * t : 24 * t + 24, :] for t in range(KF // 4)], 1)
            hi, lo = split2(v)
            v = dot3(col_blend[...], hi, lo)
            share = col_part[1, 8:136, :]
            col_q[0:8, :] = jnp.zeros((8, 768), F32)
            col_q[136:144, :] = jnp.zeros((8, 768), F32)
            for t in range(KF // 4):
                col_q[8:136, 128 * t : 128 * t + 128] = v[:, 128 * t : 128 * t + 128] * share
            q_out[0] = col_q[8:16, :]
            q_out[1] = col_q[128:136, :]

        q_each(q_send, lambda c: c.start())

    def row_strip():
        @pl.when(row_edge)
        def _():
            hi, lo = split2(lats[...])
            v = dot3(row_blend[...], hi, lo)
            v = jnp.concatenate([v[:, 128 * k : 128 * k + 128] for k in range(KF)], 0)
            row_x[...] = dot3(v, row_mats[0], row_mats[1])
            at = pl.ds(pl.multiple_of(first, 8), 24)

            def some(n, c):
                ks = [n * 6 + i for i in range(6)]
                qs = [row_x[pl.ds(pl.multiple_of(k * 24, 8), 24), :] * row_part[1] for k in ks]
                gs = list(qs)
                for _ in range(NSWEEP - 1):
                    vs = [g + pltpu.roll(g, 1, 0) + pltpu.roll(g, 23, 0)
                          + pltpu.roll(g, 1, 1) + pltpu.roll(g, 255, 1) for g in gs]
                    gs = [v * row_part[0] + q for v, q in zip(vs, qs)]
                for k, g in zip(ks, gs):
                    field[k, at, :] = field[k, at, :] + g[:, 0:128]
                return c
            lax.fori_loop(0, KF // 6, some, 0)

        @pl.when(jnp.logical_and(row_edge, jnp.logical_not(wedge)))
        def _():
            at = pl.ds(pl.multiple_of(jnp.where(y == 0, 0, 96), 32), 32)

            def last(k, c):
                nest_out[k, at, :] = field[k, at, :].astype(BF16)
                return c
            lax.fori_loop(0, KF, last, 0)

    def side_masks(rows):
        inner = lax.broadcasted_iota(jnp.int32, (rows, 128), 1) % LON
        return inner != 0, inner != LON - 1

    def side_sweeps(qs, keep, rows):
        not_first, not_last = side_masks(rows)
        gs = list(qs)
        for _ in range(NSWEEP - 1):
            vs = [g + pltpu.roll(g, 1, 0) + pltpu.roll(g, rows - 1, 0)
                  + jnp.where(not_first, pltpu.roll(g, 1, 1), 0.0)
                  + jnp.where(not_last, pltpu.roll(g, 127, 1), 0.0) for g in gs]
            gs = [v * keep + q for v, q in zip(vs, qs)]
        return gs

    def col_strip():
        @pl.when(wedge)
        def _():
            def some(n, c):
                at = [pl.ds(pl.multiple_of((n * 2 + i) * 128, 128), 128) for i in range(2)]
                gs = side_sweeps([col_q[:, a] for a in at], col_part[0], EXT)
                for a, g in zip(at, gs):
                    col_q[:, a] = g
                return c
            lax.fori_loop(0, KF // 8, some, 0)

        q_each(q_recv, lambda c: c.wait_recv())

        @pl.when(wedge)
        def _():
            sub = lax.broadcasted_iota(jnp.int32, (8, 768), 0)
            blank = jnp.zeros((8, 768), F32)
            above = jnp.concatenate([jnp.where(sub >= 4, q_in[1], 0.0), blank], 0)
            below = jnp.concatenate([blank, jnp.where(sub < 4, q_in[0], 0.0)], 0)
            tiles = range(KF // 4)
            ga = side_sweeps([above[:, 128 * t : 128 * t + 128] for t in tiles], col_part[0, 0:16, :], 16)
            gb = side_sweeps([below[:, 128 * t : 128 * t + 128] for t in tiles], col_part[0, 128:144, :], 16)
            for t in tiles:
                a = slice(128 * t, 128 * t + 128)
                col_q[8:16, a] = col_q[8:16, a] + ga[t][8:16]
                col_q[128:136, a] = col_q[128:136, a] + gb[t][0:8]
            lane_h = lax.broadcasted_iota(jnp.int32, (128, 128), 1)
            strip = (lane_h >= cbase) & (lane_h < cbase + LON)

            def add(n, c):
                for t in (n * 2, n * 2 + 1):
                    g = col_q[8:136, pl.ds(pl.multiple_of(t * 128, 128), 128)]
                    for i in range(4):
                        part = pltpu.roll(g, lax.rem(cbase + 128 - LON * i, 128), 1)
                        k = 4 * t + i
                        nest_out[k] = (field[k] + jnp.where(strip, part, 0.0)).astype(BF16)
                return c
            lax.fori_loop(0, KF // 8, add, 0)

    send_own(0)
    send_own(1)
    nest_pack()
    ring_step(0, 1)
    send_own(2)
    nest_cols()
    table(0)
    ring_step(0, 2)
    ring_step(1, 1)
    table(1)
    loads[1].wait()
    leg_rows(0)
    table(2)
    nest_rows()
    leg_rows(1)
    ring_step(0, 3)
    ring_step(2, 1)
    nest_sweeps(0, 8)
    ring_step(1, 2)
    ring_step(0, 4)
    sib_wait(0)
    loads[2].wait()
    loads[3].wait()
    fourier(0)
    wave_send(0)
    ring_step(2, 2)
    nest_sweeps(8, 16)
    ring_step(1, 3)
    wave_recv(0)
    contract(0)
    ring_step(2, 3)
    nest_sweeps(16, KF)
    nest_done()
    strip_prep()
    ring_step(1, 4)
    leg_rows(2)
    ring_step(2, 4)
    sib_wait(1)
    fourier(1)
    sib_wait(2)
    wave_send(1)
    fourier(2)
    wave_send(2)
    wave_recv(1)
    contract(1)
    wave_recv(2)
    contract(2)

    prow[:, 0:128] = jnp.zeros((KF, 128), F32)
    prow[:, 512:640] = jnp.zeros((KF, 128), F32)
    for i in range(4):
        turn[0] = jnp.transpose(acc_c[128 * i : 128 * i + 128, :], (1, 0)).reshape(8, 16, 128)
        turn[1] = jnp.transpose(acc_s[128 * i : 128 * i + 128, :], (1, 0)).reshape(8, 16, 128)
        val = [turn[0, :, j, :] + turn[0, :, j + 8, :] + turn[1, :, j + 3, :] + turn[1, :, j + 11, :]
               for j in range(3)]
        prow[:, 48 + 128 * i : 176 + 128 * i] = jnp.concatenate(val, 0)
    lane = lax.broadcasted_iota(jnp.int32, (8, 128), 1)
    for v in range(NW):
        window = prow[:, LON * v : LON * v + WIN]
        psend[v] = window
        packed = jnp.zeros((8, 128), F32)
        for j in range(3):
            part = pltpu.roll(window[8 * j : 8 * j + 8], (LON * j + 80) % 128, 1)
            packed = jnp.where((lane >= LON * j) & (lane < LON * j + LON), part, packed)
            if v in (0, NW - 1):
                beside = 80 if v == 0 else 47
                part = pltpu.roll(window[8 * j : 8 * j + 8], (96 + j - beside) % 128, 1)
                packed = jnp.where(lane == 96 + j, part, packed)
        pack_s[v] = packed

    def win(src, to_w, to_y, slot, sem):
        return pltpu.make_async_remote_copy(
            src_ref=psend.at[src], dst_ref=pbuf.at[slot], send_sem=w_s.at[sem], recv_sem=w_r.at[slot],
            device_id=dev(to_w, to_y), device_id_type=MESH)

    def edges(go):
        @pl.when(jnp.logical_and(w == 0, y > 0))
        def _():
            go(0, 0, near(-1), 17, 16)
            go(NW - 1, NW - 1, near(-1), 17, 17)

        @pl.when(jnp.logical_and(w == NW - 1, y < NY - 1))
        def _():
            go(0, 0, near(1), 0, 18)
            go(NW - 1, NW - 1, near(1), 0, 19)

        @pl.when(jnp.logical_and(w == 0, y == 1))
        def _():
            lax.fori_loop(1, NW - 1, lambda v, c: (go(v, v, near(-1), 17, 20 + v), c)[1], 0)

        @pl.when(jnp.logical_and(w == NW - 1, y == NY - 2))
        def _():
            lax.fori_loop(1, NW - 1, lambda v, c: (go(v, v, near(1), 0, 20 + v), c)[1], 0)

    def own_win(o):
        to = lax.rem(w + o, NW)
        return win(to, to, y, 1 + w, o)

    def own_pack(o):
        to = lax.rem(w + o, NW)
        return pltpu.make_async_remote_copy(
            src_ref=pack_s.at[to], dst_ref=pack_r.at[w], send_sem=w_s.at[o], recv_sem=w_r.at[1 + w],
            device_id=dev(to, y), device_id_type=MESH)

    def own_each(go):
        @pl.when(row_edge)
        def _():
            lax.fori_loop(1, NW, lambda o, c: (go(own_win(o)), c)[1], 0)

        @pl.when(jnp.logical_not(row_edge))
        def _():
            lax.fori_loop(1, NW, lambda o, c: (go(own_pack(o)), c)[1], 0)

    own_each(lambda c: c.start())
    edges(lambda *a: win(*a).start())
    pbuf[1 + w] = psend[w]
    pack_r[w] = pack_s[w]

    for ch in range(3):
        wave_done(ch)
    for piece in range(len(CHUNKS)):
        sends_done(piece)

    def got(slot):
        win(0, w, sib_y, slot, 0).wait_recv()

    here_whole = row_edge

    @pl.when(here_whole)
    def _():
        lax.fori_loop(1, NW, lambda o, c: (got(1 + lax.rem(w + o, NW)), c)[1], 0)

    @pl.when(jnp.logical_not(here_whole))
    def _():
        def one(o, c):
            src = lax.rem(w + o, NW)
            pltpu.make_async_remote_copy(
                src_ref=pack_s.at[0], dst_ref=pack_r.at[src], send_sem=w_s.at[0],
                recv_sem=w_r.at[1 + src], device_id=dev(w, sib_y), device_id_type=MESH).wait_recv()
            return c
        lax.fori_loop(1, NW, one, 0)

    @pl.when(jnp.logical_or(jnp.logical_and(wedge, y > 0), y == NY - 1))
    def _():
        got(0)

    @pl.when(jnp.logical_or(jnp.logical_and(wedge, y < NY - 1), y == 0))
    def _():
        got(17)

    @pl.when(jnp.logical_and(wedge, jnp.logical_not(row_edge)))
    def _():
        beside = jnp.where(w == 0, 80, 47)
        for s in range(16):
            for j in range(3):
                a = pltpu.roll(pack_r[s], (48 - LON * j) % 128, 1)
                b = pltpu.roll(pack_r[s], lax.rem(beside + 128 - 96 - j + 128, 128), 1)
                a = jnp.where((lane >= 48) & (lane < 80), a, jnp.where(lane == beside, b, 0.0))
                pbuf[1 + s, 8 * j : 8 * j + 8, :] = a

    @pl.when(jnp.logical_or(wedge, row_edge))
    def _():
        gather_rows()

    col_source()
    row_strip()
    col_strip()

    @pl.when(here_whole)
    def _():
        for k in range(KF):
            band_out[k] = pltpu.roll(pbuf[1:17, k, :], 80, 1)[:, 0:LON]

    @pl.when(jnp.logical_not(here_whole))
    def _():
        for i in range(8):
            v = pack_r[:, i, :]
            for j in range(3):
                band_out[8 * j + i] = (pltpu.roll(v, 128 - LON * j, 1) if j else v)[:, 0:LON]

    q_each(q_send, lambda c: c.wait_send())
    own_each(lambda c: c.wait_send())
    edges(lambda *a: win(*a).wait_send())


def vmem_spec():
    return pl.BlockSpec(memory_space=pltpu.VMEM)


def spectral(spectra, legendre, lon_anchor, zone_width, nest_state, ridx, rwt, cidx, cwt):
    spec = jnp.transpose(spectra, (1, 0, 2))
    mask, fold = first_consts()
    np_ = len(CHUNKS)
    smem = pl.BlockSpec(memory_space=pltpu.SMEM)
    dma = pltpu.SemaphoreType.DMA
    return pl.pallas_call(
        k1,
        out_shape=(
            jax.ShapeDtypeStruct((KF, 16, LON), F32),
            jax.ShapeDtypeStruct((KF, 128, 128), BF16),
        ),
        in_specs=[smem, smem] + [vmem_spec()] * 5 + [pl.BlockSpec(memory_space=pl.ANY)] * 4,
        out_specs=(vmem_spec(), vmem_spec()),
        scratch_shapes=[
            pltpu.VMEM((PD, 16, 1281), BF16),
            pltpu.VMEM(mask.shape, BF16), pltpu.VMEM(fold.shape, BF16),
            pltpu.VMEM((KF, 128, 128), BF16),
            dma((4,)),
            pltpu.VMEM((NY, 128, 1280), BF16),
            pltpu.VMEM((128, 1408), F32),
            pltpu.VMEM((2, 512, 1280), BF16),
            pltpu.VMEM((2, 256, 128), F32),
            pltpu.VMEM((32, 16, 128), F32),
            pltpu.VMEM((16, 80, 128), BF16),
            pltpu.VMEM((3, 16, 32, 128), BF16),
            pltpu.VMEM((2, NLB, NKEY), BF16),
            pltpu.VMEM((2, NLB, NKEY), BF16),
            pltpu.VMEM((NLB, 128), F32),
            pltpu.VMEM((NLB, 128), F32),
            pltpu.VMEM((2, 8, 16, 128), F32),
            pltpu.VMEM((16, KF, WIN), F32),
            pltpu.VMEM((16, 8, 128), F32),
            pltpu.VMEM((16, 8, 128), F32),
            pltpu.VMEM((KF, 640), F32),
            pltpu.VMEM((SLOTS, KF, WIN), F32),
            pltpu.VMEM((KF, EXT, 256), F32),
            pltpu.VMEM((EXT, 256), F32),
            pltpu.VMEM((2, 128, 128), BF16),
            pltpu.VMEM((2, 128, 128), BF16),
            pltpu.VMEM((96, 256), F32),
            pltpu.VMEM((2, 96, 256), BF16),
            pltpu.VMEM((2, 96, 256), BF16),
            pltpu.VMEM((8, 128), F32),
            pltpu.VMEM((2, 8, 128), F32),
            dma((6,)), dma((6,)),
            pltpu.VMEM((KF, 128, 128), F32),
            pltpu.VMEM((2, 128, 256), BF16),
            pltpu.VMEM((2, 24, 256), F32),
            pltpu.VMEM((24, SLOTS), F32),
            pltpu.VMEM((24 * KF, 256), F32),
            pltpu.VMEM((2, 512, 128), BF16),
            pltpu.VMEM((2, EXT, 128), F32),
            pltpu.VMEM((128, SLOTS), F32),
            pltpu.VMEM((SLOTS, 128 * KF), F32),
            pltpu.VMEM((EXT, 768), F32),
            pltpu.VMEM((2, 8, 768), F32),
            pltpu.VMEM((2, 8, 768), F32),
            dma((2,)), dma((2,)),
            dma((np_, 4)), dma((np_, 4)),
            dma((np_, 4)), dma((np_, 4)),
            dma((np_, 9)), dma((np_, 9)),
            dma((3, 16)), dma((3, 16)),
            dma((40,)), dma((SLOTS,)),
        ],
        compiler_params=pltpu.CompilerParams(
            collective_id=0, has_side_effects=True, vmem_limit_bytes=60 * 1024 * 1024),
    )(lon_anchor, zone_width, spec, ridx, rwt, cidx, cwt, legendre,
      jnp.asarray(mask, BF16), jnp.asarray(fold, BF16), nest_state)


def hand_over(band_in, nest_in, band_out, nest_out, band_v, nest_v, sem):
    trips = [((band_in, band_v), (band_v, band_out))]
    for i in range(4):
        at = pl.ds(6 * i, 6)
        trips.append(((nest_in.at[at], nest_v.at[at]), (nest_v.at[at], nest_out.at[at])))
    trips = [tuple(pltpu.make_async_copy(*c, sem.at[way, i]) for way, c in enumerate(trip))
             for i, trip in enumerate(trips)]
    for get, _ in trips:
        get.start()
    for get, put in trips:
        get.wait()
        put.start()
    for _, put in trips:
        put.wait()


def results(band, nest):
    hbm = pl.BlockSpec(memory_space=pl.ANY)
    return pl.pallas_call(
        hand_over,
        out_shape=(jax.ShapeDtypeStruct(band.shape, F32), jax.ShapeDtypeStruct(nest.shape, BF16)),
        in_specs=[hbm, hbm], out_specs=(hbm, hbm),
        scratch_shapes=[pltpu.VMEM(band.shape, F32), pltpu.VMEM(nest.shape, BF16),
                        pltpu.SemaphoreType.DMA((2, 5))],
        compiler_params=pltpu.CompilerParams(vmem_limit_bytes=60 * 1024 * 1024),
    )(band, nest)


def body(
    spectra, legendre, lon_anchor, row_index, row_weight, col_index, col_weight, zone_width,
    nest_state,
):
    band, nest = spectral(
        spectra, legendre, lon_anchor, zone_width, nest_state,
        row_index.reshape(1, 128), row_weight.reshape(1, 128),
        col_index.reshape(1, 128), col_weight.reshape(1, 128),
    )
    return results(band, nest)


def solution(mesh):
    placed = (
        P("wave", "ny", None), P("wave", "ny", None), P(), P("ny"), P("ny"), P("wave"), P("wave"),
        P(), P(None, "ny", "wave"),
    )
    return jax.shard_map(
        body, mesh=mesh, in_specs=placed,
        out_specs=(P(None, "ny", "wave"), P(None, "ny", "wave")), check_vma=False,
    )
```

```python
import functools
import math

import jax
import jax.numpy as jnp
import numpy as np
from jax import lax
from jax.experimental import pallas as pl
from jax.experimental.pallas import tpu as pltpu
from jax.sharding import PartitionSpec as P

MESH = pl.DeviceIdType.MESH
NW = 16
NY = 16
PD = 40
TRUNC = 1280
NLON = 5120
LON = 32
KF = 24
NLB = 512
NSWEEP = 4
DIFFUSION = 0.2
F32 = jnp.float32
BF16 = jnp.bfloat16
CHUNKS = ((0, 8, 0, 32, 8), (8, 16, 32, 48, 0), (24, 16, 80, 48, 0))
HALVES = (((0, 16), (16, 16)), ((0, 48), (0, 0)), ((0, 0), (0, 48)))
KOFF = (0, 256, 768)
NKEY = 1280
SLOTS = 24
EXT = 144
WIN = 128


def lane_of(chan):
    return 16 * (chan % 8) + chan // 8


def first_consts():
    _, n, _, rows, lead = CHUNKS[0]
    row = np.arange(2 * n * 16)
    col = np.arange(16 * rows)
    inner = col % rows - lead
    cpair = np.where(inner >= 0, inner % n, -1)
    mask = ((row // 16) % n)[:, None] == cpair[None, :]
    fold = np.zeros((2, 16 * rows, 128), np.float32)
    for i in range(16 * rows):
        if inner[i] >= 0:
            lane = lane_of((i // rows) * 3 + inner[i] // n)
            fold[0, i, lane] = 1.0
            fold[1, i, lane + 8] = 1.0
    return mask.astype(np.float32), fold


def split2(x):
    hi = x.astype(BF16)
    lo = (x - hi.astype(F32)).astype(BF16)
    return hi, lo


def dot_nt(a, b):
    return lax.dot_general(a, b, (((1,), (1,)), ((), ())), preferred_element_type=F32)


def dot_nn(a, b):
    return lax.dot_general(a, b, (((1,), (0,)), ((), ())), preferred_element_type=F32)


def ramps(pos, first, last, total):
    return jnp.maximum(
        jnp.maximum(0.0, 1.0 - pos / first), jnp.maximum(0.0, 1.0 - (total - 1 - pos) / last)
    )


def shares(row, col, zone_ref):
    z = [zone_ref[i].astype(F32) for i in range(4)]
    share = jnp.maximum(ramps(row, z[0], z[1], 2048.0), ramps(col, z[2], z[3], 2048.0))
    inside = (row >= 0.0) & (row < 2048.0) & (col >= 0.0) & (col < 2048.0)
    inside = jnp.where(inside, 1.0, 0.0)
    return (1.0 - share) * inside, share * inside


def dot3(a, bh, bl):
    ah, al = split2(a)
    return dot_nn(ah, bh) + dot_nn(ah, bl) + dot_nn(al, bh)


def pick(axis_iota, index, weight):
    return jnp.where(axis_iota == index, 1.0 - weight, 0.0) + jnp.where(
        axis_iota == index + 1.0, weight, 0.0
    )


def fiota(shape, axis):
    return lax.broadcasted_iota(jnp.int32, shape, axis).astype(F32)


def k1(
    anchor_ref, zone_ref, spec_ref, ridx_ref, rwt_ref, cidx_ref, cwt_ref,
    leg_hbm, mask_hbm, fold_hbm, nest_hbm,
    band_out, nest_out,
    leg_ref, mask_ref, fold_ref, nest_ref, load_s,
    gath, sp32, leg2, legx, fs, fsend, frecv, tcos, tsin, acc_c, acc_s, turn, psend, pack_s, pack_r, prow, pbuf,
    ext, damp, cpk_s, cpk_r, rpk, rpk_s, rpk_r, info_s, info_r, nest_s, nest_r,
    field, row_mats, row_part, row_blend, row_x, col_mats, col_part, col_blend, lats, col_q,
    q_out, q_in, q_s, q_r,
    up_s, up_r, dn_s, dn_r, sib_s, sib_r, fa_s, fa_r, w_s, w_r,
):
    w = lax.axis_index("wave")
    y = lax.axis_index("ny")
    wedge = jnp.logical_or(w == 0, w == NW - 1)

    def near(d):
        return lax.rem(y + (NY + d), NY)

    def dev(ww, yy):
        return (ww, yy)

    up_y = lax.rem(y + 2, NY)
    dn_y = lax.rem(y + NY - 2, NY)
    sib_y = y + 1 - 2 * lax.rem(y, 2)

    loads = [pltpu.make_async_copy(a, b, load_s.at[i]) for i, (a, b) in enumerate((
        (nest_hbm, nest_ref), (leg_hbm, leg_ref), (mask_hbm, mask_ref), (fold_hbm, fold_ref)))]
    for c in loads:
        c.start()

    def zero(i, c):
        pbuf[i] = jnp.zeros((KF, WIN), F32)
        return c
    lax.fori_loop(0, SLOTS, zero, 0)
    cpk_r[...] = jnp.zeros((2, 128, 128), BF16)
    rpk_r[...] = jnp.zeros((2, 96, 256), BF16)
    info_r[...] = jnp.zeros((2, 8, 128), F32)
    q_in[...] = jnp.zeros((2, 8, 768), F32)

    barrier = pltpu.get_barrier_semaphore()

    def greet(ww, yy):
        pl.semaphore_signal(barrier, inc=1, device_id=dev(ww, yy), device_id_type=MESH)

    for yy in (up_y, dn_y, sib_y):
        greet(w, yy)

    def greet_wave(o, c):
        greet(lax.rem(w + o, NW), y)
        return c
    lax.fori_loop(1, NW, greet_wave, 0)

    @pl.when(y > 0)
    def _():
        greet(w, near(-1))

    @pl.when(y < NY - 1)
    def _():
        greet(w, near(1))

    @pl.when(jnp.logical_or(jnp.logical_and(wedge, y > 0), y == NY - 1))
    def _():
        greet(NW - 1, near(-1))

    @pl.when(jnp.logical_or(jnp.logical_and(wedge, y < NY - 1), y == 0))
    def _():
        greet(0, near(1))

    sp32[0:8, :] = jnp.zeros((8, 1408), F32)
    for c in range(3):
        v = spec_ref[c].astype(F32)
        last = jnp.broadcast_to(v[:, 1280:1281], (PD, 128))
        for p0, n, r0, rows, lead in CHUNKS:
            r = r0 + lead + c * n
            sp32[r : r + n, 0:1280] = v[p0 : p0 + n, 0:1280]
            sp32[r : r + n, 1280:1408] = last[p0 : p0 + n, :]
    tail = jnp.transpose(sp32[:, 1280:1408], (1, 0))[0:8, :]
    lane = lax.broadcasted_iota(jnp.int32, (8, 128), 1)
    sub = lax.broadcasted_iota(jnp.int32, (8, 896), 0)
    extra = jnp.zeros((8, 896), F32)
    for ch, (p0, n, r0, rows, lead) in enumerate(CHUNKS):
        part = jnp.where((lane >= r0 + lead) & (lane < r0 + rows), tail, 0.0)
        part = jnp.concatenate([part, jnp.zeros((8, 768), F32)], axis=1)
        part = pltpu.roll(part, lax.rem(y * rows - r0 + 896, 896), 1)
        part = jnp.broadcast_to(part[0:1, :], (8, 896))
        extra = jnp.where(sub == ch, part, extra)
    sp32[0:8, 0:768] = extra[:, 0:768]

    def cast_own(i, c):
        r = pl.multiple_of(i * 16, 16)
        gath[y, pl.ds(r, 16), :] = sp32[pl.ds(r, 16), 0:1280].astype(BF16)
        return c
    lax.fori_loop(0, 8, cast_own, 0)

    count = 15 + 3
    count += jnp.where(y < NY - 1, 1, 0) + jnp.where(y > 0, 1, 0)
    count += jnp.where(jnp.logical_and(w == NW - 1, y < NY - 1), 2, 0)
    count += jnp.where(jnp.logical_and(w == 0, y > 0), 2, 0)
    count += jnp.where(jnp.logical_and(w == 0, y == 1), 14, 0)
    count += jnp.where(jnp.logical_and(w == NW - 1, y == NY - 2), 14, 0)
    pl.semaphore_wait(barrier, count)

    def block(origin, piece, half):
        _, _, r0, rows, _ = CHUNKS[piece]
        if half is not None:
            first, count_ = HALVES[piece][half]
            r0, rows = r0 + first, count_
        return gath.at[origin, pl.ds(r0, rows), :]

    def ring(origin, piece, step, upward):
        ref = block(origin, piece, None if step < 3 else (0 if upward else 1))
        s, r = (up_s, up_r) if upward else (dn_s, dn_r)
        return pltpu.make_async_remote_copy(
            src_ref=ref, dst_ref=ref, send_sem=s.at[piece, step], recv_sem=r.at[piece, step],
            device_id=dev(w, up_y if upward else dn_y), device_id_type=MESH)

    def to_sib(origin, piece, idx, half=None):
        ref = block(origin, piece, half)
        return pltpu.make_async_remote_copy(
            src_ref=ref, dst_ref=ref, send_sem=sib_s.at[piece, idx], recv_sem=sib_r.at[piece, idx],
            device_id=dev(w, sib_y), device_id_type=MESH)

    def origin_of(base, step, upward):
        return lax.rem(base + NY - 2 * step, NY) if upward else lax.rem(base + 2 * step, NY)

    def far(piece, upward):
        return HALVES[piece][0 if upward else 1][1] > 0

    def send_own(piece):
        ring(y, piece, 0, True).start()
        ring(y, piece, 0, False).start()
        to_sib(y, piece, 0).start()

    def ring_step(piece, step):
        for upward in (True, False):
            org = origin_of(y, step, upward)
            if step < 4:
                ring(org, piece, step - 1, upward).wait_recv()
                if step < 3 or far(piece, upward):
                    ring(org, piece, step, upward).start()
                to_sib(org, piece, 2 * step - (1 if upward else 0)).start()
            elif far(piece, upward):
                ring(org, piece, 3, upward).wait_recv()
                to_sib(org, piece, 7 if upward else 8, 0 if upward else 1).start()

    def sib_each(base, piece, go):
        go(to_sib(base, piece, 0))
        for step in range(1, 5):
            for upward in (True, False):
                org = origin_of(base, step, upward)
                if step < 4:
                    go(to_sib(org, piece, 2 * step - (1 if upward else 0)))
                elif far(piece, upward):
                    go(to_sib(org, piece, 7 if upward else 8, 0 if upward else 1))

    def sib_wait(piece):
        sib_each(sib_y, piece, lambda c: c.wait_recv())

    def sends_done(piece):
        for step in range(4):
            for upward in (True, False):
                if step < 3 or far(piece, upward):
                    ring(y, piece, step, upward).wait_send()
        sib_each(y, piece, lambda c: c.wait_send())

    anchor = anchor_ref[0].astype(F32)

    def leg_rows(ch):
        p0, n, _, _, _ = CHUNKS[ch]
        pos = lax.broadcasted_iota(jnp.int32, (1, 1280), 1)

        def one(p, c):
            limit = TRUNC - (w * PD + p0 + p)
            low = jnp.where(pos < limit, 1.0, 0.0)
            rows = leg_ref[p0 + p]
            tile = rows[:, 0:1280]
            a = pl.multiple_of(p * 16, 16)
            b = pl.multiple_of(n * 16 + p * 16, 16)
            leg2[ch % 2, pl.ds(a, 16), :] = tile * low.astype(BF16)
            leg2[ch % 2, pl.ds(b, 16), :] = tile * (1.0 - low).astype(BF16)
            last = rows[:, 1280:1281].astype(F32)
            legx[ch % 2, pl.ds(a, 16), :] = jnp.broadcast_to(last, (16, 128))
            return c
        lax.fori_loop(0, n, one, 0)

    def last_row(ch, width):
        v = gath[0, 0:16, 0:width].astype(F32)
        for i in range(1, NY):
            v = v + gath[i, 0:16, 0:width].astype(F32)
        return v[ch : ch + 1, :]

    def fourier(ch):
        p0, n, r0, rows, lead = CHUNKS[ch]
        width = 16 * rows
        g = gath[:, r0 : r0 + rows, :].reshape(width, 1280)
        x = last_row(ch, width)
        lane16 = lax.broadcasted_iota(jnp.int32, (16, 128), 1) % 16
        if ch == 0:
            res = dot_nt(leg2[0, 0:256, :], g)
            rank1 = jnp.concatenate([jnp.zeros((128, width), F32),
                                     jnp.tile(legx[0, 0:128, :], (1, width // 128)) * x], 0)
            hi, lo = split2((res + rank1) * mask_ref[...].astype(F32))
            fs[0:16] = (dot_nn(hi, fold_ref[0]) + dot_nn(lo, fold_ref[1])).reshape(16, 16, 128)
        else:
            for h in range(2):
                res = dot_nt(leg2[ch % 2, 256 * h : 256 * h + 256, :], g)
                for p in range(n):
                    v = jnp.zeros((16, 128), F32)
                    for j in range(width // 128):
                        q = res[16 * p : 16 * p + 16, 128 * j : 128 * j + 128]
                        if h == 1:
                            q = q + legx[ch % 2, 16 * p : 16 * p + 16, :] * x[:, 128 * j : 128 * j + 128]
                        q = jnp.where(lane16 == p, q, 0.0)
                        v = v + (pltpu.roll(q, (j - p) % 128, 1) if j != p else q)
                    hi = v.astype(BF16).astype(F32)
                    lo = (v - hi).astype(BF16).astype(F32)
                    fs[16 * h + p] = hi + pltpu.roll(lo, 8, 1)
        f0 = (0, 16, 48)[ch]
        for l in range(16):
            fsend[l, f0 : f0 + 2 * n, :] = fs[0 : 2 * n, l, :].astype(BF16)

    def wave_copy(ch, o):
        n = CHUNKS[ch][1]
        f0 = (0, 16, 48)[ch]
        to = lax.rem(w + o, NW)
        return pltpu.make_async_remote_copy(
            src_ref=fsend.at[to, pl.ds(f0, 2 * n), :], dst_ref=frecv.at[ch, w, pl.ds(0, 2 * n), :],
            send_sem=fa_s.at[ch, o], recv_sem=fa_r.at[ch, o],
            device_id=dev(to, y), device_id_type=MESH)

    def wave_send(ch):
        n = CHUNKS[ch][1]
        f0 = (0, 16, 48)[ch]
        lax.fori_loop(1, NW, lambda o, c: (wave_copy(ch, o).start(), c)[1], 0)
        frecv[ch, w, 0 : 2 * n, :] = fsend[w, f0 : f0 + 2 * n, :]

    def wave_recv(ch):
        lax.fori_loop(1, NW, lambda o, c: (wave_copy(ch, o).wait_recv(), c)[1], 0)

    def wave_done(ch):
        lax.fori_loop(1, NW, lambda o, c: (wave_copy(ch, o).wait_send(), c)[1], 0)

    def table(ch):
        p0, n, _, _, _ = CHUNKS[ch]
        k0 = KOFF[ch]
        shift = 4 if n == 16 else 3

        def one(t, c):
            q = t * 128 + lax.broadcasted_iota(jnp.int32, (1, 128), 1)
            ww = q >> (shift + 1)
            h = (q >> shift) & 1
            pg = ww * PD + p0 + (q & (n - 1))
            mi = jnp.where(h == 0, pg, TRUNC - 1 - pg)
            m = mi.astype(F32)
            s = jnp.where(mi == 0, 1.0, 2.0)

            def angle(x):
                return (x - NLON * jnp.floor(x * (1.0 / NLON))) * (2.0 * math.pi / NLON)

            d = lax.broadcasted_iota(jnp.int32, (LON, 128), 0).astype(F32)
            fine = angle(m * d)
            cf, sf = jnp.cos(fine) * s, jnp.sin(fine) * s
            b = lax.broadcasted_iota(jnp.int32, (16, 128), 0).astype(F32) * LON
            coarse = angle(m * (anchor + b))
            cc, sc = jnp.cos(coarse), jnp.sin(coarse)
            col = pl.multiple_of(k0 + t * 128, 128)
            for i in range(16):
                ci, si = cc[i : i + 1, :], sc[i : i + 1, :]
                vc = ci * cf - si * sf
                vs = -(si * cf + ci * sf)
                hi, lo = split2(vc)
                tcos[0, LON * i : LON * i + LON, pl.ds(col, 128)] = hi
                tcos[1, LON * i : LON * i + LON, pl.ds(col, 128)] = lo
                hi, lo = split2(vs)
                tsin[0, LON * i : LON * i + LON, pl.ds(col, 128)] = hi
                tsin[1, LON * i : LON * i + LON, pl.ds(col, 128)] = lo
            return c
        lax.fori_loop(0, 2 * n * 16 // 128, one, 0)

    def contract(ch):
        n = CHUNKS[ch][1]
        k0, k = KOFF[ch], 2 * n * 16
        f = frecv[ch, :, 0 : 2 * n, :].reshape(k, 128)

        for tab, acc in ((tcos, acc_c), (tsin, acc_s)):
            v = dot_nn(tab[0, :, k0 : k0 + k], f) + dot_nn(tab[1, :, k0 : k0 + k], f)
            if ch == 0:
                acc[...] = v
            else:
                acc[...] = acc[...] + v

    lane_h = lax.broadcasted_iota(jnp.int32, (128, 128), 1)

    def nest_copy(i):
        if i < 4:
            src, dst = (cpk_s, cpk_r) if i < 2 else (rpk_s, rpk_r)
            src, dst = src.at[i % 2], dst.at[i % 2]
        else:
            src, dst = info_s, info_r.at[i - 4]
        to = (dev(lax.rem(w + NW - 1, NW), y), dev(lax.rem(w + 1, NW), y), dev(w, near(-1)), dev(w, near(1)))[i % 4]
        return pltpu.make_async_remote_copy(
            src_ref=src, dst_ref=dst, send_sem=nest_s.at[i], recv_sem=nest_r.at[i],
            device_id=to, device_id_type=MESH)

    can_send = (w > 0, w < NW - 1, y > 0, y < NY - 1)
    can_recv = (w < NW - 1, w > 0, y < NY - 1, y > 0)

    def nest_do(which, cond, go):
        for i in which:
            @pl.when(cond[i % 4])
            def _(i=i):
                go(nest_copy(i))

    def nest_pack():
        info_s[...] = jnp.zeros((8, 128), F32)
        info_s[0:1, :] = ridx_ref[...].astype(F32)
        info_s[1:2, :] = rwt_ref[...]
        loads[0].wait()
        info_s[2:3, :] = cidx_ref[...].astype(F32)
        info_s[3:4, :] = cwt_ref[...]
        left = jnp.zeros((128, 128), F32)
        right = jnp.zeros((128, 128), F32)
        for k in range(KF):
            v = nest_ref[k].astype(F32)
            here = (lane_h >= 4 * k) & (lane_h < 4 * k + 4)
            left = jnp.where(here, pltpu.roll(v, 4 * k, 1) if k else v, left)
            right = jnp.where(here, pltpu.roll(v, 4 * k + 4, 1), right)
        cpk_s[0] = left.astype(BF16)
        cpk_s[1] = right.astype(BF16)
        row = (lax.broadcasted_iota(jnp.int32, (EXT, 256), 0) + (128 * y - 8)).astype(F32)
        j = lax.broadcasted_iota(jnp.int32, (EXT, 256), 1)
        col = (jnp.where(j < 192, j, j - 256) + 128 * w).astype(F32)
        keep, _ = shares(row, col, zone_ref)
        damp[...] = keep * DIFFUSION
        nest_do((0, 1, 4, 5), can_send, lambda c: c.start())

    def nest_cols():
        nest_do((0, 1), can_recv, lambda c: c.wait_recv())
        from_right = cpk_r[0].astype(F32)
        from_left = cpk_r[1].astype(F32)

        def one(k, c):
            a = pltpu.roll(from_right, lax.rem(128 - 4 * k, 128), 1)
            b = pltpu.roll(from_left, lax.rem(252 - 4 * k, 128), 1)
            e = jnp.where(lane_h < 4, a, jnp.where(lane_h >= 124, b, 0.0))
            ext[k, 0:8, :] = jnp.zeros((8, 256), F32)
            ext[k, 136:144, :] = jnp.zeros((8, 256), F32)
            ext[k, 8:136, 0:128] = nest_ref[k].astype(F32)
            ext[k, 8:136, 128:256] = e
            return c
        lax.fori_loop(0, KF, one, 0)
        for i, r in ((0, 8), (1, 132)):
            for k in range(KF):
                rpk[4 * k : 4 * k + 4, :] = ext[k, r : r + 4, :]
            rpk_s[i] = rpk[...].astype(BF16)
        nest_do((2, 3), can_send, lambda c: c.start())

    def nest_rows():
        nest_do((2, 3), can_recv, lambda c: c.wait_recv())
        for i, r in ((0, 136), (1, 4)):
            rpk[...] = rpk_r[i].astype(F32)
            for k in range(KF):
                ext[k, r : r + 4, :] = rpk[4 * k : 4 * k + 4, :]

    def nest_sweeps(k0, k1_):
        def one(k, c):
            x = ext[k]
            for _ in range(NSWEEP):
                t = x + pltpu.roll(x, 1, 0) + pltpu.roll(x, EXT - 1, 0)
                t = t + pltpu.roll(x, 1, 1) + pltpu.roll(x, 255, 1)
                x = t * damp[...]
            field[k] = x[8:136, 0:128]
            nest_out[k] = x[8:136, 0:128].astype(BF16)
            return c
        lax.fori_loop(k0, k1_, one, 0)

    def nest_done():
        nest_do((4, 5), can_recv, lambda c: c.wait_recv())
        nest_do(range(6), can_send, lambda c: c.wait_send())

    row_edge = jnp.logical_or(y == 0, y == NY - 1)
    first = jnp.where(y == 0, 0, 104)
    cbase = jnp.where(w == 0, 0, 96)

    def strip_prep():
        lon0 = (w * LON - 48).astype(F32)
        lat0 = (y * 16 - 1).astype(F32)
        own, right, left = info_s[...], info_r[0], info_r[1]
        lane = lax.broadcasted_iota(jnp.int32, (1, 128), 1)
        turned = jnp.transpose(jnp.concatenate([own, jnp.zeros((120, 128), F32)], 0), (1, 0))

        @pl.when(row_edge)
        def _():
            far_i = jnp.where(lane < 4, right[2:3], jnp.where(lane >= 124, left[2:3], -4096.0))
            far_w = jnp.where(lane < 4, right[3:4], left[3:4])
            cidx = jnp.concatenate([own[2:3], far_i], 1) - lon0
            cwt = jnp.concatenate([own[3:4], far_w], 1)
            hi, lo = split2(pick(fiota((128, 256), 0), cidx, cwt))
            row_mats[0] = hi
            row_mats[1] = lo
            cols = jnp.where(y == 0, turned[0:24, :], turned[104:128, :])
            ridx = cols[:, 0:1] - lat0
            rwt = cols[:, 1:2]
            row = fiota((24, 256), 0) + (128 * y + first).astype(F32)
            j = lax.broadcasted_iota(jnp.int32, (24, 256), 1)
            col = (jnp.where(j < 192, j, j - 256) + 128 * w).astype(F32)
            keep, share = shares(row, col, zone_ref)
            row_part[0] = jnp.where((row < 20.0) | (row >= 2028.0), keep * DIFFUSION, 0.0)
            row_part[1] = jnp.where((row < 16.0) | (row >= 2032.0), share, 0.0)
            row_blend[...] = pick(fiota((24, SLOTS), 1), ridx, rwt)

        @pl.when(wedge)
        def _():
            vec = jnp.concatenate([own[2:4] - jnp.where(fiota((2, 128), 0) == 0.0, lon0, 0.0),
                                   jnp.zeros((6, 128), F32)], 0)
            vec = jnp.where(w == 0, vec, pltpu.roll(vec, 32, 1))
            for i in range(4):
                v = pltpu.roll(vec, LON * i, 1) if i else vec
                here = (lane >= LON * i) & (lane < LON * i + LON)
                m = jnp.where(here, pick(fiota((128, 128), 0), v[0:1], v[1:2]), 0.0)
                hi, lo = split2(m)
                col_mats[0, 128 * i : 128 * i + 128, :] = hi
                col_mats[1, 128 * i : 128 * i + 128, :] = lo
            col_blend[...] = pick(fiota((128, SLOTS), 1), turned[:, 0:1] - lat0, turned[:, 1:2])
            row = fiota((EXT, 128), 0) + (128 * y - 8).astype(F32)
            inner = lax.broadcasted_iota(jnp.int32, (EXT, 128), 1) % LON
            col = (inner + cbase + 128 * w).astype(F32)
            keep, share = shares(row, col, zone_ref)
            share = jnp.where((col < 16.0) | (col >= 2032.0), share, 0.0)
            col_part[0] = keep * DIFFUSION
            col_part[1] = jnp.where((row >= 16.0) & (row < 2032.0), share, 0.0)

    def q_copy(i):
        return pltpu.make_async_remote_copy(
            src_ref=q_out.at[i], dst_ref=q_in.at[i], send_sem=q_s.at[i], recv_sem=q_r.at[i],
            device_id=dev(w, near(1 if i else -1)), device_id_type=MESH)

    def q_each(cond, go):
        for i in range(2):
            @pl.when(jnp.logical_and(wedge, cond[i]))
            def _(i=i):
                go(q_copy(i))

    q_send = (y > 0, y < NY - 1)
    q_recv = (y < NY - 1, y > 0)

    def gather_rows():
        for k in range(KF):
            lats[:, 128 * k : 128 * k + 128] = pbuf[:, k, :]

    def col_source():
        @pl.when(wedge)
        def _():
            v = jnp.concatenate([lats[:, 512 * t : 512 * t + 512] for t in range(KF // 4)], 0)
            v = dot3(v, col_mats[0], col_mats[1])
            v = jnp.concatenate([v[24 * t : 24 * t + 24, :] for t in range(KF // 4)], 1)
            hi, lo = split2(v)
            v = dot3(col_blend[...], hi, lo)
            share = col_part[1, 8:136, :]
            col_q[0:8, :] = jnp.zeros((8, 768), F32)
            col_q[136:144, :] = jnp.zeros((8, 768), F32)
            for t in range(KF // 4):
                col_q[8:136, 128 * t : 128 * t + 128] = v[:, 128 * t : 128 * t + 128] * share
            q_out[0] = col_q[8:16, :]
            q_out[1] = col_q[128:136, :]

        q_each(q_send, lambda c: c.start())

    def row_strip():
        @pl.when(row_edge)
        def _():
            hi, lo = split2(lats[...])
            v = dot3(row_blend[...], hi, lo)
            v = jnp.concatenate([v[:, 128 * k : 128 * k + 128] for k in range(KF)], 0)
            row_x[...] = dot3(v, row_mats[0], row_mats[1])
            at = pl.ds(pl.multiple_of(first, 8), 24)

            def some(n, c):
                ks = [n * 6 + i for i in range(6)]
                qs = [row_x[pl.ds(pl.multiple_of(k * 24, 8), 24), :] * row_part[1] for k in ks]
                gs = list(qs)
                for _ in range(NSWEEP - 1):
                    vs = [g + pltpu.roll(g, 1, 0) + pltpu.roll(g, 23, 0)
                          + pltpu.roll(g, 1, 1) + pltpu.roll(g, 255, 1) for g in gs]
                    gs = [v * row_part[0] + q for v, q in zip(vs, qs)]
                for k, g in zip(ks, gs):
                    field[k, at, :] = field[k, at, :] + g[:, 0:128]
                return c
            lax.fori_loop(0, KF // 6, some, 0)

        @pl.when(jnp.logical_and(row_edge, jnp.logical_not(wedge)))
        def _():
            at = pl.ds(pl.multiple_of(jnp.where(y == 0, 0, 96), 32), 32)

            def last(k, c):
                nest_out[k, at, :] = field[k, at, :].astype(BF16)
                return c
            lax.fori_loop(0, KF, last, 0)

    def side_masks(rows):
        inner = lax.broadcasted_iota(jnp.int32, (rows, 128), 1) % LON
        return inner != 0, inner != LON - 1

    def side_sweeps(qs, keep, rows):
        not_first, not_last = side_masks(rows)
        gs = list(qs)
        for _ in range(NSWEEP - 1):
            vs = [g + pltpu.roll(g, 1, 0) + pltpu.roll(g, rows - 1, 0)
                  + jnp.where(not_first, pltpu.roll(g, 1, 1), 0.0)
                  + jnp.where(not_last, pltpu.roll(g, 127, 1), 0.0) for g in gs]
            gs = [v * keep + q for v, q in zip(vs, qs)]
        return gs

    def col_strip():
        @pl.when(wedge)
        def _():
            def some(n, c):
                at = [pl.ds(pl.multiple_of((n * 2 + i) * 128, 128), 128) for i in range(2)]
                gs = side_sweeps([col_q[:, a] for a in at], col_part[0], EXT)
                for a, g in zip(at, gs):
                    col_q[:, a] = g
                return c
            lax.fori_loop(0, KF // 8, some, 0)

        q_each(q_recv, lambda c: c.wait_recv())

        @pl.when(wedge)
        def _():
            sub = lax.broadcasted_iota(jnp.int32, (8, 768), 0)
            blank = jnp.zeros((8, 768), F32)
            above = jnp.concatenate([jnp.where(sub >= 4, q_in[1], 0.0), blank], 0)
            below = jnp.concatenate([blank, jnp.where(sub < 4, q_in[0], 0.0)], 0)
            tiles = range(KF // 4)
            ga = side_sweeps([above[:, 128 * t : 128 * t + 128] for t in tiles], col_part[0, 0:16, :], 16)
            gb = side_sweeps([below[:, 128 * t : 128 * t + 128] for t in tiles], col_part[0, 128:144, :], 16)
            for t in tiles:
                a = slice(128 * t, 128 * t + 128)
                col_q[8:16, a] = col_q[8:16, a] + ga[t][8:16]
                col_q[128:136, a] = col_q[128:136, a] + gb[t][0:8]
            lane_h = lax.broadcasted_iota(jnp.int32, (128, 128), 1)
            strip = (lane_h >= cbase) & (lane_h < cbase + LON)

            def add(n, c):
                for t in (n * 2, n * 2 + 1):
                    g = col_q[8:136, pl.ds(pl.multiple_of(t * 128, 128), 128)]
                    for i in range(4):
                        part = pltpu.roll(g, lax.rem(cbase + 128 - LON * i, 128), 1)
                        k = 4 * t + i
                        nest_out[k] = (field[k] + jnp.where(strip, part, 0.0)).astype(BF16)
                return c
            lax.fori_loop(0, KF // 8, add, 0)

    send_own(0)
    send_own(1)
    nest_pack()
    ring_step(0, 1)
    send_own(2)
    nest_cols()
    table(0)
    ring_step(0, 2)
    ring_step(1, 1)
    table(1)
    loads[1].wait()
    leg_rows(0)
    table(2)
    nest_rows()
    leg_rows(1)
    ring_step(0, 3)
    ring_step(2, 1)
    nest_sweeps(0, 8)
    ring_step(1, 2)
    ring_step(0, 4)
    sib_wait(0)
    loads[2].wait()
    loads[3].wait()
    fourier(0)
    wave_send(0)
    ring_step(2, 2)
    nest_sweeps(8, 16)
    ring_step(1, 3)
    wave_recv(0)
    contract(0)
    ring_step(2, 3)
    nest_sweeps(16, KF)
    nest_done()
    strip_prep()
    ring_step(1, 4)
    leg_rows(2)
    ring_step(2, 4)
    sib_wait(1)
    fourier(1)
    sib_wait(2)
    wave_send(1)
    fourier(2)
    wave_send(2)
    wave_recv(1)
    contract(1)
    wave_recv(2)
    contract(2)

    prow[:, 0:128] = jnp.zeros((KF, 128), F32)
    prow[:, 512:640] = jnp.zeros((KF, 128), F32)
    for i in range(4):
        turn[0] = jnp.transpose(acc_c[128 * i : 128 * i + 128, :], (1, 0)).reshape(8, 16, 128)
        turn[1] = jnp.transpose(acc_s[128 * i : 128 * i + 128, :], (1, 0)).reshape(8, 16, 128)
        val = [turn[0, :, j, :] + turn[0, :, j + 8, :] + turn[1, :, j + 3, :] + turn[1, :, j + 11, :]
               for j in range(3)]
        prow[:, 48 + 128 * i : 176 + 128 * i] = jnp.concatenate(val, 0)
    lane = lax.broadcasted_iota(jnp.int32, (8, 128), 1)
    for v in range(NW):
        window = prow[:, LON * v : LON * v + WIN]
        psend[v] = window
        packed = jnp.zeros((8, 128), F32)
        for j in range(3):
            part = pltpu.roll(window[8 * j : 8 * j + 8], (LON * j + 80) % 128, 1)
            packed = jnp.where((lane >= LON * j) & (lane < LON * j + LON), part, packed)
            if v in (0, NW - 1):
                beside = 80 if v == 0 else 47
                part = pltpu.roll(window[8 * j : 8 * j + 8], (96 + j - beside) % 128, 1)
                packed = jnp.where(lane == 96 + j, part, packed)
        pack_s[v] = packed

    def win(src, to_w, to_y, slot, sem):
        return pltpu.make_async_remote_copy(
            src_ref=psend.at[src], dst_ref=pbuf.at[slot], send_sem=w_s.at[sem], recv_sem=w_r.at[slot],
            device_id=dev(to_w, to_y), device_id_type=MESH)

    def edges(go):
        @pl.when(jnp.logical_and(w == 0, y > 0))
        def _():
            go(0, 0, near(-1), 17, 16)
            go(NW - 1, NW - 1, near(-1), 17, 17)

        @pl.when(jnp.logical_and(w == NW - 1, y < NY - 1))
        def _():
            go(0, 0, near(1), 0, 18)
            go(NW - 1, NW - 1, near(1), 0, 19)

        @pl.when(jnp.logical_and(w == 0, y == 1))
        def _():
            lax.fori_loop(1, NW - 1, lambda v, c: (go(v, v, near(-1), 17, 20 + v), c)[1], 0)

        @pl.when(jnp.logical_and(w == NW - 1, y == NY - 2))
        def _():
            lax.fori_loop(1, NW - 1, lambda v, c: (go(v, v, near(1), 0, 20 + v), c)[1], 0)

    def own_win(o):
        to = lax.rem(w + o, NW)
        return win(to, to, y, 1 + w, o)

    def own_pack(o):
        to = lax.rem(w + o, NW)
        return pltpu.make_async_remote_copy(
            src_ref=pack_s.at[to], dst_ref=pack_r.at[w], send_sem=w_s.at[o], recv_sem=w_r.at[1 + w],
            device_id=dev(to, y), device_id_type=MESH)

    def own_each(go):
        @pl.when(row_edge)
        def _():
            lax.fori_loop(1, NW, lambda o, c: (go(own_win(o)), c)[1], 0)

        @pl.when(jnp.logical_not(row_edge))
        def _():
            lax.fori_loop(1, NW, lambda o, c: (go(own_pack(o)), c)[1], 0)

    edges(lambda *a: win(*a).start())
    own_each(lambda c: c.start())
    pbuf[1 + w] = psend[w]
    pack_r[w] = pack_s[w]

    for ch in range(3):
        wave_done(ch)
    for piece in range(len(CHUNKS)):
        sends_done(piece)

    def got(slot):
        win(0, w, sib_y, slot, 0).wait_recv()

    here_whole = row_edge

    @pl.when(here_whole)
    def _():
        lax.fori_loop(1, NW, lambda o, c: (got(1 + lax.rem(w + o, NW)), c)[1], 0)

    @pl.when(jnp.logical_not(here_whole))
    def _():
        def one(o, c):
            src = lax.rem(w + o, NW)
            pltpu.make_async_remote_copy(
                src_ref=pack_s.at[0], dst_ref=pack_r.at[src], send_sem=w_s.at[0],
                recv_sem=w_r.at[1 + src], device_id=dev(w, sib_y), device_id_type=MESH).wait_recv()
            return c
        lax.fori_loop(1, NW, one, 0)

    @pl.when(jnp.logical_or(jnp.logical_and(wedge, y > 0), y == NY - 1))
    def _():
        got(0)

    @pl.when(jnp.logical_or(jnp.logical_and(wedge, y < NY - 1), y == 0))
    def _():
        got(17)

    @pl.when(jnp.logical_and(wedge, jnp.logical_not(row_edge)))
    def _():
        beside = jnp.where(w == 0, 80, 47)
        for s in range(16):
            for j in range(3):
                a = pltpu.roll(pack_r[s], (48 - LON * j) % 128, 1)
                b = pltpu.roll(pack_r[s], lax.rem(beside + 128 - 96 - j + 128, 128), 1)
                a = jnp.where((lane >= 48) & (lane < 80), a, jnp.where(lane == beside, b, 0.0))
                pbuf[1 + s, 8 * j : 8 * j + 8, :] = a

    @pl.when(jnp.logical_or(wedge, row_edge))
    def _():
        gather_rows()

    col_source()
    row_strip()
    col_strip()

    @pl.when(here_whole)
    def _():
        for k in range(KF):
            band_out[k] = pltpu.roll(pbuf[1:17, k, :], 80, 1)[:, 0:LON]

    @pl.when(jnp.logical_not(here_whole))
    def _():
        for i in range(8):
            v = pack_r[:, i, :]
            for j in range(3):
                band_out[8 * j + i] = (pltpu.roll(v, 128 - LON * j, 1) if j else v)[:, 0:LON]

    q_each(q_send, lambda c: c.wait_send())
    own_each(lambda c: c.wait_send())
    edges(lambda *a: win(*a).wait_send())


def vmem_spec():
    return pl.BlockSpec(memory_space=pltpu.VMEM)


def spectral(spectra, legendre, lon_anchor, zone_width, nest_state, ridx, rwt, cidx, cwt):
    spec = jnp.transpose(spectra, (1, 0, 2))
    mask, fold = first_consts()
    np_ = len(CHUNKS)
    smem = pl.BlockSpec(memory_space=pltpu.SMEM)
    dma = pltpu.SemaphoreType.DMA
    return pl.pallas_call(
        k1,
        out_shape=(
            jax.ShapeDtypeStruct((KF, 16, LON), F32),
            jax.ShapeDtypeStruct((KF, 128, 128), BF16),
        ),
        in_specs=[smem, smem] + [vmem_spec()] * 5 + [pl.BlockSpec(memory_space=pl.ANY)] * 4,
        out_specs=(vmem_spec(), vmem_spec()),
        scratch_shapes=[
            pltpu.VMEM((PD, 16, 1281), BF16),
            pltpu.VMEM(mask.shape, BF16), pltpu.VMEM(fold.shape, BF16),
            pltpu.VMEM((KF, 128, 128), BF16),
            dma((4,)),
            pltpu.VMEM((NY, 128, 1280), BF16),
            pltpu.VMEM((128, 1408), F32),
            pltpu.VMEM((2, 512, 1280), BF16),
            pltpu.VMEM((2, 256, 128), F32),
            pltpu.VMEM((32, 16, 128), F32),
            pltpu.VMEM((16, 80, 128), BF16),
            pltpu.VMEM((3, 16, 32, 128), BF16),
            pltpu.VMEM((2, NLB, NKEY), BF16),
            pltpu.VMEM((2, NLB, NKEY), BF16),
            pltpu.VMEM((NLB, 128), F32),
            pltpu.VMEM((NLB, 128), F32),
            pltpu.VMEM((2, 8, 16, 128), F32),
            pltpu.VMEM((16, KF, WIN), F32),
            pltpu.VMEM((16, 8, 128), F32),
            pltpu.VMEM((16, 8, 128), F32),
            pltpu.VMEM((KF, 640), F32),
            pltpu.VMEM((SLOTS, KF, WIN), F32),
            pltpu.VMEM((KF, EXT, 256), F32),
            pltpu.VMEM((EXT, 256), F32),
            pltpu.VMEM((2, 128, 128), BF16),
            pltpu.VMEM((2, 128, 128), BF16),
            pltpu.VMEM((96, 256), F32),
            pltpu.VMEM((2, 96, 256), BF16),
            pltpu.VMEM((2, 96, 256), BF16),
            pltpu.VMEM((8, 128), F32),
            pltpu.VMEM((2, 8, 128), F32),
            dma((6,)), dma((6,)),
            pltpu.VMEM((KF, 128, 128), F32),
            pltpu.VMEM((2, 128, 256), BF16),
            pltpu.VMEM((2, 24, 256), F32),
            pltpu.VMEM((24, SLOTS), F32),
            pltpu.VMEM((24 * KF, 256), F32),
            pltpu.VMEM((2, 512, 128), BF16),
            pltpu.VMEM((2, EXT, 128), F32),
            pltpu.VMEM((128, SLOTS), F32),
            pltpu.VMEM((SLOTS, 128 * KF), F32),
            pltpu.VMEM((EXT, 768), F32),
            pltpu.VMEM((2, 8, 768), F32),
            pltpu.VMEM((2, 8, 768), F32),
            dma((2,)), dma((2,)),
            dma((np_, 4)), dma((np_, 4)),
            dma((np_, 4)), dma((np_, 4)),
            dma((np_, 9)), dma((np_, 9)),
            dma((3, 16)), dma((3, 16)),
            dma((40,)), dma((SLOTS,)),
        ],
        compiler_params=pltpu.CompilerParams(
            collective_id=0, has_side_effects=True, vmem_limit_bytes=60 * 1024 * 1024),
    )(lon_anchor, zone_width, spec, ridx, rwt, cidx, cwt, legendre,
      jnp.asarray(mask, BF16), jnp.asarray(fold, BF16), nest_state)


def hand_over(band_in, nest_in, band_out, nest_out, band_v, nest_v, sem):
    trips = [((band_in, band_v), (band_v, band_out))]
    for i in range(4):
        at = pl.ds(6 * i, 6)
        trips.append(((nest_in.at[at], nest_v.at[at]), (nest_v.at[at], nest_out.at[at])))
    trips = [tuple(pltpu.make_async_copy(*c, sem.at[way, i]) for way, c in enumerate(trip))
             for i, trip in enumerate(trips)]
    for get, _ in trips:
        get.start()
    for get, put in trips:
        get.wait()
        put.start()
    for _, put in trips:
        put.wait()


def results(band, nest):
    hbm = pl.BlockSpec(memory_space=pl.ANY)
    return pl.pallas_call(
        hand_over,
        out_shape=(jax.ShapeDtypeStruct(band.shape, F32), jax.ShapeDtypeStruct(nest.shape, BF16)),
        in_specs=[hbm, hbm], out_specs=(hbm, hbm),
        scratch_shapes=[pltpu.VMEM(band.shape, F32), pltpu.VMEM(nest.shape, BF16),
                        pltpu.SemaphoreType.DMA((2, 5))],
        compiler_params=pltpu.CompilerParams(vmem_limit_bytes=60 * 1024 * 1024),
    )(band, nest)


def body(
    spectra, legendre, lon_anchor, row_index, row_weight, col_index, col_weight, zone_width,
    nest_state,
):
    band, nest = spectral(
        spectra, legendre, lon_anchor, zone_width, nest_state,
        row_index.reshape(1, 128), row_weight.reshape(1, 128),
        col_index.reshape(1, 128), col_weight.reshape(1, 128),
    )
    return results(band, nest)


def solution(mesh):
    placed = (
        P("wave", "ny", None), P("wave", "ny", None), P(), P("ny"), P("ny"), P("wave"), P("wave"),
        P(), P(None, "ny", "wave"),
    )
    return jax.shard_map(
        body, mesh=mesh, in_specs=placed,
        out_specs=(P(None, "ny", "wave"), P(None, "ny", "wave")), check_vma=False,
    )
```
